256 devices in a mesh: sp: 16 (over z, y_lo), tp: 16 (over y_hi, x, core).
Axes of the slice: x: 4, y: 4 (y_hi: 2, y_lo: 2; y = y_hi * 2 + y_lo), z: 8, core: 2. Of those that a mesh axis runs over, the one named last changes fastest.
Arguments:
- residual: bfloat16 [2048, 8192], P('sp', 'tp'), may hold values from -6 to 6
- queries: bfloat16 [2048, 8192], P(('tp', 'sp')), may hold values from -150 to 150
- keys: bfloat16 [2048, 1024], P(('tp', 'sp')), may hold values from -6 to 6
- values: bfloat16 [2048, 1024], P(('tp', 'sp')), may hold values from -24 to 24
- cache_keys: bfloat16 [16384, 1024], P('tp'), may hold values from -6 to 6
- cache_values: bfloat16 [16384, 1024], P('tp'), may hold values from -24 to 24
- offset: int32 [1], replicated, may hold values from 6144 to 16384
- w_out: bfloat16 [8192, 8192], P('sp', 'tp'), may hold values from -0.0625 to 0.0625
- norm_gain: bfloat16 [8192], P('tp'), may hold values from 0.099609375 to 1.8984375
- w_gate: bfloat16 [8192, 16384], P('tp', 'sp'), may hold values from -0.0625 to 0.0625
- w_up: bfloat16 [8192, 16384], P('tp', 'sp'), may hold values from -0.0625 to 0.0625
- w_down: bfloat16 [16384, 8192], P('sp', 'tp'), may hold values from -0.046875 to 0.046875
Outputs:
- block_out: bfloat16 [2048, 8192], P('sp', 'tp')
The draws below stay inside these ranges and needn't reach their ends.
All inputs are finite; a program needn't handle non-finite values.
Results may differ from the reference program's by a relative error of at most 0.02.
Values may be sent and summed in bfloat16 or wider, within the bound.
A program may use at most 128 MiB of HBM per device.

```python
import jax
import jax.numpy as jnp
from jax import lax

D = 8192
H = 64
KV = 8
HD = 128
FF = 16384
TOKENS = 2048
CTX = 16384
N_TP = 16


def shared_rows(key):
    cache_rows = jax.random.truncated_normal(jax.random.fold_in(key, 11), -6.0, 6.0, (CTX, KV * HD), jnp.float32)
    return cache_rows


def draw_cache_keys(key, part):
    cache_rows = shared_rows(key)
    return cache_rows.astype(jnp.bfloat16)


def draw_queries(key, part):
    key = jax.random.fold_in(key, 5)
    drawn = 2.0 * jax.random.truncated_normal(key, -6.0, 6.0, (TOKENS, H * HD), jnp.float32)
    return drawn.astype(jnp.bfloat16)


def shard_levels(own_key, dims, shards, least, largest):
    def one(position, blocks):
        steps = jax.random.uniform(jax.random.fold_in(jax.random.fold_in(own_key, 6), position), (blocks,), jnp.float32, least / len(shards), largest / len(shards))
        return jnp.repeat(jnp.exp(steps), dims[position] // blocks).reshape((-1,) + (1,) * (len(dims) - position - 1))

    gain = one(*shards[0])
    for cut in shards[1:]:
        gain = gain * one(*cut)
    return gain


def scatter_about(rng, dims, width, most, split=(), held_as=jnp.bfloat16):
    values = jax.random.normal(rng, dims, jnp.float32) * width
    if len(split) > 0:
        values = shard_levels(rng, dims, split, -0.22, 0.18) * values
    return jnp.clip(values, min=-most, max=most).astype(held_as)


def setup_inputs(seed: int = 0) -> dict:
    key_list = jax.random.split(jax.random.key(seed), 13)
    return {
        "residual": scatter_about(key_list[0], (TOKENS, D), 1.0, 6.0, ((0, 16), (1, 16))),
        "queries": draw_queries(jax.random.fold_in(key_list[12], 71), 0),
        "keys": scatter_about(key_list[2], (TOKENS, KV * HD), 1.0, 6.0, ((0, 256),)),
        "values": scatter_about(key_list[3], (TOKENS, KV * HD), 4.0, 24.0, ((0, 256),)),
        "cache_keys": draw_cache_keys(jax.random.fold_in(key_list[12], 71), 0),
        "cache_values": scatter_about(key_list[5], (CTX, KV * HD), 4.0, 24.0, ((0, 16),)),
        "offset": jax.random.randint(key_list[6], (1,), 3 * CTX // 8, CTX + 1).astype(jnp.int32),
        "w_out": scatter_about(key_list[7], (H * HD, D), (H * HD) ** -0.5, 0.0625, ((0, 16), (1, 16))),
        "norm_gain": jnp.clip(1.0 + 0.18 * jax.random.normal(key_list[8], (D,), jnp.float32), 0.099609375, 1.8984375).astype(jnp.bfloat16),
        "w_gate": scatter_about(key_list[9], (D, FF), D ** -0.5, 0.0625, ((0, 16), (1, 16))),
        "w_up": scatter_about(key_list[10], (D, FF), D ** -0.5, 0.0625, ((0, 16), (1, 16))),
        "w_down": scatter_about(key_list[11], (FF, D), FF ** -0.5, 0.046875, ((0, 16), (1, 16))),
    }


def attend_head(head, queries, keys, values, cache_keys, cache_values, start):
    group = H // KV
    shared = (head // group).astype(jnp.int32)
    query_cols = lax.dynamic_slice_in_dim(queries, (head * HD).astype(jnp.int32), HD, 1)
    key_rows = jnp.concatenate([lax.dynamic_slice_in_dim(cache_keys, shared * HD, HD, 1), lax.dynamic_slice_in_dim(keys, shared * HD, HD, 1)], 0)
    value_rows = jnp.concatenate([lax.dynamic_slice_in_dim(cache_values, shared * HD, HD, 1), lax.dynamic_slice_in_dim(values, shared * HD, HD, 1)], 0)
    scores = jnp.dot(query_cols, key_rows.T, preferred_element_type=jnp.float32) * (1.0 / HD ** 0.5)
    columns = jnp.arange(CTX + TOKENS, dtype=jnp.int32)
    tokens_at = jnp.arange(TOKENS, dtype=jnp.int32)
    visible = jnp.where(columns[None, :] < CTX, columns[None, :] < start, columns[None, :] - CTX <= tokens_at[:, None])
    highest = lax.optimization_barrier(jnp.max(jnp.where(visible, scores, -1e+30), axis=1, keepdims=True))
    weights = jnp.where(visible, jnp.exp(scores - highest), 0.0)
    total = lax.optimization_barrier(jnp.sum(weights, axis=1, keepdims=True))
    mixed = jnp.dot(weights.astype(jnp.bfloat16), value_rows, preferred_element_type=jnp.float32)
    return (mixed / total).astype(jnp.bfloat16)

def reference(residual, queries, keys, values, cache_keys, cache_values, offset, w_out, norm_gain, w_gate, w_up, w_down):
    start = offset[0]
    heads = lax.map(lambda head: attend_head(head, queries, keys, values, cache_keys, cache_values, start), jnp.arange(H, dtype=jnp.int32))
    attended = jnp.transpose(heads, (1, 0, 2)).reshape(TOKENS, H * HD)
    attn_out = jnp.dot(attended, w_out, preferred_element_type=jnp.float32)
    stream = (residual.astype(jnp.float32) + attn_out).astype(jnp.bfloat16)
    wide = stream.astype(jnp.float32)
    scale_rows = lax.rsqrt(lax.optimization_barrier(jnp.mean(wide * wide, axis=1, keepdims=True)) + 1e-06)
    normed = (wide * scale_rows * norm_gain.astype(jnp.float32)[None, :]).astype(jnp.bfloat16)
    block = D // N_TP

    def add_block(index, carry):
        gate_sum, up_sum = carry
        first = (index * block).astype(jnp.int32)
        cols = lax.dynamic_slice_in_dim(normed, first, block, 1)
        gate_part = jnp.dot(cols, lax.dynamic_slice_in_dim(w_gate, first, block, 0), preferred_element_type=jnp.float32).astype(jnp.bfloat16)
        up_part = jnp.dot(cols, lax.dynamic_slice_in_dim(w_up, first, block, 0), preferred_element_type=jnp.float32).astype(jnp.bfloat16)
        gate_part, up_part = lax.optimization_barrier((gate_part, up_part))
        return (gate_sum + gate_part.astype(jnp.float32), up_sum + up_part.astype(jnp.float32))
    empty = jnp.zeros((TOKENS, FF), jnp.float32)
    gate, up = lax.fori_loop(0, N_TP, add_block, (empty, empty))
    hidden = (jax.nn.silu(gate) * up).astype(jnp.bfloat16)
    down = jnp.dot(hidden, w_down, preferred_element_type=jnp.float32)
    return (stream.astype(jnp.float32) + down).astype(jnp.bfloat16)
```

```python
import functools

import jax
import jax.numpy as jnp
from jax import lax
from jax.experimental import pallas as pl
from jax.experimental.pallas import tpu as pltpu
from jax.sharding import PartitionSpec as P

D = 8192
H = 64
KV = 8
HD = 128
EPS = 1e-6
BF = jnp.bfloat16
F32 = jnp.float32
MESH = pl.DeviceIdType.MESH
VM = pltpu.VMEM
DMA = pltpu.SemaphoreType.DMA
SCORE_SCALE = 1.4426950408889634 / HD**0.5
LOWEST = -1e30
VMEM_LIMIT = 56 * 2**20


def here():
    return lax.axis_index("sp"), lax.axis_index("tp")


def remote(src, dst, send, recv, device):
    return pltpu.make_async_remote_copy(
        src_ref=src,
        dst_ref=dst,
        send_sem=send,
        recv_sem=recv,
        device_id=device,
        device_id_type=MESH,
    )


def chip_at(tp, k, sign):
    chip = tp // 2
    high = (chip // 4 + k // 4) % 2
    x = (chip % 4 + 4 + sign * (k % 4)) % 4
    return (high * 4 + x) * 2 + tp % 2


def greet(devices):
    barrier = pltpu.get_barrier_semaphore()
    for device in devices:
        pl.semaphore_signal(barrier, inc=1, device_id=device, device_id_type=MESH)
    pl.semaphore_wait(barrier, len(devices))


def gather_tp(own_ref, all_ref, same_send, same_recv, pair_send, pair_recv):
    sp, tp = here()
    sibling = (sp, tp + 1 - 2 * (tp % 2))
    for k in range(1, 8):
        remote(own_ref, all_ref.at[tp], same_send.at[k], same_recv.at[k], (sp, chip_at(tp, k, 1))).start()
    remote(own_ref, all_ref.at[tp], pair_send.at[0], pair_recv.at[0], sibling).start()
    all_ref[tp] = own_ref[...]

    def forward(k, _):
        source = chip_at(tp, k, -1)
        block = all_ref.at[source]
        remote(block, block, same_send.at[k], same_recv.at[k], sibling).wait_recv()
        remote(block, block, pair_send.at[k], pair_recv.at[k], sibling).start()
        return 0

    lax.fori_loop(1, 8, forward, 0)

    def settle(k, _):
        source = chip_at(tp, k, -1)
        other = all_ref.at[source + 1 - 2 * (tp % 2)]
        remote(other, other, pair_send.at[k], pair_recv.at[k], sibling).wait_recv()
        remote(own_ref, other, pair_send.at[k], pair_recv.at[k], sibling).wait_send()
        return 0

    lax.fori_loop(0, 8, settle, 0)

    def sent(k, _):
        remote(own_ref, all_ref.at[tp], same_send.at[k], same_recv.at[k], sibling).wait_send()
        return 0

    lax.fori_loop(1, 8, sent, 0)


def attention_kernel(
    offset_ref,
    message_ref,
    cache_k_ref,
    cache_v_ref,
    w_gate_ref,
    w_up_ref,
    attended_ref,
    other_gate_ref,
    other_up_ref,
    received,
    keys,
    vals,
    new_keys,
    new_vals,
    vals_t,
    queries,
    own,
    out_send,
    out_recv,
    stat_send,
    stat_recv,
    a2a_send,
    a2a_recv,
    local_sem,
    pair_send,
    pair_recv,
    q_send,
    q_recv,
    o_send,
    o_recv,
    st_send,
    st_recv,
    ag_send,
    ag_recv,
    fw_send,
    fw_recv,
):
    sp, tp = here()
    core = tp % 2
    chip = tp // 2
    sibling = (sp, tp + 1 - 2 * core)
    greet(
        [((sp + j) % 16, tp) for j in range(1, 16)]
        + [(sp, chip_at(tp, k, 1)) for k in range(1, 8)]
        + [sibling]
    )

    def exchange(j, _):
        target = (sp + j) % 16
        remote(message_ref.at[target], received.at[sp], a2a_send.at[j], a2a_recv.at[j], (target, tp)).start()
        return 0

    lax.fori_loop(1, 16, exchange, 0)
    columns = pl.ds(pl.multiple_of((sp // 2) * HD, HD), HD)
    local_k = pltpu.make_async_copy(cache_k_ref.at[:, columns], keys.at[core], local_sem.at[0])
    local_v = pltpu.make_async_copy(cache_v_ref.at[:, columns], vals.at[core], local_sem.at[1])
    local_k.start()
    local_v.start()
    pair_k = remote(cache_k_ref.at[:, columns], keys.at[core], pair_send.at[0], pair_recv.at[0], sibling)
    pair_v = remote(cache_v_ref.at[:, columns], vals.at[core], pair_send.at[1], pair_recv.at[1], sibling)
    pair_k.start()
    pair_v.start()
    received[sp] = message_ref[sp]

    def arrived(j, _):
        source = (sp + 16 - j) % 16
        block = received.at[source]
        remote(block, block, a2a_send.at[j], a2a_recv.at[j], sibling).wait()
        return 0

    lax.fori_loop(1, 16, arrived, 0)
    queries[0] = received[:, :32, :].reshape(512, HD)

    def ask(k, _):
        remote(queries.at[0], queries.at[k], q_send.at[k], q_recv.at[k], (sp, chip_at(tp, k, 1))).start()
        return 0

    lax.fori_loop(1, 8, ask, 0)
    fresh = received[:, 32:, :].astype(F32).reshape(16, 2, 8, HD)
    new_keys[core] = fresh[:, 0].reshape(HD, HD).astype(BF)
    new_vals[core] = fresh[:, 1].reshape(HD, HD).astype(BF)
    pair_nk = remote(new_keys.at[core], new_keys.at[core], pair_send.at[2], pair_recv.at[2], sibling)
    pair_nv = remote(new_vals.at[core], new_vals.at[core], pair_send.at[3], pair_recv.at[3], sibling)
    pair_nk.start()
    pair_nv.start()
    local_k.wait()
    local_v.wait()
    for copy in (pair_k, pair_v, pair_nk, pair_nv):
        copy.wait()
    pair_g = remote(w_gate_ref, other_gate_ref, pair_send.at[4], pair_recv.at[4], sibling)
    pair_u = remote(w_up_ref, other_up_ref, pair_send.at[5], pair_recv.at[5], sibling)
    pair_g.start()
    pair_u.start()
    for half in range(2):
        for piece in range(4):
            rows = vals[half, piece * 256 : piece * 256 + 256, :].astype(F32)
            vals_t[:, half * 1024 + piece * 256 : half * 1024 + piece * 256 + 256] = rows.T.astype(BF)
    vals_t[:, 2048:2304] = new_vals[...].reshape(256, HD).astype(F32).T.astype(BF)
    cached = offset_ref[0] - chip * 2048
    step = 512

    def attend(k, _):
        asker = chip_at(tp, k, -1)

        @pl.when(k > 0)
        def _():
            remote(queries.at[k], queries.at[k], q_send.at[k], q_recv.at[k], sibling).wait()

        q = queries[k]
        top = jnp.full((1, 512), LOWEST, F32)
        total = jnp.zeros((1, 512), F32)
        summed = jnp.zeros((HD, 512), F32)
        for first in range(0, 2304, step):
            if first < 2048:
                block = keys[first // 1024, first % 1024 : first % 1024 + step, :]
            else:
                block = new_keys[...].reshape(256, HD)
            scores = lax.dot_general(block, q, (((1,), (1,)), ((), ())), preferred_element_type=F32)
            count = block.shape[0]
            place = lax.broadcasted_iota(jnp.int32, (count, 512), 0)
            if first < 2048:
                scores = jnp.where(place < cached - first, scores, LOWEST)
            else:
                lane = lax.broadcasted_iota(jnp.int32, (count, 512), 1)
                token = (lane // 32) * 8 + lane % 8
                scores = jnp.where(place - token <= asker * 128 - chip * 256, scores, LOWEST)
            higher = jnp.maximum(top, jnp.max(scores, axis=0, keepdims=True))
            weights = jnp.exp2((scores - higher) * SCORE_SCALE)
            factor = jnp.exp2((top - higher) * SCORE_SCALE)
            total = total * factor + jnp.sum(weights, axis=0, keepdims=True)
            summed = summed * factor + jnp.dot(
                vals_t[:, first : first + count], weights.astype(BF), preferred_element_type=F32
            )
            top = higher
        out_send[k] = summed.astype(BF)
        stat_send[k] = jnp.concatenate([jnp.broadcast_to(top, (4, 512)), jnp.broadcast_to(total, (4, 512))], 0)

        @pl.when(k > 0)
        def _():
            remote(out_send.at[k], out_recv.at[k], o_send.at[k], o_recv.at[k], (sp, asker)).start()
            remote(stat_send.at[k], stat_recv.at[k], st_send.at[k], st_recv.at[k], (sp, asker)).start()

        return 0

    lax.fori_loop(0, 8, attend, 0)

    def collect(k, _):
        remote(out_send.at[k], out_recv.at[k], o_send.at[k], o_recv.at[k], sibling).wait()
        remote(stat_send.at[k], stat_recv.at[k], st_send.at[k], st_recv.at[k], sibling).wait()
        return 0

    lax.fori_loop(1, 8, collect, 0)
    tops = [stat_send[0, 0:1, :]] + [stat_recv[k, 0:1, :] for k in range(1, 8)]
    highest = functools.reduce(jnp.maximum, tops)
    shares = [jnp.exp2((top - highest) * SCORE_SCALE) for top in tops]
    total = stat_send[0, 4:5, :] * shares[0]
    summed = out_send[0].astype(F32) * shares[0]
    for k in range(1, 8):
        total = total + stat_recv[k, 4:5, :] * shares[k]
        summed = summed + out_recv[k].astype(F32) * shares[k]
    mixed = (summed / total).T.reshape(16, 4, 8, HD)
    for h in range(4):
        own[:, h * HD : (h + 1) * HD] = mixed[:, h].reshape(HD, HD).astype(BF)
    gather_tp(own, attended_ref, ag_send, ag_recv, fw_send, fw_recv)
    pair_g.wait()
    pair_u.wait()


def params(number):
    return pltpu.CompilerParams(
        collective_id=number, has_side_effects=True, vmem_limit_bytes=VMEM_LIMIT
    )


def in_vmem(count):
    return [pl.BlockSpec(memory_space=pltpu.VMEM)] * count


def anywhere(count):
    return [pl.BlockSpec(memory_space=pl.ANY)] * count


def run_attention(offset, message, cache_keys, cache_values, w_gate, w_up):
    return pl.pallas_call(
        attention_kernel,
        out_shape=(
            jax.ShapeDtypeStruct((16, 128, 512), BF),
            jax.ShapeDtypeStruct(w_gate.shape, BF),
            jax.ShapeDtypeStruct(w_up.shape, BF),
        ),
        in_specs=[pl.BlockSpec(memory_space=pltpu.SMEM)] + in_vmem(1) + anywhere(4),
        out_specs=tuple(in_vmem(1) + anywhere(2)),
        scratch_shapes=[
            VM((16, 48, HD), BF),
            VM((2, 1024, HD), BF),
            VM((2, 1024, HD), BF),
            VM((2, 128, HD), BF),
            VM((2, 128, HD), BF),
            VM((HD, 2304), BF),
            VM((8, 512, HD), BF),
            VM((128, 512), BF),
            VM((8, HD, 512), BF),
            VM((8, HD, 512), BF),
            VM((8, 8, 512), F32),
            VM((8, 8, 512), F32),
            DMA((16,)),
            DMA((16,)),
            DMA((2,)),
            DMA((6,)),
            DMA((6,)),
        ]
        + [DMA((8,))] * 10,
        compiler_params=params(0),
        name="attention",
    )(offset, message, cache_keys, cache_values, w_gate, w_up)


def per_device(
    residual,
    queries,
    keys,
    values,
    cache_keys,
    cache_values,
    offset,
    w_out,
    norm_gain,
    w_gate,
    w_up,
    w_down,
):
    asked = jnp.transpose(queries.reshape(8, 16, 4, HD), (1, 2, 0, 3)).reshape(16, 32, HD)
    pairs = jnp.stack([keys.reshape(8, KV, HD), values.reshape(8, KV, HD)], 0)
    pairs = jnp.transpose(pairs, (2, 0, 1, 3)).reshape(KV, 16, HD)
    message = jnp.concatenate([asked, jnp.repeat(pairs, 2, axis=0)], 1)
    attended_all, other_gate, other_up = run_attention(
        offset, message, cache_keys, cache_values, w_gate, w_up
    )
    attended_all = attended_all.reshape(2048, 512)
    attn_out = lax.psum_scatter(
        jnp.dot(attended_all, w_out, preferred_element_type=jnp.float32).astype(jnp.bfloat16),
        "sp",
        scatter_dimension=0,
        tiled=True,
    ).astype(jnp.float32)
    stream = (residual.astype(jnp.float32) + attn_out).astype(jnp.bfloat16)
    wide = stream.astype(jnp.float32)
    squares = lax.psum(jnp.sum(wide * wide, axis=1), "tp")
    scale_rows = lax.rsqrt(squares / D + 1e-06)
    normed = (wide * scale_rows[:, None] * norm_gain.astype(jnp.float32)[None, :]).astype(
        jnp.bfloat16
    )
    normed_all = lax.all_gather(normed, "sp", axis=0, tiled=True)
    both_weights = jnp.concatenate([w_gate, w_up], 1)
    width = w_gate.shape[1]
    both = lax.psum_scatter(
        jnp.dot(normed_all, both_weights, preferred_element_type=jnp.float32).astype(jnp.bfloat16),
        "tp",
        scatter_dimension=0,
        tiled=True,
    ).astype(jnp.float32)
    hidden = (jax.nn.silu(both[:, :width]) * both[:, width:]).astype(jnp.bfloat16)
    hidden_all = lax.all_gather(hidden, "tp", axis=0, tiled=True)
    down = lax.psum_scatter(
        jnp.dot(hidden_all, w_down, preferred_element_type=jnp.float32).astype(jnp.bfloat16),
        "sp",
        scatter_dimension=0,
        tiled=True,
    ).astype(jnp.float32)
    return (wide + down).astype(jnp.bfloat16)


def solution(mesh):
    in_specs = (
        P("sp", "tp"),
        P(("tp", "sp"), None),
        P(("tp", "sp"), None),
        P(("tp", "sp"), None),
        P("tp", None),
        P("tp", None),
        P(),
        P("sp", "tp"),
        P("tp"),
        P("tp", "sp"),
        P("tp", "sp"),
        P("sp", "tp"),
    )
    out_specs = P("sp", "tp")
    return jax.shard_map(
        per_device, mesh=mesh, in_specs=in_specs, out_specs=out_specs, check_vma=False
    )
```

```python
import functools

import jax
import jax.numpy as jnp
from jax import lax
from jax.experimental import pallas as pl
from jax.experimental.pallas import tpu as pltpu
from jax.sharding import PartitionSpec as P

D = 8192
H = 64
KV = 8
HD = 128
EPS = 1e-6
BF = jnp.bfloat16
F32 = jnp.float32
MESH = pl.DeviceIdType.MESH
VM = pltpu.VMEM
DMA = pltpu.SemaphoreType.DMA
SCORE_SCALE = 1.4426950408889634 / HD**0.5
LOWEST = -1e30
VMEM_LIMIT = 56 * 2**20


def here():
    return lax.axis_index("sp"), lax.axis_index("tp")


def remote(src, dst, send, recv, device):
    return pltpu.make_async_remote_copy(
        src_ref=src,
        dst_ref=dst,
        send_sem=send,
        recv_sem=recv,
        device_id=device,
        device_id_type=MESH,
    )


def chip_at(tp, k, sign):
    chip = tp // 2
    high = (chip // 4 + k // 4) % 2
    x = (chip % 4 + 4 + sign * (k % 4)) % 4
    return (high * 4 + x) * 2 + tp % 2


def greet(devices):
    barrier = pltpu.get_barrier_semaphore()
    for device in devices:
        pl.semaphore_signal(barrier, inc=1, device_id=device, device_id_type=MESH)
    pl.semaphore_wait(barrier, len(devices))


def gather_tp(own_ref, all_ref, same_send, same_recv, pair_send, pair_recv):
    sp, tp = here()
    sibling = (sp, tp + 1 - 2 * (tp % 2))
    for k in range(1, 8):
        remote(own_ref, all_ref.at[tp], same_send.at[k], same_recv.at[k], (sp, chip_at(tp, k, 1))).start()
    remote(own_ref, all_ref.at[tp], pair_send.at[0], pair_recv.at[0], sibling).start()
    all_ref[tp] = own_ref[...]

    def forward(k, _):
        source = chip_at(tp, k, -1)
        block = all_ref.at[source]
        remote(block, block, same_send.at[k], same_recv.at[k], sibling).wait_recv()
        remote(block, block, pair_send.at[k], pair_recv.at[k], sibling).start()
        return 0

    lax.fori_loop(1, 8, forward, 0)

    def settle(k, _):
        source = chip_at(tp, k, -1)
        other = all_ref.at[source + 1 - 2 * (tp % 2)]
        remote(other, other, pair_send.at[k], pair_recv.at[k], sibling).wait_recv()
        remote(own_ref, other, pair_send.at[k], pair_recv.at[k], sibling).wait_send()
        return 0

    lax.fori_loop(0, 8, settle, 0)

    def sent(k, _):
        remote(own_ref, all_ref.at[tp], same_send.at[k], same_recv.at[k], sibling).wait_send()
        return 0

    lax.fori_loop(1, 8, sent, 0)


def attention_kernel(
    offset_ref,
    message_ref,
    cache_k_ref,
    cache_v_ref,
    w_gate_ref,
    w_up_ref,
    attended_ref,
    other_gate_ref,
    other_up_ref,
    received,
    keys,
    vals,
    new_keys,
    new_vals,
    vals_t,
    queries,
    own,
    out_send,
    out_recv,
    stat_send,
    stat_recv,
    a2a_send,
    a2a_recv,
    local_sem,
    pair_send,
    pair_recv,
    q_send,
    q_recv,
    o_send,
    o_recv,
    st_send,
    st_recv,
    ag_send,
    ag_recv,
    fw_send,
    fw_recv,
):
    sp, tp = here()
    core = tp % 2
    chip = tp // 2
    sibling = (sp, tp + 1 - 2 * core)
    greet(
        [((sp + j) % 16, tp) for j in range(1, 16)]
        + [(sp, chip_at(tp, k, 1)) for k in range(1, 8)]
        + [sibling]
    )

    def exchange(j, _):
        target = (sp + j) % 16
        remote(message_ref.at[target], received.at[sp], a2a_send.at[j], a2a_recv.at[j], (target, tp)).start()
        return 0

    lax.fori_loop(1, 16, exchange, 0)
    columns = pl.ds(pl.multiple_of((sp // 2) * HD, HD), HD)
    local_k = pltpu.make_async_copy(cache_k_ref.at[:, columns], keys.at[core], local_sem.at[0])
    local_v = pltpu.make_async_copy(cache_v_ref.at[:, columns], vals.at[core], local_sem.at[1])
    local_k.start()
    local_v.start()
    pair_k = remote(cache_k_ref.at[:, columns], keys.at[core], pair_send.at[0], pair_recv.at[0], sibling)
    pair_v = remote(cache_v_ref.at[:, columns], vals.at[core], pair_send.at[1], pair_recv.at[1], sibling)
    pair_k.start()
    pair_v.start()
    received[sp] = message_ref[sp]

    def arrived(j, _):
        source = (sp + 16 - j) % 16
        block = received.at[source]
        remote(block, block, a2a_send.at[j], a2a_recv.at[j], sibling).wait()
        return 0

    lax.fori_loop(1, 16, arrived, 0)
    queries[0] = received[:, :32, :].reshape(512, HD)

    def ask(k, _):
        remote(queries.at[0], queries.at[k], q_send.at[k], q_recv.at[k], (sp, chip_at(tp, k, 1))).start()
        return 0

    lax.fori_loop(1, 8, ask, 0)
    fresh = received[:, 32:, :].astype(F32).reshape(16, 2, 8, HD)
    new_keys[core] = fresh[:, 0].reshape(HD, HD).astype(BF)
    new_vals[core] = fresh[:, 1].reshape(HD, HD).astype(BF)
    pair_nk = remote(new_keys.at[core], new_keys.at[core], pair_send.at[2], pair_recv.at[2], sibling)
    pair_nv = remote(new_vals.at[core], new_vals.at[core], pair_send.at[3], pair_recv.at[3], sibling)
    pair_nk.start()
    pair_nv.start()
    local_k.wait()
    local_v.wait()
    for copy in (pair_k, pair_v, pair_nk, pair_nv):
        copy.wait()
    pair_g = remote(w_gate_ref, other_gate_ref, pair_send.at[4], pair_recv.at[4], sibling)
    pair_u = remote(w_up_ref, other_up_ref, pair_send.at[5], pair_recv.at[5], sibling)
    pair_g.start()
    pair_u.start()
    for half in range(2):
        for piece in range(4):
            rows = vals[half, piece * 256 : piece * 256 + 256, :].astype(F32)
            vals_t[:, half * 1024 + piece * 256 : half * 1024 + piece * 256 + 256] = rows.T.astype(BF)
    vals_t[:, 2048:2304] = new_vals[...].reshape(256, HD).astype(F32).T.astype(BF)
    cached = offset_ref[0] - chip * 2048
    step = 512

    def attend(k, _):
        asker = chip_at(tp, k, -1)

        @pl.when(k > 0)
        def _():
            remote(queries.at[k], queries.at[k], q_send.at[k], q_recv.at[k], sibling).wait()

        q = queries[k]
        top = jnp.full((1, 512), LOWEST, F32)
        total = jnp.zeros((1, 512), F32)
        summed = jnp.zeros((HD, 512), F32)
        for first in range(0, 2304, step):
            if first < 2048:
                block = keys[first // 1024, first % 1024 : first % 1024 + step, :]
            else:
                block = new_keys[...].reshape(256, HD)
            scores = lax.dot_general(block, q, (((1,), (1,)), ((), ())), preferred_element_type=F32)
            count = block.shape[0]
            place = lax.broadcasted_iota(jnp.int32, (count, 512), 0)
            if first < 2048:
                scores = jnp.where(place < cached - first, scores, LOWEST)
            else:
                lane = lax.broadcasted_iota(jnp.int32, (count, 512), 1)
                token = (lane // 32) * 8 + lane % 8
                scores = jnp.where(place - token <= asker * 128 - chip * 256, scores, LOWEST)
            higher = jnp.maximum(top, jnp.max(scores, axis=0, keepdims=True))
            weights = jnp.exp2((scores - higher) * SCORE_SCALE)
            factor = jnp.exp2((top - higher) * SCORE_SCALE)
            total = total * factor + jnp.sum(weights, axis=0, keepdims=True)
            summed = summed * factor + jnp.dot(
                vals_t[:, first : first + count], weights.astype(BF), preferred_element_type=F32
            )
            top = higher
        out_send[k] = summed.astype(BF)
        stat_send[k] = jnp.concatenate([jnp.broadcast_to(top, (4, 512)), jnp.broadcast_to(total, (4, 512))], 0)

        @pl.when(k > 0)
        def _():
            remote(out_send.at[k], out_recv.at[k], o_send.at[k], o_recv.at[k], (sp, asker)).start()
            remote(stat_send.at[k], stat_recv.at[k], st_send.at[k], st_recv.at[k], (sp, asker)).start()

        return 0

    lax.fori_loop(0, 8, attend, 0)

    def collect(k, _):
        remote(out_send.at[k], out_recv.at[k], o_send.at[k], o_recv.at[k], sibling).wait()
        remote(stat_send.at[k], stat_recv.at[k], st_send.at[k], st_recv.at[k], sibling).wait()
        return 0

    lax.fori_loop(1, 8, collect, 0)
    tops = [stat_send[0, 0:1, :]] + [stat_recv[k, 0:1, :] for k in range(1, 8)]
    highest = functools.reduce(jnp.maximum, tops)
    shares = [jnp.exp2((top - highest) * SCORE_SCALE) for top in tops]
    total = stat_send[0, 4:5, :] * shares[0]
    summed = out_send[0].astype(F32) * shares[0]
    for k in range(1, 8):
        total = total + stat_recv[k, 4:5, :] * shares[k]
        summed = summed + out_recv[k].astype(F32) * shares[k]
    mixed = (summed / total).T.reshape(16, 4, 8, HD)
    for h in range(4):
        own[:, h * HD : (h + 1) * HD] = mixed[:, h].reshape(HD, HD).astype(BF)
    gather_tp(own, attended_ref, ag_send, ag_recv, fw_send, fw_recv)
    pair_g.wait()
    pair_u.wait()


def params(number):
    return pltpu.CompilerParams(
        collective_id=number, has_side_effects=True, vmem_limit_bytes=VMEM_LIMIT
    )


def in_vmem(count):
    return [pl.BlockSpec(memory_space=pltpu.VMEM)] * count


def anywhere(count):
    return [pl.BlockSpec(memory_space=pl.ANY)] * count


def run_attention(offset, message, cache_keys, cache_values, w_gate, w_up):
    return pl.pallas_call(
        attention_kernel,
        out_shape=(
            jax.ShapeDtypeStruct((16, 128, 512), BF),
            jax.ShapeDtypeStruct(w_gate.shape, BF),
            jax.ShapeDtypeStruct(w_up.shape, BF),
        ),
        in_specs=[pl.BlockSpec(memory_space=pltpu.SMEM)] + in_vmem(1) + anywhere(4),
        out_specs=tuple(in_vmem(1) + anywhere(2)),
        scratch_shapes=[
            VM((16, 48, HD), BF),
            VM((2, 1024, HD), BF),
            VM((2, 1024, HD), BF),
            VM((2, 128, HD), BF),
            VM((2, 128, HD), BF),
            VM((HD, 2304), BF),
            VM((8, 512, HD), BF),
            VM((128, 512), BF),
            VM((8, HD, 512), BF),
            VM((8, HD, 512), BF),
            VM((8, 8, 512), F32),
            VM((8, 8, 512), F32),
            DMA((16,)),
            DMA((16,)),
            DMA((2,)),
            DMA((6,)),
            DMA((6,)),
        ]
        + [DMA((8,))] * 10,
        compiler_params=params(0),
        name="attention",
    )(offset, message, cache_keys, cache_values, w_gate, w_up)


def scatter_z(product, total, sent, got, cross_send, cross_recv, send_sem, recv_sem, cross_sem):
    sp, tp = here()
    z, low = sp // 2, sp % 2
    neighbours = (((sp + 2) % 16, tp), ((sp + 14) % 16, tp))
    other = (sp + 1 - 2 * low, tp)

    def hop(way, step, b):
        return remote(
            sent.at[way, step, b],
            got.at[way, step, b],
            send_sem.at[way * 8 + step * 2 + b],
            recv_sem.at[way * 8 + step * 2 + b],
            neighbours[way],
        )

    far = product((z + 4) % 8)
    for way in range(2):
        sent[way, 0, way] = far[way * 128 : way * 128 + 128].astype(BF)
        hop(way, 0, way).start()
    for step in range(1, 4):
        distance = 4 - step
        for way in range(2):
            part = product((z + (distance if way == 0 else 8 - distance)) % 8)
            for b in (1 - way, way):
                piece = part[b * 128 : b * 128 + 128]
                if step > 1 or b == way:
                    hop(way, step - 1, b).wait_recv()
                    piece = piece + got[way, step - 1, b].astype(F32)
                sent[way, step, b] = piece.astype(BF)
                hop(way, step, b).start()
    total[...] = product(z).reshape(2, 128, 512)
    for way in range(2):
        for b in range(2):
            hop(way, 3, b).wait_recv()
            total[b] = total[b] + got[way, 3, b].astype(F32)
    cross_send[...] = total[1 - low].astype(BF)
    cross = remote(cross_send, cross_recv, cross_sem.at[0], cross_sem.at[1], other)
    cross.start()
    for way in range(2):
        hop(way, 0, way).wait_send()
        for step in range(1, 4):
            for b in range(2):
                hop(way, step, b).wait_send()
    cross.wait()
    return total[low] + cross_recv[...].astype(F32)


def gather_z(own, blocks, paired, send_sem, recv_sem, cross_sem, pair_send, pair_recv):
    sp, tp = here()
    z, low = sp // 2, sp % 2
    core = tp % 2
    neighbours = (((sp + 2) % 16, tp), ((sp + 14) % 16, tp))
    other = (sp + 1 - 2 * low, tp)
    sibling = (sp, tp + 1 - 2 * core)

    def hop(way, distance, place, b):
        block = blocks.at[place, b]
        index = way * 10 + distance * 2 + b
        return remote(block, block, send_sem.at[index], recv_sem.at[index], neighbours[way])

    def pass_on(place, b, offset):
        @pl.when(b == 1 - core)
        def _():
            remote(blocks.at[place, b], paired.at[place], pair_send.at[offset], pair_recv.at[offset], sibling).start()

    def from_way(way, distance):
        return (z + (8 - distance if way == 0 else distance)) % 8

    blocks[z, low] = own[...]
    cross = remote(own, blocks.at[z, low], cross_sem.at[0], cross_sem.at[1], other)
    cross.start()
    for way in range(2):
        hop(way, 1, z, low).start()
    pass_on(z, low, 0)
    came = blocks.at[z, 1 - low]
    remote(own, came, cross_sem.at[0], cross_sem.at[1], other).wait_recv()
    for way in range(2):
        hop(way, 1, z, 1 - low).start()
    pass_on(z, 1 - low, 0)
    for distance in range(1, 4):
        for b in (low, 1 - low):
            for way in range(2):
                place = from_way(way, distance)
                hop(way, distance, place, b).wait_recv()
                if distance < 3:
                    hop(way, distance + 1, place, b).start()
                else:

                    @pl.when(b == way)
                    def _():
                        hop(way, 4, place, b).start()

                pass_on(place, b, distance if way == 0 else 8 - distance)
    for way in range(2):
        place = (z + 4) % 8
        hop(way, 4, place, way).wait_recv()
        pass_on(place, way, 4)
    cross.wait_send()
    for way in range(2):
        for distance in range(1, 4):
            for b in range(2):
                hop(way, distance, z, b).wait_send()
        hop(way, 4, z, way).wait_send()

    def settle(offset, _):
        place = (z + 8 - offset) % 8
        remote(blocks.at[place, 0], paired.at[place], pair_send.at[offset], pair_recv.at[offset], sibling).wait()
        return 0

    lax.fori_loop(0, 8, settle, 0)


def tail_kernel(
    attended_ref,
    w_out_ref,
    residual_ref,
    gain_ref,
    w_gate_ref,
    w_up_ref,
    other_gate_ref,
    other_up_ref,
    w_down_ref,
    out_ref,
    stream,
    total,
    sent_a,
    got_a,
    sent_d,
    got_d,
    cross_a,
    cross_d,
    squares,
    own_squares,
    own_normed,
    normed,
    paired,
    x_sent,
    x_got,
    y_sent,
    y_got,
    own_hidden,
    hidden,
    za_send,
    za_recv,
    zd_send,
    zd_recv,
    ca_sem,
    cd_sem,
    cn_sem,
    sq_send,
    sq_recv,
    zn_send,
    zn_recv,
    pn_send,
    pn_recv,
    x_send,
    x_recv,
    y_sem,
    ag_send,
    ag_recv,
    fw_send,
    fw_recv,
):
    sp, tp = here()
    core, chip = tp % 2, tp // 2
    high, x = chip // 4, chip % 4
    greet(
        [((sp + 2) % 16, tp), ((sp + 14) % 16, tp), (sp + 1 - 2 * (sp % 2), tp)]
        + [(sp, (tp + j) % 16) for j in range(1, 16)]
    )
    attended = attended_ref
    attn_out = scatter_z(
        lambda place: jnp.dot(attended[place], w_out_ref[...], preferred_element_type=F32),
        total, sent_a, got_a, cross_a.at[0], cross_a.at[1], za_send, za_recv, ca_sem,
    )
    stream[...] = (residual_ref[...].astype(F32) + attn_out).astype(BF)
    wide = stream[...].astype(F32)
    square = wide * wide
    square = square[:, :128] + square[:, 128:256] + square[:, 256:384] + square[:, 384:]
    own_squares[...] = jnp.broadcast_to(jnp.sum(square.T, axis=0, keepdims=True), (8, 128))
    squares[tp] = own_squares[...]

    def tell(j, _):
        remote(own_squares, squares.at[tp], sq_send.at[j], sq_recv.at[j], (sp, (tp + j) % 16)).start()
        return 0

    lax.fori_loop(1, 16, tell, 0)

    def told(j, _):
        block = squares.at[(tp + 16 - j) % 16]
        remote(own_squares, block, sq_send.at[j], sq_recv.at[j], (sp, (tp + j) % 16)).wait()
        return 0

    lax.fori_loop(1, 16, told, 0)
    summed = jnp.sum(squares[...], axis=0)
    scale = lax.rsqrt(jnp.broadcast_to(summed[0:1], (128, 128)).T / D + EPS)
    scale = jnp.concatenate([scale] * 4, axis=1)
    own_normed[...] = (stream[...].astype(F32) * scale * gain_ref[...]).astype(BF)
    gather_z(own_normed, normed, paired, zn_send, zn_recv, cn_sem, pn_send, pn_recv)

    def part(upper, column, up):
        place = upper * 4 + (x + column) % 4
        mine, others = (w_up_ref, other_up_ref) if up else (w_gate_ref, other_gate_ref)
        return jnp.dot(normed[place, core], mine[...], preferred_element_type=F32) + jnp.dot(
            paired[place], others[...], preferred_element_type=F32
        )

    neighbours = (
        (sp, (high * 4 + (x + 1) % 4) * 2 + core),
        (sp, (high * 4 + (x + 3) % 4) * 2 + core),
    )

    def hop(turn, which):
        index = turn * 6 + which
        return remote(
            x_sent.at[index], x_got.at[index], x_send.at[index], x_recv.at[index], neighbours[which // 3]
        )

    def post(turn, which, value):
        x_sent[turn * 6 + which] = value.astype(BF)
        hop(turn, which).start()

    def arrived(turn, which):
        hop(turn, which).wait_recv()
        return x_got[turn * 6 + which].astype(F32)

    uppers = (1 - high, high)

    def open_turn(turn):
        upper = uppers[turn]
        post(turn, 0, part(upper, 2, False))
        post(turn, 3, part(upper, 2, True))
        post(turn, 2, part(upper, 1, True))
        post(turn, 5, part(upper, 3, False))

    def second_hop(turn):
        upper = uppers[turn]
        gate = part(upper, 1, False)
        post(turn, 1, gate + arrived(turn, 0))
        up = part(upper, 3, True)
        post(turn, 4, up + arrived(turn, 3))

    def close_turn(turn, up):
        value = part(uppers[turn], 0, up)
        first, second = (2, 4) if up else (5, 1)
        return value + arrived(turn, first) + arrived(turn, second)

    opposite = (sp, ((1 - high) * 4 + x) * 2 + core)

    def over(index):
        return remote(y_sent.at[index], y_got.at[index], y_sem.at[index], y_sem.at[2 + index], opposite)

    open_turn(0)
    second_hop(0)
    open_turn(1)
    for index in range(2):
        y_sent[index] = close_turn(0, index == 1).astype(BF)
        over(index).start()
    second_hop(1)
    gate = close_turn(1, False)
    up = close_turn(1, True)
    over(0).wait()
    gate = gate + y_got[0].astype(F32)
    over(1).wait()
    up = up + y_got[1].astype(F32)
    own_hidden[...] = (gate / (1.0 + jnp.exp(-gate)) * up).astype(BF)
    gather_tp(own_hidden, hidden, ag_send, ag_recv, fw_send, fw_recv)
    for turn in range(2):
        for which in range(6):
            hop(turn, which).wait_send()

    def down(place):
        first = jnp.dot(hidden[2 * place], w_down_ref[...], preferred_element_type=F32)
        second = jnp.dot(hidden[2 * place + 1], w_down_ref[...], preferred_element_type=F32)
        return jnp.concatenate([first, second], 0)

    added = scatter_z(down, total, sent_d, got_d, cross_d.at[0], cross_d.at[1], zd_send, zd_recv, cd_sem)
    out_ref[...] = (stream[...].astype(F32) + added).astype(BF)


def run_tail(attended, w_out, residual, gain, w_gate, w_up, other_gate, other_up, w_down):
    hop = VM((2, 4, 2, 128, 512), BF)
    return pl.pallas_call(
        tail_kernel,
        out_shape=jax.ShapeDtypeStruct((128, 512), BF),
        in_specs=in_vmem(9),
        out_specs=in_vmem(1)[0],
        scratch_shapes=[
            VM((128, 512), BF),
            VM((2, 128, 512), F32),
            hop,
            hop,
            hop,
            hop,
            VM((2, 128, 512), BF),
            VM((2, 128, 512), BF),
            VM((16, 8, 128), F32),
            VM((8, 128), F32),
            VM((128, 512), BF),
            VM((8, 2, 128, 512), BF),
            VM((8, 128, 512), BF),
            VM((12, 128, 1024), BF),
            VM((12, 128, 1024), BF),
            VM((2, 128, 1024), BF),
            VM((2, 128, 1024), BF),
            VM((128, 1024), BF),
            VM((16, 128, 1024), BF),
        ]
        + [DMA((16,))] * 4
        + [DMA((2,))] * 3
        + [DMA((16,))] * 2
        + [DMA((20,))] * 2
        + [DMA((8,))] * 2
        + [DMA((12,))] * 2
        + [DMA((4,))]
        + [DMA((8,))] * 4,
        compiler_params=params(1),
        name="tail",
    )(attended, w_out, residual, gain, w_gate, w_up, other_gate, other_up, w_down)


def per_device(
    residual,
    queries,
    keys,
    values,
    cache_keys,
    cache_values,
    offset,
    w_out,
    norm_gain,
    w_gate,
    w_up,
    w_down,
):
    asked = jnp.transpose(queries.reshape(8, 16, 4, HD), (1, 2, 0, 3)).reshape(16, 32, HD)
    pairs = jnp.stack([keys.reshape(8, KV, HD), values.reshape(8, KV, HD)], 0)
    pairs = jnp.transpose(pairs, (2, 0, 1, 3)).reshape(KV, 16, HD)
    message = jnp.concatenate([asked, jnp.repeat(pairs, 2, axis=0)], 1)
    attended_all, other_gate, other_up = run_attention(
        offset, message, cache_keys, cache_values, w_gate, w_up
    )
    gain = norm_gain.astype(F32).reshape(1, 512)
    return run_tail(
        attended_all.reshape(8, 256, 512),
        w_out,
        residual,
        gain,
        w_gate,
        w_up,
        other_gate,
        other_up,
        w_down,
    )


def solution(mesh):
    in_specs = (
        P("sp", "tp"),
        P(("tp", "sp"), None),
        P(("tp", "sp"), None),
        P(("tp", "sp"), None),
        P("tp", None),
        P("tp", None),
        P(),
        P("sp", "tp"),
        P("tp"),
        P("tp", "sp"),
        P("tp", "sp"),
        P("sp", "tp"),
    )
    out_specs = P("sp", "tp")
    return jax.shard_map(
        per_device, mesh=mesh, in_specs=in_specs, out_specs=out_specs, check_vma=False
    )
```

```python
import functools

import jax
import jax.numpy as jnp
from jax import lax
from jax.experimental import pallas as pl
from jax.experimental.pallas import tpu as pltpu
from jax.sharding import PartitionSpec as P

D = 8192
H = 64
KV = 8
HD = 128
EPS = 1e-6
BF = jnp.bfloat16
F32 = jnp.float32
MESH = pl.DeviceIdType.MESH
VM = pltpu.VMEM
DMA = pltpu.SemaphoreType.DMA
SCORE_SCALE = 1.4426950408889634 / HD**0.5
LOWEST = -1e30
VMEM_LIMIT = 56 * 2**20


def remote(src, dst, send, recv, device):
    return pltpu.make_async_remote_copy(
        src_ref=src,
        dst_ref=dst,
        send_sem=send,
        recv_sem=recv,
        device_id=device,
        device_id_type=MESH,
    )


def tp_of(place, x):
    return ((place // 2) * 4 + x) * 2 + place % 2


def greet(devices):
    barrier = pltpu.get_barrier_semaphore()
    for device in devices:
        pl.semaphore_signal(barrier, inc=1, device_id=device, device_id_type=MESH)
    pl.semaphore_wait(barrier, len(devices))


class Spread:
    def __init__(self, source, buffer, sems, first, local=True):
        sp, tp = lax.axis_index("sp"), lax.axis_index("tp")
        high, x, core = tp // 8, (tp // 2) % 4, tp % 2
        self.sems = sems
        self.first = first
        self.buffer = buffer
        self.sibling = (sp, tp + 1 - 2 * core)
        opposite = (sp, (tp + 8) % 16)
        mine = buffer.at[high * 2 + core]
        self.local = pltpu.make_async_copy(source, mine, sems.at[first]) if local else None
        self.pair = remote(source, mine, sems.at[first + 1], sems.at[first + 2], self.sibling)
        self.over = remote(source, mine, sems.at[first + 3], sems.at[first + 4], opposite)
        across = buffer.at[(1 - high) * 2 + core]
        self.passed = remote(across, across, sems.at[first + 5], sems.at[first + 6], self.sibling)

    def keep(self):
        self.local.start()

    def send(self):
        self.over.start()
        self.pair.start()

    def forward(self):
        self.over.wait_recv()
        self.passed.start()

    def finish(self):
        if self.local is not None:
            self.local.wait()
        self.pair.wait()
        self.over.wait_send()
        self.passed.wait()


def gather_x(own, blocks, send_sem, recv_sem):
    sp, tp = lax.axis_index("sp"), lax.axis_index("tp")
    x, place = (tp // 2) % 4, (tp // 8) * 2 + tp % 2
    copies = [
        remote(own, blocks.at[x], send_sem.at[k], recv_sem.at[k], (sp, tp_of(place, (x + k) % 4)))
        for k in (1, 3, 2)
    ]
    for copy in copies:
        copy.start()
    blocks[x] = own[...]
    for copy in copies:
        copy.wait()


def scatter_z(product, sent, got, cross_send, cross_recv, send_sem, recv_sem, cross_sem):
    sp, tp = lax.axis_index("sp"), lax.axis_index("tp")
    z, low = sp // 2, sp % 2
    neighbours = (((sp + 2) % 16, tp), ((sp + 14) % 16, tp))
    other = (sp + 1 - 2 * low, tp)

    def hop(way, step, r):
        index = way * 8 + step * 2 + r
        return remote(
            sent.at[way, step, r], got.at[way, step, r], send_sem.at[index], recv_sem.at[index], neighbours[way]
        )

    def split(place):
        part = product(place)
        return jnp.where(low == 0, part[32:], part[:32]), jnp.where(low == 0, part[:32], part[32:])

    far = split((z + 4) % 8)
    for way in range(2):
        sent[way, 0, way] = far[way].astype(BF)
        hop(way, 0, way).start()
    for step in range(1, 4):
        parts = [split((z + 4 - step) % 8), split((z + 4 + step) % 8)]
        for r in range(2):
            for way in range(2):
                piece = parts[way][r]
                if step > 1 or r == way:
                    hop(way, step - 1, r).wait_recv()
                    piece = piece + got[way, step - 1, r].astype(F32)
                sent[way, step, r] = piece.astype(BF)
                hop(way, step, r).start()
    away, mine = split(z)
    for way in range(2):
        hop(way, 3, 0).wait_recv()
        away = away + got[way, 3, 0].astype(F32)
    cross_send[...] = away.astype(BF)
    cross = remote(cross_send, cross_recv, cross_sem.at[0], cross_sem.at[1], other)
    cross.start()
    for way in range(2):
        hop(way, 3, 1).wait_recv()
        mine = mine + got[way, 3, 1].astype(F32)
    for way in range(2):
        hop(way, 0, way).wait_send()
        for step in range(1, 4):
            for r in range(2):
                hop(way, step, r).wait_send()
    cross.wait()
    return mine + cross_recv[...].astype(F32)


def gather_z(own, blocks, send_sem, recv_sem, cross_sem):
    sp, tp = lax.axis_index("sp"), lax.axis_index("tp")
    z, low = sp // 2, sp % 2
    neighbours = (((sp + 2) % 16, tp), ((sp + 14) % 16, tp))
    other = (sp + 1 - 2 * low, tp)

    def hop(way, distance, place, r):
        block = blocks.at[place, low if r == 0 else 1 - low]
        index = way * 10 + distance * 2 + r
        return remote(block, block, send_sem.at[index], recv_sem.at[index], neighbours[way])

    blocks[z, low] = own[...]
    cross = remote(own, blocks.at[z, low], cross_sem.at[0], cross_sem.at[1], other)
    cross.start()
    for way in range(2):
        hop(way, 1, z, 0).start()
    remote(own, blocks.at[z, 1 - low], cross_sem.at[0], cross_sem.at[1], other).wait_recv()
    for way in range(2):
        hop(way, 1, z, 1).start()
    for distance in range(1, 4):
        for r in range(2):
            for way in range(2):
                place = (z + (8 - distance if way == 0 else distance)) % 8
                hop(way, distance, place, r).wait_recv()
                if distance < 3 or r == way:
                    hop(way, distance + 1, place, r).start()
    for way in range(2):
        hop(way, 4, (z + 4) % 8, way).wait_recv()
    cross.wait_send()
    for way in range(2):
        for distance in range(1, 4):
            for r in range(2):
                hop(way, distance, z, r).wait_send()
        hop(way, 4, z, way).wait_send()


def block_kernel(
    offset_ref,
    message_ref,
    residual_ref,
    gain_ref,
    cache_k_ref,
    cache_v_ref,
    w_out_ref,
    w_gate_ref,
    w_up_ref,
    w_down_ref,
    out_ref,
    received,
    keys,
    own_vals,
    vals_t,
    new_keys,
    new_vals_t,
    own_queries,
    queries,
    out_send,
    out_recv,
    stat_send,
    stat_recv,
    own_attended,
    attended,
    w_out,
    w_gate,
    w_up,
    w_down,
    gains,
    residuals,
    stream,
    sent_a,
    got_a,
    sent_d,
    got_d,
    cross_a,
    cross_d,
    own_squares,
    squares,
    own_normed,
    normed,
    x_sent,
    x_got,
    own_hidden,
    hidden,
    own_out,
    a2a_send,
    a2a_recv,
    spread_sem,
    small_sem,
    q_send,
    q_recv,
    o_send,
    o_recv,
    st_send,
    st_recv,
    aa_send,
    aa_recv,
    za_send,
    za_recv,
    sq_send,
    sq_recv,
    zn_send,
    zn_recv,
    x_send,
    x_recv,
    ah_send,
    ah_recv,
    zd_send,
    zd_recv,
    cross_sem,
    back_sem,
):
    sp, tp = lax.axis_index("sp"), lax.axis_index("tp")
    high, x, core = tp // 8, (tp // 2) % 4, tp % 2
    place = high * 2 + core
    greet([((sp + j) % 16, tp) for j in range(1, 16)] + [(sp, (tp + j) % 16) for j in range(1, 16)])

    def exchange(j, _):
        target = (sp + j) % 16
        remote(message_ref.at[target], received.at[sp], a2a_send.at[j], a2a_recv.at[j], (target, tp)).start()
        return 0

    lax.fori_loop(1, 16, exchange, 0)
    columns = pl.ds(pl.multiple_of((sp // 2) * HD, HD), HD)
    spread_k = Spread(cache_k_ref.at[:, columns], keys, spread_sem, 0)
    spread_v = Spread(vals_t.at[place], vals_t, spread_sem, 7, local=False)
    spread_o = Spread(w_out_ref, w_out, spread_sem, 14)
    spread_g = Spread(w_gate_ref, w_gate, spread_sem, 21)
    spread_u = Spread(w_up_ref, w_up, spread_sem, 28)
    spread_d = Spread(w_down_ref, w_down, spread_sem, 35)
    load_v = pltpu.make_async_copy(cache_v_ref.at[:, columns], own_vals, small_sem.at[0])
    load_v.start()
    spread_k.keep()
    spread_k.send()
    received[sp] = message_ref[sp]
    load_v.wait()
    for piece in range(4):
        rows = own_vals[piece * 256 : piece * 256 + 256, :].astype(F32)
        vals_t[place, :, piece * 256 : piece * 256 + 256] = rows.T.astype(BF)
    spread_v.send()
    for spread in (spread_o, spread_g, spread_u, spread_d):
        spread.keep()

    def arrived(j, _):
        block = received.at[(sp + 16 - j) % 16]
        remote(block, block, a2a_send.at[j], a2a_recv.at[j], (sp, tp)).wait()
        return 0

    lax.fori_loop(1, 16, arrived, 0)
    own_queries[...] = received[:, :32, :].reshape(4, 128, HD)
    queries[x, place] = own_queries[place]

    def ask(i, _):
        target = tp_of(i % 4, (x + i // 4) % 4)
        j = (target - tp + 16) % 16

        @pl.when(j > 0)
        def _():
            remote(own_queries.at[i % 4], queries.at[x, place], q_send.at[j], q_recv.at[j], (sp, target)).start()

        return 0

    lax.fori_loop(0, 16, ask, 0)
    fresh = received[:, 32:, :].astype(F32).reshape(16, 2, 8, HD)
    new_keys[place] = fresh[:, 0].reshape(HD, HD).astype(BF)
    new_vals_t[place] = fresh[:, 1].reshape(HD, HD).T.astype(BF)

    def quad(i):
        peer = (place + i) % 4
        return (sp, tp_of(peer, x))

    def to_quad(i, kind, src, dst):
        index = 1 + kind * 6 + (i - 1) * 2
        return remote(src, dst, small_sem.at[index], small_sem.at[index + 1], quad(i))

    smalls = []
    for i in range(1, 4):
        peer = (place + i) % 4
        rows = pl.ds(pl.multiple_of(peer * 32, 32), 32)
        smalls.append(to_quad(i, 0, new_keys.at[place], new_keys.at[place]))
        smalls.append(to_quad(i, 1, new_vals_t.at[place], new_vals_t.at[place]))
        smalls.append(to_quad(i, 2, residual_ref.at[rows], residuals.at[place]))
        smalls.append(to_quad(i, 3, gain_ref, gains.at[place]))
    for copy in smalls:
        copy.start()
    residuals[place] = residual_ref[pl.ds(pl.multiple_of(place * 32, 32), 32)]
    gains[place] = gain_ref[...]
    spread_k.forward()
    spread_v.forward()
    spread_k.finish()
    spread_v.finish()
    for copy in smalls:
        copy.wait()
    spread_o.send()
    spread_g.send()

    def attend(k, _):
        asker = (x + 4 - k) % 4
        for source in range(4):
            j = (tp - tp_of(source, asker) + 16) % 16

            @pl.when(j > 0)
            def _():
                block = queries.at[asker, source]
                remote(block, block, q_send.at[j], q_recv.at[j], (sp, tp)).wait_recv()

        q = queries[asker].reshape(512, HD)
        top = jnp.full((1, 512), LOWEST, F32)
        total = jnp.zeros((1, 512), F32)
        summed = jnp.zeros((HD, 512), F32)
        lane = lax.broadcasted_iota(jnp.int32, (128, 512), 1)
        token = ((lane // 256) * 4 + asker) * 256 + ((lane // 128) % 2) * 128
        token = token + place * 32 + ((lane // 32) % 4) * 8 + lane % 8
        ahead = lax.broadcasted_iota(jnp.int32, (128, 512), 0) - token
        for chunk in range(9):
            held, first = chunk // 2, (chunk % 2) * 512
            if chunk < 8:
                block = keys[held, first : first + 512, :]
                block_t = vals_t[held, :, first : first + 512]
            else:
                block = new_keys[...].reshape(512, HD)
                block_t = jnp.concatenate([new_vals_t[i] for i in range(4)], 1)
            scores = lax.dot_general(block, q, (((1,), (1,)), ((), ())), preferred_element_type=F32)
            if chunk < 8:
                position = lax.broadcasted_iota(jnp.int32, (512, 512), 0)
                scores = jnp.where(position < offset_ref[0] - tp_of(held, x) * 1024 - first, scores, LOWEST)
            else:
                scores = jnp.concatenate(
                    [
                        jnp.where(ahead <= -tp_of(i, x) * 128, scores[i * 128 : i * 128 + 128], LOWEST)
                        for i in range(4)
                    ],
                    0,
                )
            higher = jnp.maximum(top, jnp.max(scores, axis=0, keepdims=True))
            weights = jnp.exp2((scores - higher) * SCORE_SCALE)
            factor = jnp.exp2((top - higher) * SCORE_SCALE)
            total = total * factor + jnp.sum(weights, axis=0, keepdims=True)
            summed = summed * factor + jnp.dot(block_t, weights.astype(BF), preferred_element_type=F32)
            top = higher
        out_send[k] = summed.astype(BF)
        stat_send[k] = jnp.concatenate([jnp.broadcast_to(top, (4, 512)), jnp.broadcast_to(total, (4, 512))], 0)

        @pl.when(k > 0)
        def _():
            target = (sp, tp_of(place, asker))
            remote(out_send.at[k], out_recv.at[k], o_send.at[k], o_recv.at[k], target).start()
            remote(stat_send.at[k], stat_recv.at[k], st_send.at[k], st_recv.at[k], target).start()

        return 0

    lax.fori_loop(0, 4, attend, 0)
    spread_o.forward()
    spread_u.send()

    def asked(j, _):
        remote(own_queries.at[0], queries.at[x, place], q_send.at[j], q_recv.at[j], (sp, tp)).wait_send()
        return 0

    lax.fori_loop(1, 16, asked, 0)

    def collect(k, _):
        remote(out_send.at[k], out_recv.at[k], o_send.at[k], o_recv.at[k], (sp, tp)).wait()
        remote(stat_send.at[k], stat_recv.at[k], st_send.at[k], st_recv.at[k], (sp, tp)).wait()
        return 0

    lax.fori_loop(1, 4, collect, 0)
    tops = [stat_send[0, 0:1, :]] + [stat_recv[k, 0:1, :] for k in range(1, 4)]
    highest = functools.reduce(jnp.maximum, tops)
    shares = [jnp.exp2((top - highest) * SCORE_SCALE) for top in tops]
    total = stat_send[0, 4:5, :] * shares[0]
    summed = out_send[0].astype(F32) * shares[0]
    for k in range(1, 4):
        total = total + stat_recv[k, 4:5, :] * shares[k]
        summed = summed + out_recv[k].astype(F32) * shares[k]
    mixed = (summed / total).T.reshape(16, 4, 8, HD)
    for h in range(4):
        own_attended[:, :, h * HD : (h + 1) * HD] = mixed[:, h].reshape(2, 64, HD).astype(BF)
    gather_x(own_attended, attended, aa_send, aa_recv)
    spread_o.finish()

    def project(z):
        rows = attended[z % 4, z // 4]
        return jnp.concatenate(
            [jnp.dot(rows, w_out[i], preferred_element_type=F32) for i in range(4)], 1
        )

    attn_out = scatter_z(
        project, sent_a, got_a, cross_a.at[0], cross_a.at[1], za_send, za_recv, cross_sem.at[pl.ds(0, 2)]
    )
    spread_g.forward()
    spread_u.forward()
    spread_d.send()
    own_residual = jnp.concatenate([residuals[i] for i in range(4)], 1)
    stream[...] = (own_residual.astype(F32) + attn_out).astype(BF)
    wide = stream[...].astype(F32)
    own_squares[...] = jnp.broadcast_to(jnp.sum(wide * wide, axis=1, keepdims=True), (32, 128))
    tells = [
        remote(own_squares, squares.at[k], sq_send.at[k], sq_recv.at[k], (sp, tp_of(place, (x + k) % 4)))
        for k in range(1, 4)
    ]
    for copy in tells:
        copy.start()
    for copy in tells:
        copy.wait()
    mean = (own_squares[...] + squares[1] + squares[2] + squares[3]) / D
    scale = jnp.concatenate([lax.rsqrt(mean + EPS)] * 16, 1)
    gain = jnp.concatenate([gains[i, 0:1, :] for i in range(4)], 1)
    own_normed[...] = (stream[...].astype(F32) * scale * gain).astype(BF)
    gather_z(own_normed, normed, zn_send, zn_recv, cross_sem.at[pl.ds(2, 2)])
    spread_d.forward()
    spread_g.finish()
    spread_u.finish()

    def part(column, up):
        rows = normed[pl.ds(2 * ((x + column) % 4), 2)].reshape(128, 2048)
        weight = w_up if up else w_gate
        return jnp.dot(rows, weight[...].reshape(2048, 1024), preferred_element_type=F32)

    neighbours = ((sp, tp_of(place, (x + 1) % 4)), (sp, tp_of(place, (x + 3) % 4)))

    def hop(which):
        return remote(
            x_sent.at[which], x_got.at[which], x_send.at[which], x_recv.at[which], neighbours[which // 3]
        )

    def post(which, value):
        x_sent[which] = value.astype(BF)
        hop(which).start()

    def came(which):
        hop(which).wait_recv()
        return x_got[which].astype(F32)

    post(0, part(2, False))
    post(3, part(2, True))
    post(2, part(1, True))
    post(5, part(3, False))
    second = part(1, False)
    post(1, second + came(0))
    second = part(3, True)
    post(4, second + came(3))
    gate = part(0, False)
    up = part(0, True)
    gate = gate + came(5) + came(1)
    up = up + came(2) + came(4)
    own_hidden[...] = (gate / (1.0 + jnp.exp(-gate)) * up).astype(BF).reshape(2, 64, 1024)
    gather_x(own_hidden, hidden, ah_send, ah_recv)
    spread_d.finish()
    for which in range(6):
        hop(which).wait_send()

    def down(z):
        rows = hidden[z // 2, z % 2]
        return jnp.concatenate(
            [jnp.dot(rows, w_down[i], preferred_element_type=F32) for i in range(4)], 1
        )

    added = scatter_z(
        down, sent_d, got_d, cross_d.at[0], cross_d.at[1], zd_send, zd_recv, cross_sem.at[pl.ds(4, 2)]
    )
    result = (stream[...].astype(F32) + added).astype(BF)
    for i in range(4):
        own_out[i] = result[:, i * 512 : i * 512 + 512]
    mine = pl.ds(pl.multiple_of(place * 32, 32), 32)
    backs = [
        remote(own_out.at[(place + i) % 4], out_ref.at[mine], back_sem.at[2 * i], back_sem.at[2 * i + 1], quad(i))
        for i in range(1, 4)
    ]
    for copy in backs:
        copy.start()
    out_ref[mine] = own_out[place]
    for copy in backs:
        copy.wait()


def run_block(offset, message, residual, gain, cache_keys, cache_values, w_out, w_gate, w_up, w_down):
    hop = VM((2, 4, 2, 32, 2048), BF)
    vmem = pl.BlockSpec(memory_space=pltpu.VMEM)
    return pl.pallas_call(
        block_kernel,
        out_shape=jax.ShapeDtypeStruct((128, 512), BF),
        in_specs=[pl.BlockSpec(memory_space=pltpu.SMEM)] + [vmem] * 3 + [pl.BlockSpec(memory_space=pl.ANY)] * 6,
        out_specs=vmem,
        scratch_shapes=[
            VM((16, 48, HD), BF),
            VM((4, 1024, HD), BF),
            VM((1024, HD), BF),
            VM((4, HD, 1024), BF),
            VM((4, 128, HD), BF),
            VM((4, HD, 128), BF),
            VM((4, 128, HD), BF),
            VM((4, 4, 128, HD), BF),
            VM((4, HD, 512), BF),
            VM((4, HD, 512), BF),
            VM((4, 8, 512), F32),
            VM((4, 8, 512), F32),
            VM((2, 64, 512), BF),
            VM((4, 2, 64, 512), BF),
            VM((4, 512, 512), BF),
            VM((4, 512, 1024), BF),
            VM((4, 512, 1024), BF),
            VM((4, 1024, 512), BF),
            VM((4, 8, 512), F32),
            VM((4, 32, 512), BF),
            VM((32, 2048), BF),
            hop,
            hop,
            hop,
            hop,
            VM((2, 32, 2048), BF),
            VM((2, 32, 2048), BF),
            VM((32, 128), F32),
            VM((4, 32, 128), F32),
            VM((32, 2048), BF),
            VM((8, 2, 32, 2048), BF),
            VM((6, 128, 1024), BF),
            VM((6, 128, 1024), BF),
            VM((2, 64, 1024), BF),
            VM((4, 2, 64, 1024), BF),
            VM((4, 32, 512), BF),
        ]
        + [DMA((16,))] * 2
        + [DMA((42,)), DMA((25,))]
        + [DMA((16,))] * 2
        + [DMA((4,))] * 6
        + [DMA((16,))] * 2
        + [DMA((4,))] * 2
        + [DMA((20,))] * 2
        + [DMA((6,))] * 2
        + [DMA((4,))] * 2
        + [DMA((16,))] * 2
        + [DMA((6,)), DMA((8,))],
        compiler_params=pltpu.CompilerParams(
            collective_id=0, has_side_effects=True, vmem_limit_bytes=VMEM_LIMIT
        ),
        name="block",
    )(offset, message, residual, gain, cache_keys, cache_values, w_out, w_gate, w_up, w_down)


def per_device(
    residual,
    queries,
    keys,
    values,
    cache_keys,
    cache_values,
    offset,
    w_out,
    norm_gain,
    w_gate,
    w_up,
    w_down,
):
    asked = jnp.transpose(queries.reshape(8, 16, 4, HD), (1, 2, 0, 3)).reshape(16, 32, HD)
    pairs = jnp.stack([keys.reshape(8, KV, HD), values.reshape(8, KV, HD)], 0)
    pairs = jnp.transpose(pairs, (2, 0, 1, 3)).reshape(KV, 16, HD)
    message = jnp.concatenate([asked, jnp.repeat(pairs, 2, axis=0)], 1)
    gain = jnp.broadcast_to(norm_gain.astype(F32)[None, :], (8, 512))
    return run_block(
        offset, message, residual, gain, cache_keys, cache_values, w_out, w_gate, w_up, w_down
    )


def solution(mesh):
    in_specs = (
        P("sp", "tp"),
        P(("tp", "sp"), None),
        P(("tp", "sp"), None),
        P(("tp", "sp"), None),
        P("tp", None),
        P("tp", None),
        P(),
        P("sp", "tp"),
        P("tp"),
        P("tp", "sp"),
        P("tp", "sp"),
        P("sp", "tp"),
    )
    out_specs = P("sp", "tp")
    return jax.shard_map(
        per_device, mesh=mesh, in_specs=in_specs, out_specs=out_specs, check_vma=False
    )
```

```python
import functools

import jax
import jax.numpy as jnp
from jax import lax
from jax.experimental import pallas as pl
from jax.experimental.pallas import tpu as pltpu
from jax.sharding import PartitionSpec as P

D = 8192
H = 64
KV = 8
HD = 128
EPS = 1e-6
BF = jnp.bfloat16
F32 = jnp.float32
MESH = pl.DeviceIdType.MESH
VM = pltpu.VMEM
DMA = pltpu.SemaphoreType.DMA
SCORE_SCALE = 1.4426950408889634 / HD**0.5
LOWEST = -1e30
VMEM_LIMIT = 56 * 2**20


def remote(src, dst, send, recv, device):
    return pltpu.make_async_remote_copy(
        src_ref=src,
        dst_ref=dst,
        send_sem=send,
        recv_sem=recv,
        device_id=device,
        device_id_type=MESH,
    )


def tp_of(place, x):
    return ((place // 2) * 4 + x) * 2 + place % 2


class Spread:
    def __init__(self, source, buffer, sems, first, local=True):
        sp, tp = lax.axis_index("sp"), lax.axis_index("tp")
        high, x, core = tp // 8, (tp // 2) % 4, tp % 2
        self.sems = sems
        self.first = first
        self.buffer = buffer
        self.sibling = (sp, tp + 1 - 2 * core)
        opposite = (sp, (tp + 8) % 16)
        mine = buffer.at[high * 2 + core]
        self.local = pltpu.make_async_copy(source, mine, sems.at[first]) if local else None
        self.pair = remote(source, mine, sems.at[first + 1], sems.at[first + 2], self.sibling)
        self.over = remote(source, mine, sems.at[first + 3], sems.at[first + 4], opposite)
        across = buffer.at[(1 - high) * 2 + core]
        self.passed = remote(across, across, sems.at[first + 5], sems.at[first + 6], self.sibling)

    def keep(self):
        self.local.start()

    def send(self):
        self.over.start()
        self.pair.start()

    def forward(self):
        self.over.wait_recv()
        self.passed.start()

    def near(self):
        if self.local is not None:
            self.local.wait()
        self.pair.wait_recv()

    def finish(self):
        self.pair.wait_send()
        self.over.wait_send()
        self.passed.wait()


def gather_x(own, blocks, send_sem, recv_sem):
    sp, tp = lax.axis_index("sp"), lax.axis_index("tp")
    x, place = (tp // 2) % 4, (tp // 8) * 2 + tp % 2
    copies = [
        remote(own, blocks.at[x], send_sem.at[k], recv_sem.at[k], (sp, tp_of(place, (x + k) % 4)))
        for k in (1, 3, 2)
    ]
    for copy in copies:
        copy.start()
    blocks[x] = own[...]

    def settle():
        for copy in copies:
            copy.wait()

    return settle


def scatter_z(product, sent, got, cross_send, cross_recv, send_sem, recv_sem, cross_sem):
    sp, tp = lax.axis_index("sp"), lax.axis_index("tp")
    z, low = sp // 2, sp % 2
    neighbours = (((sp + 2) % 16, tp), ((sp + 14) % 16, tp))
    other = (sp + 1 - 2 * low, tp)

    def hop(way, step, r):
        index = way * 8 + step * 2 + r
        return remote(
            sent.at[way, step, r], got.at[way, step, r], send_sem.at[index], recv_sem.at[index], neighbours[way]
        )

    def split(place):
        part = product(place)
        return jnp.where(low == 0, part[32:], part[:32]), jnp.where(low == 0, part[:32], part[32:])

    far = split((z + 4) % 8)
    for way in range(2):
        sent[way, 0, way] = far[way].astype(BF)
        hop(way, 0, way).start()
    for step in range(1, 4):
        parts = [split((z + 4 - step) % 8), split((z + 4 + step) % 8)]
        for r in range(2):
            for way in range(2):
                piece = parts[way][r]
                if step > 1 or r == way:
                    hop(way, step - 1, r).wait_recv()
                    piece = piece + got[way, step - 1, r].astype(F32)
                sent[way, step, r] = piece.astype(BF)
                hop(way, step, r).start()
    away, mine = split(z)
    for way in range(2):
        hop(way, 3, 0).wait_recv()
        away = away + got[way, 3, 0].astype(F32)
    cross_send[...] = away.astype(BF)
    cross = remote(cross_send, cross_recv, cross_sem.at[0], cross_sem.at[1], other)
    cross.start()
    for way in range(2):
        hop(way, 3, 1).wait_recv()
        mine = mine + got[way, 3, 1].astype(F32)
    for way in range(2):
        hop(way, 0, way).wait_send()
        for step in range(1, 4):
            for r in range(2):
                hop(way, step, r).wait_send()
    cross.wait()
    return mine + cross_recv[...].astype(F32)


def gather_z(own, blocks, send_sem, recv_sem, cross_sem, beside):
    sp, tp = lax.axis_index("sp"), lax.axis_index("tp")
    z, low = sp // 2, sp % 2
    neighbours = (((sp + 2) % 16, tp), ((sp + 14) % 16, tp))
    other = (sp + 1 - 2 * low, tp)

    def hop(way, distance, place, r):
        block = blocks.at[place, low if r == 0 else 1 - low]
        index = way * 10 + distance * 2 + r
        return remote(block, block, send_sem.at[index], recv_sem.at[index], neighbours[way])

    blocks[z, low] = own[...]
    cross = remote(own, blocks.at[z, low], cross_sem.at[0], cross_sem.at[1], other)
    cross.start()
    for way in range(2):
        hop(way, 1, z, 0).start()
    remote(own, blocks.at[z, 1 - low], cross_sem.at[0], cross_sem.at[1], other).wait_recv()
    for way in range(2):
        hop(way, 1, z, 1).start()
    for distance in range(1, 4):
        for r in range(2):
            for way in range(2):
                place = (z + (8 - distance if way == 0 else distance)) % 8
                hop(way, distance, place, r).wait_recv()
                if distance < 3 or r == way:
                    hop(way, distance + 1, place, r).start()
        beside[distance]()
    for way in range(2):
        hop(way, 4, (z + 4) % 8, way).wait_recv()
    cross.wait_send()
    for way in range(2):
        for distance in range(1, 4):
            for r in range(2):
                hop(way, distance, z, r).wait_send()
        hop(way, 4, z, way).wait_send()


def block_kernel(
    offset_ref,
    queries_ref,
    keys_ref,
    values_ref,
    residual_ref,
    gain_ref,
    cache_k_ref,
    cache_v_ref,
    w_out_ref,
    w_gate_ref,
    w_up_ref,
    w_down_ref,
    out_ref,
    message,
    own_gain,
    received,
    keys,
    own_vals,
    vals_t,
    new_keys,
    new_vals_t,
    own_queries,
    queries,
    tops,
    totals,
    sums,
    out_send,
    out_recv,
    stat_send,
    stat_recv,
    own_attended,
    attended,
    w_out,
    w_gate,
    w_up,
    w_down,
    gains,
    residuals,
    stream,
    sent_a,
    got_a,
    sent_d,
    got_d,
    cross_a,
    cross_d,
    own_squares,
    squares,
    own_normed,
    normed,
    x_sent,
    x_got,
    own_hidden,
    hidden,
    own_out,
    a2a_send,
    a2a_recv,
    spread_sem,
    small_sem,
    q_send,
    q_recv,
    o_send,
    o_recv,
    st_send,
    st_recv,
    aa_send,
    aa_recv,
    za_send,
    za_recv,
    sq_send,
    sq_recv,
    zn_send,
    zn_recv,
    x_send,
    x_recv,
    ah_send,
    ah_recv,
    zd_send,
    zd_recv,
    cross_sem,
    back_sem,
):
    sp, tp = lax.axis_index("sp"), lax.axis_index("tp")
    high, x, core = tp // 8, (tp // 2) % 4, tp % 2
    place = high * 2 + core
    barrier = pltpu.get_barrier_semaphore()
    peers = [((sp + j) % 16, tp) for j in range(1, 16)] + [(sp, (tp + j) % 16) for j in range(1, 16)]
    for device in peers:
        pl.semaphore_signal(barrier, inc=1, device_id=device, device_id_type=MESH)
    columns = pl.ds(pl.multiple_of((sp // 2) * HD, HD), HD)
    spread_k = Spread(cache_k_ref.at[:, columns], keys, spread_sem, 0)
    spread_v = Spread(vals_t.at[place], vals_t, spread_sem, 7, local=False)
    spread_o = Spread(w_out_ref, w_out, spread_sem, 14)
    spread_g = Spread(w_gate_ref, w_gate, spread_sem, 21)
    spread_u = Spread(w_up_ref, w_up, spread_sem, 28)
    spread_d = Spread(w_down_ref, w_down, spread_sem, 35)
    load_v = pltpu.make_async_copy(cache_v_ref.at[:, columns], own_vals, small_sem.at[0])
    load_v.start()
    for spread in (spread_k, spread_o, spread_g, spread_u, spread_d):
        spread.keep()
    for target in range(16):
        lanes = target // 2 * HD
        rows = [
            queries_ref[:, target * 512 + h * HD : target * 512 + h * HD + HD].astype(F32) for h in range(4)
        ]
        rows.append(keys_ref[:, lanes : lanes + HD].astype(F32))
        rows.append(values_ref[:, lanes : lanes + HD].astype(F32))
        message[target] = jnp.concatenate(rows, 0).astype(BF)
    own_gain[...] = jnp.broadcast_to(gain_ref[...].astype(F32), (8, 512))
    load_v.wait()
    for piece in range(4):
        rows = own_vals[piece * 256 : piece * 256 + 256, :].astype(F32)
        vals_t[place, :, piece * 256 : piece * 256 + 256] = rows.T.astype(BF)
    pl.semaphore_wait(barrier, len(peers))

    def exchange(j, _):
        target = (sp + j) % 16
        remote(message.at[target], received.at[sp], a2a_send.at[j], a2a_recv.at[j], (target, tp)).start()
        return 0

    lax.fori_loop(1, 16, exchange, 0)
    spread_k.send()
    spread_v.send()
    received[sp] = message[sp]

    def arrived(j, _):
        block = received.at[(sp + 16 - j) % 16]
        remote(block, block, a2a_send.at[j], a2a_recv.at[j], (sp, tp)).wait()
        return 0

    lax.fori_loop(1, 16, arrived, 0)
    own_queries[...] = received[:, :32, :].reshape(4, 128, HD)
    queries[x, place] = own_queries[place]

    def ask(i, _):
        target = tp_of(i % 4, (x + i // 4) % 4)
        j = (target - tp + 16) % 16

        @pl.when(j > 0)
        def _():
            remote(own_queries.at[i % 4], queries.at[x, place], q_send.at[j], q_recv.at[j], (sp, target)).start()

        return 0

    lax.fori_loop(0, 16, ask, 0)
    spread_o.send()
    fresh = received[:, 32:, :].astype(F32).reshape(16, 2, 8, HD)
    new_keys[place] = fresh[:, 0].reshape(HD, HD).astype(BF)
    new_vals_t[place] = fresh[:, 1].reshape(HD, HD).T.astype(BF)

    def quad(i):
        peer = (place + i) % 4
        return (sp, tp_of(peer, x))

    def to_quad(i, kind, src, dst):
        index = 1 + kind * 6 + (i - 1) * 2
        return remote(src, dst, small_sem.at[index], small_sem.at[index + 1], quad(i))

    smalls = []
    for i in range(1, 4):
        peer = (place + i) % 4
        rows = pl.ds(pl.multiple_of(peer * 32, 32), 32)
        smalls.append(to_quad(i, 0, new_keys.at[place], new_keys.at[place]))
        smalls.append(to_quad(i, 1, new_vals_t.at[place], new_vals_t.at[place]))
        smalls.append(to_quad(i, 2, residual_ref.at[rows], residuals.at[place]))
        smalls.append(to_quad(i, 3, own_gain, gains.at[place]))
    for copy in smalls:
        copy.start()
    residuals[place] = residual_ref[pl.ds(pl.multiple_of(place * 32, 32), 32)]
    gains[place] = own_gain[...]
    spread_k.near()
    spread_v.near()

    def attend(k, turn):
        asker = (x + 4 - k) % 4
        if turn == 0:

            @pl.when(k == 2)
            def _():
                spread_k.forward()

            @pl.when(k == 3)
            def _():
                spread_v.forward()

            for source in range(4):
                j = (tp - tp_of(source, asker) + 16) % 16

                @pl.when(j > 0)
                def _():
                    block = queries.at[asker, source]
                    remote(block, block, q_send.at[j], q_recv.at[j], (sp, tp)).wait_recv()

        q = queries[asker].reshape(512, HD)
        if turn == 0:
            top = jnp.full((1, 512), LOWEST, F32)
            total = jnp.zeros((1, 512), F32)
            summed = jnp.zeros((HD, 512), F32)
        else:
            top = tops[k, 0:1, :]
            total = totals[k, 0:1, :]
            summed = sums[k]
        for chunk in range(4 + turn):
            if chunk < 4:
                held = (high + turn) % 2 * 2 + chunk // 2
                first = (chunk % 2) * 512
                block = keys[held, first : first + 512, :]
                block_t = vals_t[held, :, first : first + 512]
            else:
                block = new_keys[...].reshape(512, HD)
                block_t = jnp.concatenate([new_vals_t[i] for i in range(4)], 1)
            scores = lax.dot_general(block, q, (((1,), (1,)), ((), ())), preferred_element_type=F32)
            if chunk < 4:
                position = lax.broadcasted_iota(jnp.int32, (512, 512), 0)
                scores = jnp.where(position < offset_ref[0] - tp_of(held, x) * 1024 - first, scores, LOWEST)
            else:
                lane = lax.broadcasted_iota(jnp.int32, (128, 512), 1)
                token = ((lane // 256) * 4 + asker) * 256 + ((lane // 128) % 2) * 128
                token = token + place * 32 + ((lane // 32) % 4) * 8 + lane % 8
                ahead = lax.broadcasted_iota(jnp.int32, (128, 512), 0) - token
                scores = jnp.concatenate(
                    [
                        jnp.where(ahead <= -tp_of(i, x) * 128, scores[i * 128 : i * 128 + 128], LOWEST)
                        for i in range(4)
                    ],
                    0,
                )
            higher = jnp.maximum(top, jnp.max(scores, axis=0, keepdims=True))
            weights = jnp.exp2((scores - higher) * SCORE_SCALE)
            factor = jnp.exp2((top - higher) * SCORE_SCALE)
            total = total * factor + jnp.sum(weights, axis=0, keepdims=True)
            summed = summed * factor + jnp.dot(block_t, weights.astype(BF), preferred_element_type=F32)
            top = higher
        if turn == 0:
            tops[k] = jnp.broadcast_to(top, (8, 512))
            totals[k] = jnp.broadcast_to(total, (8, 512))
            sums[k] = summed
            return
        out_send[k] = summed.astype(BF)
        stat_send[k] = jnp.concatenate([jnp.broadcast_to(top, (4, 512)), jnp.broadcast_to(total, (4, 512))], 0)

        @pl.when(k > 0)
        def _():
            target = (sp, tp_of(place, asker))
            remote(out_send.at[k], out_recv.at[k], o_send.at[k], o_recv.at[k], target).start()
            remote(stat_send.at[k], stat_recv.at[k], st_send.at[k], st_recv.at[k], target).start()

    def attend_near(k, _):
        attend(k, 0)
        return 0

    def attend_far(k, _):
        attend((k + 1) % 4, 1)
        return 0

    lax.fori_loop(0, 4, attend_near, 0)
    spread_g.send()
    spread_k.finish()
    spread_v.finish()
    for copy in smalls:
        copy.wait()
    lax.fori_loop(0, 4, attend_far, 0)
    spread_o.forward()
    spread_u.send()

    def asked(j, _):
        remote(own_queries.at[0], queries.at[x, place], q_send.at[j], q_recv.at[j], (sp, tp)).wait_send()
        return 0

    lax.fori_loop(1, 16, asked, 0)

    def collect(k, _):
        remote(out_send.at[k], out_recv.at[k], o_send.at[k], o_recv.at[k], (sp, tp)).wait()
        remote(stat_send.at[k], stat_recv.at[k], st_send.at[k], st_recv.at[k], (sp, tp)).wait()
        return 0

    lax.fori_loop(1, 4, collect, 0)
    tops = [stat_send[0, 0:1, :]] + [stat_recv[k, 0:1, :] for k in range(1, 4)]
    highest = functools.reduce(jnp.maximum, tops)
    shares = [jnp.exp2((top - highest) * SCORE_SCALE) for top in tops]
    total = stat_send[0, 4:5, :] * shares[0]
    summed = out_send[0].astype(F32) * shares[0]
    for k in range(1, 4):
        total = total + stat_recv[k, 4:5, :] * shares[k]
        summed = summed + out_recv[k].astype(F32) * shares[k]
    mixed = (summed / total).T.reshape(16, 4, 8, HD)
    for h in range(4):
        own_attended[:, :, h * HD : (h + 1) * HD] = mixed[:, h].reshape(2, 64, HD).astype(BF)
    gather_x(own_attended, attended, aa_send, aa_recv)()
    spread_d.send()
    spread_o.near()
    spread_o.finish()

    def project(z):
        rows = attended[z % 4, z // 4]
        return jnp.concatenate(
            [jnp.dot(rows, w_out[i], preferred_element_type=F32) for i in range(4)], 1
        )

    attn_out = scatter_z(
        project, sent_a, got_a, cross_a.at[0], cross_a.at[1], za_send, za_recv, cross_sem.at[pl.ds(0, 2)]
    )
    spread_g.forward()
    own_residual = jnp.concatenate([residuals[i] for i in range(4)], 1)
    stream[...] = (own_residual.astype(F32) + attn_out).astype(BF)
    wide = stream[...].astype(F32)
    own_squares[...] = jnp.broadcast_to(jnp.sum(wide * wide, axis=1, keepdims=True), (32, 128))
    tells = [
        remote(own_squares, squares.at[k], sq_send.at[k], sq_recv.at[k], (sp, tp_of(place, (x + k) % 4)))
        for k in range(1, 4)
    ]
    for copy in tells:
        copy.start()
    for copy in tells:
        copy.wait()
    mean = (own_squares[...] + squares[1] + squares[2] + squares[3]) / D
    scale = jnp.concatenate([lax.rsqrt(mean + EPS)] * 16, 1)
    gain = jnp.concatenate([gains[i, 0:1, :] for i in range(4)], 1)
    own_normed[...] = (stream[...].astype(F32) * scale * gain).astype(BF)
    spread_u.forward()
    for spread in (spread_g, spread_u):
        spread.near()
        spread.finish()
    z = sp // 2

    def part(turn, column, up):
        rows = normed[(z + 7 + (x + column) % 4 + 4 * turn) % 8].reshape(64, 2048)
        weight = w_up if up else w_gate
        return jnp.dot(rows, weight[...].reshape(2048, 1024), preferred_element_type=F32)

    neighbours = ((sp, tp_of(place, (x + 1) % 4)), (sp, tp_of(place, (x + 3) % 4)))

    def hop(turn, which):
        index = turn * 6 + which
        return remote(
            x_sent.at[index], x_got.at[index], x_send.at[index], x_recv.at[index], neighbours[which // 3]
        )

    def post(turn, which, value):
        x_sent[turn * 6 + which] = value.astype(BF)
        hop(turn, which).start()

    def came(turn, which):
        hop(turn, which).wait_recv()
        return x_got[turn * 6 + which].astype(F32)

    def open_turn(turn):
        post(turn, 0, part(turn, 2, False))
        post(turn, 3, part(turn, 2, True))
        post(turn, 2, part(turn, 1, True))
        post(turn, 5, part(turn, 3, False))

    def pass_turn(turn):
        second = part(turn, 1, False)
        post(turn, 1, second + came(turn, 0))
        second = part(turn, 3, True)
        post(turn, 4, second + came(turn, 3))

    def close_turn(turn):
        gate = part(turn, 0, False)
        up = part(turn, 0, True)
        gate = gate + came(turn, 5) + came(turn, 1)
        up = up + came(turn, 2) + came(turn, 4)
        own_hidden[turn] = (gate / (1.0 + jnp.exp(-gate)) * up).astype(BF)
        return gather_x(
            own_hidden.at[turn], hidden.at[turn], ah_send.at[pl.ds(4 * turn, 4)], ah_recv.at[pl.ds(4 * turn, 4)]
        )

    gather_z(
        own_normed,
        normed,
        zn_send,
        zn_recv,
        cross_sem.at[pl.ds(2, 2)],
        {1: lambda: None, 2: lambda: open_turn(0), 3: lambda: pass_turn(0)},
    )
    open_turn(1)
    first_half = close_turn(0)
    pass_turn(1)
    spread_d.forward()
    second_half = close_turn(1)
    first_half()
    second_half()
    spread_d.near()
    spread_d.finish()
    for turn in range(2):
        for which in range(6):
            hop(turn, which).wait_send()

    def down(target):
        offset = (target + 9 - z) % 8
        rows = hidden[offset // 4, offset % 4]
        return jnp.concatenate(
            [jnp.dot(rows, w_down[i], preferred_element_type=F32) for i in range(4)], 1
        )

    added = scatter_z(
        down, sent_d, got_d, cross_d.at[0], cross_d.at[1], zd_send, zd_recv, cross_sem.at[pl.ds(4, 2)]
    )
    result = (stream[...].astype(F32) + added).astype(BF)
    for i in range(4):
        own_out[i] = result[:, i * 512 : i * 512 + 512]
    mine = pl.ds(pl.multiple_of(place * 32, 32), 32)
    backs = [
        remote(own_out.at[(place + i) % 4], out_ref.at[mine], back_sem.at[2 * i], back_sem.at[2 * i + 1], quad(i))
        for i in range(1, 4)
    ]
    for copy in backs:
        copy.start()
    out_ref[mine] = own_out[place]
    for copy in backs:
        copy.wait()


def run_block(offset, queries, keys, values, residual, gain, cache_keys, cache_values, w_out, w_gate, w_up, w_down):
    hop = VM((2, 4, 2, 32, 2048), BF)
    vmem = pl.BlockSpec(memory_space=pltpu.VMEM)
    return pl.pallas_call(
        block_kernel,
        out_shape=jax.ShapeDtypeStruct((128, 512), BF),
        in_specs=[pl.BlockSpec(memory_space=pltpu.SMEM)] + [vmem] * 5 + [pl.BlockSpec(memory_space=pl.ANY)] * 6,
        out_specs=vmem,
        scratch_shapes=[
            VM((16, 48, HD), BF),
            VM((8, 512), F32),
            VM((16, 48, HD), BF),
            VM((4, 1024, HD), BF),
            VM((1024, HD), BF),
            VM((4, HD, 1024), BF),
            VM((4, 128, HD), BF),
            VM((4, HD, 128), BF),
            VM((4, 128, HD), BF),
            VM((4, 4, 128, HD), BF),
            VM((4, 8, 512), F32),
            VM((4, 8, 512), F32),
            VM((4, HD, 512), F32),
            VM((4, HD, 512), BF),
            VM((4, HD, 512), BF),
            VM((4, 8, 512), F32),
            VM((4, 8, 512), F32),
            VM((2, 64, 512), BF),
            VM((4, 2, 64, 512), BF),
            VM((4, 512, 512), BF),
            VM((4, 512, 1024), BF),
            VM((4, 512, 1024), BF),
            VM((4, 1024, 512), BF),
            VM((4, 8, 512), F32),
            VM((4, 32, 512), BF),
            VM((32, 2048), BF),
            hop,
            hop,
            hop,
            hop,
            VM((2, 32, 2048), BF),
            VM((2, 32, 2048), BF),
            VM((32, 128), F32),
            VM((4, 32, 128), F32),
            VM((32, 2048), BF),
            VM((8, 2, 32, 2048), BF),
            VM((12, 64, 1024), BF),
            VM((12, 64, 1024), BF),
            VM((2, 64, 1024), BF),
            VM((2, 4, 64, 1024), BF),
            VM((4, 32, 512), BF),
        ]
        + [DMA((16,))] * 2
        + [DMA((42,)), DMA((25,))]
        + [DMA((16,))] * 2
        + [DMA((4,))] * 6
        + [DMA((16,))] * 2
        + [DMA((4,))] * 2
        + [DMA((20,))] * 2
        + [DMA((12,))] * 2
        + [DMA((8,))] * 2
        + [DMA((16,))] * 2
        + [DMA((6,)), DMA((8,))],
        compiler_params=pltpu.CompilerParams(
            collective_id=0, has_side_effects=True, vmem_limit_bytes=VMEM_LIMIT
        ),
        name="block",
    )(offset, queries, keys, values, residual, gain, cache_keys, cache_values, w_out, w_gate, w_up, w_down)


def per_device(
    residual,
    queries,
    keys,
    values,
    cache_keys,
    cache_values,
    offset,
    w_out,
    norm_gain,
    w_gate,
    w_up,
    w_down,
):
    return run_block(
        offset,
        queries,
        keys,
        values,
        residual,
        norm_gain.reshape(1, 512),
        cache_keys,
        cache_values,
        w_out,
        w_gate,
        w_up,
        w_down,
    )


def solution(mesh):
    in_specs = (
        P("sp", "tp"),
        P(("tp", "sp"), None),
        P(("tp", "sp"), None),
        P(("tp", "sp"), None),
        P("tp", None),
        P("tp", None),
        P(),
        P("sp", "tp"),
        P("tp"),
        P("tp", "sp"),
        P("tp", "sp"),
        P("sp", "tp"),
    )
    out_specs = P("sp", "tp")
    return jax.shard_map(
        per_device, mesh=mesh, in_specs=in_specs, out_specs=out_specs, check_vma=False
    )
```

```python
import functools

import jax
import jax.numpy as jnp
from jax import lax
from jax.experimental import pallas as pl
from jax.experimental.pallas import tpu as pltpu
from jax.sharding import PartitionSpec as P

D = 8192
H = 64
KV = 8
HD = 128
EPS = 1e-6
BF = jnp.bfloat16
F32 = jnp.float32
MESH = pl.DeviceIdType.MESH
VM = pltpu.VMEM
DMA = pltpu.SemaphoreType.DMA
SCORE_SCALE = 1.4426950408889634 / HD**0.5
LOWEST = -1e30
VMEM_LIMIT = 56 * 2**20


def remote(src, dst, send, recv, device):
    return pltpu.make_async_remote_copy(
        src_ref=src,
        dst_ref=dst,
        send_sem=send,
        recv_sem=recv,
        device_id=device,
        device_id_type=MESH,
    )


def tp_of(place, x):
    return ((place // 2) * 4 + x) * 2 + place % 2


class Spread:
    def __init__(self, source, buffer, sems, first, local=True, rows=None):
        sp, tp = lax.axis_index("sp"), lax.axis_index("tp")
        high, x, core = tp // 8, (tp // 2) % 4, tp % 2
        self.sibling = (sp, tp + 1 - 2 * core)
        opposite = (sp, (tp + 8) % 16)
        at = (lambda i: buffer.at[i]) if rows is None else (lambda i: buffer.at[i, rows])
        mine = at(high * 2 + core)
        self.local = pltpu.make_async_copy(source, mine, sems.at[first]) if local else None
        self.pair = remote(source, mine, sems.at[first + 1], sems.at[first + 2], self.sibling)
        self.over = remote(source, mine, sems.at[first + 3], sems.at[first + 4], opposite)
        across = at((1 - high) * 2 + core)
        self.passed = remote(across, across, sems.at[first + 5], sems.at[first + 6], self.sibling)

    def keep(self):
        self.local.start()

    def send(self):
        self.over.start()
        self.pair.start()

    def forward(self):
        self.over.wait_recv()
        self.passed.start()

    def near(self):
        if self.local is not None:
            self.local.wait()
        self.pair.wait_recv()

    def finish(self):
        self.pair.wait_send()
        self.over.wait_send()
        self.passed.wait()


def gather_x(own, blocks, send_sem, recv_sem):
    sp, tp = lax.axis_index("sp"), lax.axis_index("tp")
    x, place = (tp // 2) % 4, (tp // 8) * 2 + tp % 2
    copies = [
        remote(own, blocks.at[x], send_sem.at[k], recv_sem.at[k], (sp, tp_of(place, (x + k) % 4)))
        for k in (1, 3, 2)
    ]
    for copy in copies:
        copy.start()
    blocks[x] = own[...]

    def settle():
        for copy in copies:
            copy.wait()

    return settle


def scatter_z(product, sent, got, cross_send, cross_recv, send_sem, recv_sem, cross_sem, beside=None):
    sp, tp = lax.axis_index("sp"), lax.axis_index("tp")
    z, low = sp // 2, sp % 2
    neighbours = (((sp + 2) % 16, tp), ((sp + 14) % 16, tp))
    other = (sp + 1 - 2 * low, tp)

    def hop(way, step, r):
        index = way * 8 + step * 2 + r
        return remote(
            sent.at[way, step, r], got.at[way, step, r], send_sem.at[index], recv_sem.at[index], neighbours[way]
        )

    def split(place):
        part = product(place)
        return jnp.where(low == 0, part[32:], part[:32]), jnp.where(low == 0, part[:32], part[32:])

    far = split((z + 4) % 8)
    for way in range(2):
        sent[way, 0, way] = far[way].astype(BF)
        hop(way, 0, way).start()
    for step in range(1, 4):
        parts = [split((z + 4 - step) % 8), split((z + 4 + step) % 8)]
        for r in range(2):
            for way in range(2):
                piece = parts[way][r]
                if step > 1 or r == way:
                    hop(way, step - 1, r).wait_recv()
                    piece = piece + got[way, step - 1, r].astype(F32)
                sent[way, step, r] = piece.astype(BF)
                hop(way, step, r).start()
    away, mine = split(z)
    for way in range(2):
        hop(way, 3, 0).wait_recv()
        away = away + got[way, 3, 0].astype(F32)
    cross_send[...] = away.astype(BF)
    cross = remote(cross_send, cross_recv, cross_sem.at[0], cross_sem.at[1], other)
    cross.start()
    if beside is not None:
        beside()
    for way in range(2):
        hop(way, 3, 1).wait_recv()
        mine = mine + got[way, 3, 1].astype(F32)
    for way in range(2):
        hop(way, 0, way).wait_send()
        for step in range(1, 4):
            for r in range(2):
                hop(way, step, r).wait_send()
    cross.wait()
    return mine + cross_recv[...].astype(F32)


def gather_z(own, blocks, send_sem, recv_sem, cross_sem, beside):
    sp, tp = lax.axis_index("sp"), lax.axis_index("tp")
    z, low = sp // 2, sp % 2
    neighbours = (((sp + 2) % 16, tp), ((sp + 14) % 16, tp))
    other = (sp + 1 - 2 * low, tp)

    def hop(way, distance, place, r):
        block = blocks.at[place, low if r == 0 else 1 - low]
        index = way * 10 + distance * 2 + r
        return remote(block, block, send_sem.at[index], recv_sem.at[index], neighbours[way])

    blocks[z, low] = own[...]
    cross = remote(own, blocks.at[z, low], cross_sem.at[0], cross_sem.at[1], other)
    cross.start()
    for way in range(2):
        hop(way, 1, z, 0).start()
    beside[0]()
    remote(own, blocks.at[z, 1 - low], cross_sem.at[0], cross_sem.at[1], other).wait_recv()
    for way in range(2):
        hop(way, 1, z, 1).start()
    for distance in range(1, 4):
        for r in range(2):
            for way in range(2):
                place = (z + (8 - distance if way == 0 else distance)) % 8
                hop(way, distance, place, r).wait_recv()
                if distance < 3 or r == way:
                    hop(way, distance + 1, place, r).start()
        beside[distance]()
    for way in range(2):
        hop(way, 4, (z + 4) % 8, way).wait_recv()
    cross.wait_send()
    for way in range(2):
        for distance in range(1, 4):
            for r in range(2):
                hop(way, distance, z, r).wait_send()
        hop(way, 4, z, way).wait_send()


def block_kernel(
    offset_ref,
    queries_ref,
    keys_ref,
    values_ref,
    residual_ref,
    gain_ref,
    cache_k_ref,
    cache_v_ref,
    w_out_ref,
    w_gate_ref,
    w_up_ref,
    w_down_ref,
    out_ref,
    message,
    own_gain,
    received,
    keys,
    own_vals,
    vals_t,
    new_keys,
    new_vals_t,
    own_queries,
    queries,
    tops,
    totals,
    sums,
    out_send,
    out_recv,
    stat_send,
    stat_recv,
    own_attended,
    attended,
    w_out,
    w_gate,
    w_up,
    w_down,
    gains,
    residuals,
    stream,
    sent_a,
    got_a,
    sent_d,
    got_d,
    cross_a,
    cross_d,
    own_squares,
    squares,
    own_normed,
    normed,
    x_sent,
    x_got,
    own_hidden,
    hidden,
    own_out,
    a2a_send,
    a2a_recv,
    spread_sem,
    small_sem,
    q_send,
    q_recv,
    o_send,
    o_recv,
    st_send,
    st_recv,
    aa_send,
    aa_recv,
    za_send,
    za_recv,
    sq_send,
    sq_recv,
    zn_send,
    zn_recv,
    x_send,
    x_recv,
    ah_send,
    ah_recv,
    zd_send,
    zd_recv,
    cross_sem,
    back_sem,
):
    sp, tp = lax.axis_index("sp"), lax.axis_index("tp")
    high, x, core = tp // 8, (tp // 2) % 4, tp % 2
    place = high * 2 + core
    barrier = pltpu.get_barrier_semaphore()
    peers = [((sp + j) % 16, tp) for j in range(1, 16)] + [(sp, (tp + j) % 16) for j in range(1, 16)]
    for device in peers:
        pl.semaphore_signal(barrier, inc=1, device_id=device, device_id_type=MESH)
    columns = pl.ds(pl.multiple_of((sp // 2) * HD, HD), HD)
    spread_k = Spread(cache_k_ref.at[:, columns], keys, spread_sem, 0)
    spread_v = Spread(vals_t.at[place], vals_t, spread_sem, 7, local=False)
    spread_o = Spread(w_out_ref, w_out, spread_sem, 14)
    spread_g = Spread(w_gate_ref, w_gate, spread_sem, 21)
    spread_u = [
        Spread(w_up_ref.at[first : first + count], w_up, spread_sem, index, rows=pl.ds(first, count))
        for first, count, index in ((0, 256, 28), (256, 128, 35), (384, 128, 42))
    ]
    spread_d = Spread(w_down_ref, w_down, spread_sem, 49)
    load_v = pltpu.make_async_copy(cache_v_ref.at[:, columns], own_vals, small_sem.at[0])
    load_v.start()
    for spread in (spread_k, spread_o, spread_g, *spread_u, spread_d):
        spread.keep()
    for target in range(16):
        lanes = target // 2 * HD
        rows = [
            queries_ref[:, target * 512 + h * HD : target * 512 + h * HD + HD].astype(F32) for h in range(4)
        ]
        rows.append(keys_ref[:, lanes : lanes + HD].astype(F32))
        rows.append(values_ref[:, lanes : lanes + HD].astype(F32))
        message[target] = jnp.concatenate(rows, 0).astype(BF)
    own_gain[...] = jnp.broadcast_to(gain_ref[...].astype(F32).reshape(1, 512), (8, 512))
    load_v.wait()
    for piece in range(4):
        rows = own_vals[piece * 256 : piece * 256 + 256, :].astype(F32)
        vals_t[place, :, piece * 256 : piece * 256 + 256] = rows.T.astype(BF)
    pl.semaphore_wait(barrier, len(peers))

    def exchange(j, _):
        target = (sp + j) % 16
        remote(message.at[target], received.at[sp], a2a_send.at[j], a2a_recv.at[j], (target, tp)).start()
        return 0

    lax.fori_loop(1, 16, exchange, 0)
    spread_k.send()
    spread_v.pair.start()
    received[sp] = message[sp]

    def arrived(j, _):
        block = received.at[(sp + 16 - j) % 16]
        remote(block, block, a2a_send.at[j], a2a_recv.at[j], (sp, tp)).wait()
        return 0

    lax.fori_loop(1, 16, arrived, 0)
    own_queries[...] = received[:, :32, :].reshape(4, 128, HD)
    queries[x, place] = own_queries[place]

    def ask(i, _):
        target = tp_of(i % 4, (x + i // 4) % 4)
        j = (target - tp + 16) % 16

        @pl.when(j > 0)
        def _():
            remote(own_queries.at[i % 4], queries.at[x, place], q_send.at[j], q_recv.at[j], (sp, target)).start()

        return 0

    lax.fori_loop(0, 16, ask, 0)
    spread_v.over.start()
    fresh = received[:, 32:, :].astype(F32).reshape(16, 2, 8, HD)
    new_keys[place] = fresh[:, 0].reshape(HD, HD).astype(BF)
    new_vals_t[place] = fresh[:, 1].reshape(HD, HD).T.astype(BF)

    def quad(i):
        peer = (place + i) % 4
        return (sp, tp_of(peer, x))

    def to_quad(i, kind, src, dst):
        index = 1 + kind * 6 + (i - 1) * 2
        return remote(src, dst, small_sem.at[index], small_sem.at[index + 1], quad(i))

    smalls = []
    for i in range(1, 4):
        peer = (place + i) % 4
        rows = pl.ds(pl.multiple_of(peer * 32, 32), 32)
        smalls.append(to_quad(i, 0, new_keys.at[place], new_keys.at[place]))
        smalls.append(to_quad(i, 1, new_vals_t.at[place], new_vals_t.at[place]))
        smalls.append(to_quad(i, 2, residual_ref.at[rows], residuals.at[place]))
        smalls.append(to_quad(i, 3, own_gain, gains.at[place]))
    for copy in smalls:
        copy.start()
    residuals[place] = residual_ref[pl.ds(pl.multiple_of(place * 32, 32), 32)]
    gains[place] = own_gain[...]
    spread_o.send()
    spread_k.near()
    spread_v.near()

    def attend(k, turn):
        asker = (x + 4 - k) % 4
        if turn == 0:

            @pl.when(k == 2)
            def _():
                spread_k.forward()

            for source in range(4):
                j = (tp - tp_of(source, asker) + 16) % 16

                @pl.when(j > 0)
                def _():
                    block = queries.at[asker, source]
                    remote(block, block, q_send.at[j], q_recv.at[j], (sp, tp)).wait_recv()

        q = queries[asker].reshape(512, HD)
        if turn == 0:
            top = jnp.full((1, 512), LOWEST, F32)
            total = jnp.zeros((1, 512), F32)
            summed = jnp.zeros((HD, 512), F32)
        else:
            top = tops[k, 0:1, :]
            total = totals[k, 0:1, :]
            summed = sums[k]
        for chunk in range(4 + turn):
            if chunk < 4:
                held = (high + turn) % 2 * 2 + chunk // 2
                first = (chunk % 2) * 512
                block = keys[held, first : first + 512, :]
                block_t = vals_t[held, :, first : first + 512]
            else:
                block = new_keys[...].reshape(512, HD)
                block_t = jnp.concatenate([new_vals_t[i] for i in range(4)], 1)
            scores = lax.dot_general(block, q, (((1,), (1,)), ((), ())), preferred_element_type=F32)
            if chunk < 4:
                position = lax.broadcasted_iota(jnp.int32, (512, 512), 0)
                scores = jnp.where(position < offset_ref[0] - tp_of(held, x) * 1024 - first, scores, LOWEST)
            else:
                lane = lax.broadcasted_iota(jnp.int32, (128, 512), 1)
                token = ((lane // 256) * 4 + asker) * 256 + ((lane // 128) % 2) * 128
                token = token + place * 32 + ((lane // 32) % 4) * 8 + lane % 8
                ahead = lax.broadcasted_iota(jnp.int32, (128, 512), 0) - token
                scores = jnp.concatenate(
                    [
                        jnp.where(ahead <= -tp_of(i, x) * 128, scores[i * 128 : i * 128 + 128], LOWEST)
                        for i in range(4)
                    ],
                    0,
                )
            higher = jnp.maximum(top, jnp.max(scores, axis=0, keepdims=True))
            weights = jnp.exp2((scores - higher) * SCORE_SCALE)
            factor = jnp.exp2((top - higher) * SCORE_SCALE)
            total = total * factor + jnp.sum(weights, axis=0, keepdims=True)
            summed = summed * factor + jnp.dot(block_t, weights.astype(BF), preferred_element_type=F32)
            top = higher
        if turn == 0:
            tops[k] = jnp.broadcast_to(top, (8, 512))
            totals[k] = jnp.broadcast_to(total, (8, 512))
            sums[k] = summed
            return
        out_send[k] = summed.astype(BF)
        stat_send[k] = jnp.concatenate([jnp.broadcast_to(top, (4, 512)), jnp.broadcast_to(total, (4, 512))], 0)

        @pl.when(k > 0)
        def _():
            target = (sp, tp_of(place, asker))
            remote(out_send.at[k], out_recv.at[k], o_send.at[k], o_recv.at[k], target).start()
            remote(stat_send.at[k], stat_recv.at[k], st_send.at[k], st_recv.at[k], target).start()

    def attend_near(k, _):
        attend(k, 0)
        return 0

    def attend_far(k, _):
        attend((k + 1) % 4, 1)
        return 0

    lax.fori_loop(0, 4, attend_near, 0)
    spread_v.forward()
    spread_g.send()
    spread_k.finish()
    spread_v.finish()
    for copy in smalls:
        copy.wait()
    lax.fori_loop(0, 4, attend_far, 0)
    spread_o.forward()
    spread_u[0].send()

    def asked(j, _):
        remote(own_queries.at[0], queries.at[x, place], q_send.at[j], q_recv.at[j], (sp, tp)).wait_send()
        return 0

    lax.fori_loop(1, 16, asked, 0)

    def collect(k, _):
        remote(out_send.at[k], out_recv.at[k], o_send.at[k], o_recv.at[k], (sp, tp)).wait()
        remote(stat_send.at[k], stat_recv.at[k], st_send.at[k], st_recv.at[k], (sp, tp)).wait()
        return 0

    lax.fori_loop(1, 4, collect, 0)
    tops = [stat_send[0, 0:1, :]] + [stat_recv[k, 0:1, :] for k in range(1, 4)]
    highest = functools.reduce(jnp.maximum, tops)
    shares = [jnp.exp2((top - highest) * SCORE_SCALE) for top in tops]
    total = stat_send[0, 4:5, :] * shares[0]
    summed = out_send[0].astype(F32) * shares[0]
    for k in range(1, 4):
        total = total + stat_recv[k, 4:5, :] * shares[k]
        summed = summed + out_recv[k].astype(F32) * shares[k]
    mixed = (summed / total).T.reshape(16, 4, 8, HD)
    for h in range(4):
        own_attended[:, :, h * HD : (h + 1) * HD] = mixed[:, h].reshape(2, 64, HD).astype(BF)
    gather_x(own_attended, attended, aa_send, aa_recv)()
    spread_o.near()
    spread_o.finish()

    def project(z):
        rows = attended[z % 4, z // 4]
        return jnp.concatenate(
            [jnp.dot(rows, w_out[i], preferred_element_type=F32) for i in range(4)], 1
        )

    attn_out = scatter_z(
        project,
        sent_a,
        got_a,
        cross_a.at[0],
        cross_a.at[1],
        za_send,
        za_recv,
        cross_sem.at[pl.ds(0, 2)],
        spread_u[1].send,
    )
    spread_g.forward()
    spread_u[0].forward()
    own_residual = jnp.concatenate([residuals[i] for i in range(4)], 1)
    stream[...] = (own_residual.astype(F32) + attn_out).astype(BF)
    wide = stream[...].astype(F32)
    own_squares[...] = jnp.broadcast_to(jnp.sum(wide * wide, axis=1, keepdims=True), (32, 128))
    tells = [
        remote(own_squares, squares.at[k], sq_send.at[k], sq_recv.at[k], (sp, tp_of(place, (x + k) % 4)))
        for k in range(1, 4)
    ]
    for copy in tells:
        copy.start()
    for copy in tells:
        copy.wait()
    mean = (own_squares[...] + squares[1] + squares[2] + squares[3]) / D
    scale = jnp.concatenate([lax.rsqrt(mean + EPS)] * 16, 1)
    gain = jnp.concatenate([gains[i, 0:1, :] for i in range(4)], 1)
    own_normed[...] = (stream[...].astype(F32) * scale * gain).astype(BF)
    z = sp // 2

    def send_rest():
        spread_u[2].send()
        spread_d.send()

    def have_weights():
        spread_u[2].forward()
        for spread in (spread_g, *spread_u):
            spread.near()
            spread.finish()
        open_turn(0)

    def part(turn, column, up):
        rows = normed[(z + 7 + (x + column) % 4 + 4 * turn) % 8].reshape(64, 2048)
        weight = w_up if up else w_gate
        return jnp.dot(rows, weight[...].reshape(2048, 1024), preferred_element_type=F32)

    neighbours = ((sp, tp_of(place, (x + 1) % 4)), (sp, tp_of(place, (x + 3) % 4)))

    def hop(turn, which):
        index = turn * 6 + which
        return remote(
            x_sent.at[index], x_got.at[index], x_send.at[index], x_recv.at[index], neighbours[which // 3]
        )

    def post(turn, which, value):
        x_sent[turn * 6 + which] = value.astype(BF)
        hop(turn, which).start()

    def came(turn, which):
        hop(turn, which).wait_recv()
        return x_got[turn * 6 + which].astype(F32)

    def open_turn(turn):
        post(turn, 0, part(turn, 2, False))
        post(turn, 3, part(turn, 2, True))
        post(turn, 2, part(turn, 1, True))
        post(turn, 5, part(turn, 3, False))

    def pass_turn(turn):
        second = part(turn, 1, False)
        post(turn, 1, second + came(turn, 0))
        second = part(turn, 3, True)
        post(turn, 4, second + came(turn, 3))

    def close_turn(turn):
        gate = part(turn, 0, False)
        up = part(turn, 0, True)
        gate = gate + came(turn, 5) + came(turn, 1)
        up = up + came(turn, 2) + came(turn, 4)
        own_hidden[turn] = (gate / (1.0 + jnp.exp(-gate)) * up).astype(BF)
        return gather_x(
            own_hidden.at[turn], hidden.at[turn], ah_send.at[pl.ds(4 * turn, 4)], ah_recv.at[pl.ds(4 * turn, 4)]
        )

    gather_z(
        own_normed,
        normed,
        zn_send,
        zn_recv,
        cross_sem.at[pl.ds(2, 2)],
        {0: send_rest, 1: spread_u[1].forward, 2: have_weights, 3: lambda: pass_turn(0)},
    )
    open_turn(1)
    first_half = close_turn(0)
    pass_turn(1)
    second_half = close_turn(1)
    spread_d.forward()
    first_half()
    second_half()
    spread_d.near()
    spread_d.finish()
    for turn in range(2):
        for which in range(6):
            hop(turn, which).wait_send()

    def down(target):
        offset = (target + 9 - z) % 8
        rows = hidden[offset // 4, offset % 4]
        return jnp.concatenate(
            [jnp.dot(rows, w_down[i], preferred_element_type=F32) for i in range(4)], 1
        )

    added = scatter_z(
        down, sent_d, got_d, cross_d.at[0], cross_d.at[1], zd_send, zd_recv, cross_sem.at[pl.ds(4, 2)]
    )
    result = (stream[...].astype(F32) + added).astype(BF)
    for i in range(4):
        own_out[i] = result[:, i * 512 : i * 512 + 512]
    mine = pl.ds(pl.multiple_of(place * 32, 32), 32)
    backs = [
        remote(own_out.at[(place + i) % 4], out_ref.at[mine], back_sem.at[2 * i], back_sem.at[2 * i + 1], quad(i))
        for i in range(1, 4)
    ]
    for copy in backs:
        copy.start()
    out_ref[mine] = own_out[place]
    for copy in backs:
        copy.wait()


def run_block(offset, queries, keys, values, residual, gain, cache_keys, cache_values, w_out, w_gate, w_up, w_down):
    hop = VM((2, 4, 2, 32, 2048), BF)
    vmem = pl.BlockSpec(memory_space=pltpu.VMEM)
    return pl.pallas_call(
        block_kernel,
        out_shape=jax.ShapeDtypeStruct((128, 512), BF),
        in_specs=[pl.BlockSpec(memory_space=pltpu.SMEM)] + [vmem] * 5 + [pl.BlockSpec(memory_space=pl.ANY)] * 6,
        out_specs=vmem,
        scratch_shapes=[
            VM((16, 48, HD), BF),
            VM((8, 512), F32),
            VM((16, 48, HD), BF),
            VM((4, 1024, HD), BF),
            VM((1024, HD), BF),
            VM((4, HD, 1024), BF),
            VM((4, 128, HD), BF),
            VM((4, HD, 128), BF),
            VM((4, 128, HD), BF),
            VM((4, 4, 128, HD), BF),
            VM((4, 8, 512), F32),
            VM((4, 8, 512), F32),
            VM((4, HD, 512), F32),
            VM((4, HD, 512), BF),
            VM((4, HD, 512), BF),
            VM((4, 8, 512), F32),
            VM((4, 8, 512), F32),
            VM((2, 64, 512), BF),
            VM((4, 2, 64, 512), BF),
            VM((4, 512, 512), BF),
            VM((4, 512, 1024), BF),
            VM((4, 512, 1024), BF),
            VM((4, 1024, 512), BF),
            VM((4, 8, 512), F32),
            VM((4, 32, 512), BF),
            VM((32, 2048), BF),
            hop,
            hop,
            hop,
            hop,
            VM((2, 32, 2048), BF),
            VM((2, 32, 2048), BF),
            VM((32, 128), F32),
            VM((4, 32, 128), F32),
            VM((32, 2048), BF),
            VM((8, 2, 32, 2048), BF),
            VM((12, 64, 1024), BF),
            VM((12, 64, 1024), BF),
            VM((2, 64, 1024), BF),
            VM((2, 4, 64, 1024), BF),
            VM((4, 32, 512), BF),
        ]
        + [DMA((16,))] * 2
        + [DMA((56,)), DMA((25,))]
        + [DMA((16,))] * 2
        + [DMA((4,))] * 6
        + [DMA((16,))] * 2
        + [DMA((4,))] * 2
        + [DMA((20,))] * 2
        + [DMA((12,))] * 2
        + [DMA((8,))] * 2
        + [DMA((16,))] * 2
        + [DMA((6,)), DMA((8,))],
        compiler_params=pltpu.CompilerParams(
            collective_id=0, has_side_effects=True, vmem_limit_bytes=VMEM_LIMIT
        ),
        name="block",
    )(offset, queries, keys, values, residual, gain, cache_keys, cache_values, w_out, w_gate, w_up, w_down)


def per_device(
    residual,
    queries,
    keys,
    values,
    cache_keys,
    cache_values,
    offset,
    w_out,
    norm_gain,
    w_gate,
    w_up,
    w_down,
):
    return run_block(
        offset,
        queries,
        keys,
        values,
        residual,
        norm_gain,
        cache_keys,
        cache_values,
        w_out,
        w_gate,
        w_up,
        w_down,
    )


def solution(mesh):
    in_specs = (
        P("sp", "tp"),
        P(("tp", "sp"), None),
        P(("tp", "sp"), None),
        P(("tp", "sp"), None),
        P("tp", None),
        P("tp", None),
        P(),
        P("sp", "tp"),
        P("tp"),
        P("tp", "sp"),
        P("tp", "sp"),
        P("sp", "tp"),
    )
    out_specs = P("sp", "tp")
    return jax.shard_map(
        per_device, mesh=mesh, in_specs=in_specs, out_specs=out_specs, check_vma=False
    )
```

```python
import functools

import jax
import jax.numpy as jnp
from jax import lax
from jax.experimental import pallas as pl
from jax.experimental.pallas import tpu as pltpu
from jax.sharding import PartitionSpec as P

D = 8192
H = 64
KV = 8
HD = 128
EPS = 1e-6
BF = jnp.bfloat16
F32 = jnp.float32
MESH = pl.DeviceIdType.MESH
VM = pltpu.VMEM
DMA = pltpu.SemaphoreType.DMA
SCORE_SCALE = 1.4426950408889634 / HD**0.5
LOWEST = -1e30
VMEM_LIMIT = 56 * 2**20


def remote(src, dst, send, recv, device):
    return pltpu.make_async_remote_copy(
        src_ref=src,
        dst_ref=dst,
        send_sem=send,
        recv_sem=recv,
        device_id=device,
        device_id_type=MESH,
    )


def tp_of(place, x):
    return ((place // 2) * 4 + x) * 2 + place % 2


class Spread:
    def __init__(self, source, buffer, sems, first, local=True, rows=None):
        sp, tp = lax.axis_index("sp"), lax.axis_index("tp")
        high, x, core = tp // 8, (tp // 2) % 4, tp % 2
        self.sibling = (sp, tp + 1 - 2 * core)
        opposite = (sp, (tp + 8) % 16)
        at = (lambda i: buffer.at[i]) if rows is None else (lambda i: buffer.at[i, rows])
        mine = at(high * 2 + core)
        self.local = pltpu.make_async_copy(source, mine, sems.at[first]) if local else None
        self.pair = remote(source, mine, sems.at[first + 1], sems.at[first + 2], self.sibling)
        self.over = remote(source, mine, sems.at[first + 3], sems.at[first + 4], opposite)
        across = at((1 - high) * 2 + core)
        self.passed = remote(across, across, sems.at[first + 5], sems.at[first + 6], self.sibling)

    def keep(self):
        self.local.start()

    def send(self):
        self.over.start()
        self.pair.start()

    def forward(self):
        self.over.wait_recv()
        self.passed.start()

    def near(self):
        if self.local is not None:
            self.local.wait()
        self.pair.wait_recv()

    def finish(self):
        self.pair.wait_send()
        self.over.wait_send()
        self.passed.wait()


class GatherX:
    def __init__(self, own, blocks, send_sem, recv_sem):
        sp, tp = lax.axis_index("sp"), lax.axis_index("tp")
        x, place = (tp // 2) % 4, (tp // 8) * 2 + tp % 2
        self.x = x
        self.blocks = blocks
        self.copies = {
            k: remote(own, blocks.at[x], send_sem.at[k], recv_sem.at[k], (sp, tp_of(place, (x + k) % 4)))
            for k in (1, 3, 2)
        }
        self.incoming = lambda k, block: remote(own, block, send_sem.at[k], recv_sem.at[k], (sp, tp))
        for copy in self.copies.values():
            copy.start()
        blocks[x] = own[...]

    def have(self, source):
        k = (self.x + 4 - source) % 4

        @pl.when(k > 0)
        def _():
            self.incoming(k, self.blocks.at[source]).wait_recv()

    def sent(self):
        for copy in self.copies.values():
            copy.wait_send()


def scatter_z(product, sent, got, cross_send, cross_recv, send_sem, recv_sem, cross_sem):
    sp, tp = lax.axis_index("sp"), lax.axis_index("tp")
    z, low = sp // 2, sp % 2
    neighbours = (((sp + 2) % 16, tp), ((sp + 14) % 16, tp))
    other = (sp + 1 - 2 * low, tp)

    def hop(way, step, r):
        index = way * 8 + step * 2 + r
        return remote(
            sent.at[way, step, r], got.at[way, step, r], send_sem.at[index], recv_sem.at[index], neighbours[way]
        )

    def split(place):
        part = product(place)
        return jnp.where(low == 0, part[32:], part[:32]), jnp.where(low == 0, part[:32], part[32:])

    far = split((z + 4) % 8)
    for way in range(2):
        sent[way, 0, way] = far[way].astype(BF)
        hop(way, 0, way).start()
    for step in range(1, 4):
        parts = [split((z + 4 - step) % 8), split((z + 4 + step) % 8)]
        for r in range(2):
            for way in range(2):
                piece = parts[way][r]
                if step > 1 or r == way:
                    hop(way, step - 1, r).wait_recv()
                    piece = piece + got[way, step - 1, r].astype(F32)
                sent[way, step, r] = piece.astype(BF)
                hop(way, step, r).start()
    away, mine = split(z)
    for way in range(2):
        hop(way, 3, 0).wait_recv()
        away = away + got[way, 3, 0].astype(F32)
    cross_send[...] = away.astype(BF)
    cross = remote(cross_send, cross_recv, cross_sem.at[0], cross_sem.at[1], other)
    cross.start()
    for way in range(2):
        hop(way, 3, 1).wait_recv()
        mine = mine + got[way, 3, 1].astype(F32)
    for way in range(2):
        hop(way, 0, way).wait_send()
        for step in range(1, 4):
            for r in range(2):
                hop(way, step, r).wait_send()
    cross.wait()
    return mine + cross_recv[...].astype(F32)


def gather_z(own, blocks, send_sem, recv_sem, cross_sem, beside):
    sp, tp = lax.axis_index("sp"), lax.axis_index("tp")
    z, low = sp // 2, sp % 2
    neighbours = (((sp + 2) % 16, tp), ((sp + 14) % 16, tp))
    other = (sp + 1 - 2 * low, tp)

    def hop(way, distance, place, r):
        block = blocks.at[place, low if r == 0 else 1 - low]
        index = way * 10 + distance * 2 + r
        return remote(block, block, send_sem.at[index], recv_sem.at[index], neighbours[way])

    blocks[z, low] = own[...]
    cross = remote(own, blocks.at[z, low], cross_sem.at[0], cross_sem.at[1], other)
    cross.start()
    for way in range(2):
        hop(way, 1, z, 0).start()
    beside[0]()
    remote(own, blocks.at[z, 1 - low], cross_sem.at[0], cross_sem.at[1], other).wait_recv()
    for way in range(2):
        hop(way, 1, z, 1).start()
    for distance in range(1, 4):
        for r in range(2):
            for way in range(2):
                place = (z + (8 - distance if way == 0 else distance)) % 8
                hop(way, distance, place, r).wait_recv()
                if distance < 3 or r == way:
                    hop(way, distance + 1, place, r).start()
        beside[distance]()
    for way in range(2):
        hop(way, 4, (z + 4) % 8, way).wait_recv()
    cross.wait_send()
    for way in range(2):
        for distance in range(1, 4):
            for r in range(2):
                hop(way, distance, z, r).wait_send()
        hop(way, 4, z, way).wait_send()


def block_kernel(
    offset_ref,
    queries_ref,
    keys_ref,
    values_ref,
    residual_ref,
    gain_ref,
    cache_k_ref,
    cache_v_ref,
    w_out_ref,
    w_gate_ref,
    w_up_ref,
    w_down_ref,
    out_ref,
    message,
    own_gain,
    hides,
    received,
    keys,
    own_vals,
    vals_t,
    new_keys,
    new_vals_t,
    own_queries,
    queries,
    tops,
    totals,
    sums,
    out_send,
    out_recv,
    stat_send,
    stat_recv,
    own_attended,
    attended,
    w_out,
    w_gate,
    w_up,
    w_down,
    gains,
    residuals,
    stream,
    sent_a,
    got_a,
    sent_d,
    got_d,
    cross_a,
    cross_d,
    own_squares,
    squares,
    own_scale,
    scales,
    streams,
    normed,
    x_sent,
    x_got,
    own_hidden,
    hidden,
    own_out,
    a2a_send,
    a2a_recv,
    spread_sem,
    small_sem,
    q_send,
    q_recv,
    o_send,
    o_recv,
    st_send,
    st_recv,
    aa_send,
    aa_recv,
    za_send,
    za_recv,
    sq_send,
    sq_recv,
    zn_send,
    zn_recv,
    x_send,
    x_recv,
    ah_send,
    ah_recv,
    zd_send,
    zd_recv,
    cross_sem,
    back_sem,
    sc_send,
    sc_recv,
):
    sp, tp = lax.axis_index("sp"), lax.axis_index("tp")
    high, x, core = tp // 8, (tp // 2) % 4, tp % 2
    place = high * 2 + core
    barrier = pltpu.get_barrier_semaphore()
    peers = [((sp + j) % 16, tp) for j in range(1, 16)] + [(sp, (tp + j) % 16) for j in range(1, 16)]
    for device in peers:
        pl.semaphore_signal(barrier, inc=1, device_id=device, device_id_type=MESH)
    columns = pl.ds(pl.multiple_of((sp // 2) * HD, HD), HD)
    spread_k = Spread(cache_k_ref.at[:, columns], keys, spread_sem, 0)
    spread_v = Spread(vals_t.at[place], vals_t, spread_sem, 7, local=False)
    spread_o = Spread(w_out_ref, w_out, spread_sem, 14)
    spread_g = Spread(w_gate_ref, w_gate, spread_sem, 21)
    spread_u = [
        Spread(w_up_ref.at[first : first + count], w_up, spread_sem, index, rows=pl.ds(first, count))
        for first, count, index in ((0, 256, 28), (256, 128, 35), (384, 128, 42))
    ]
    spread_d = Spread(w_down_ref, w_down, spread_sem, 49)
    load_v = pltpu.make_async_copy(cache_v_ref.at[:, columns], own_vals, small_sem.at[0])
    load_v.start()
    for spread in (spread_k, spread_o, spread_g, *spread_u, spread_d):
        spread.keep()
    for target in range(16):
        lanes = target // 2 * HD
        rows = [
            queries_ref[:, target * 512 + h * HD : target * 512 + h * HD + HD].astype(F32) for h in range(4)
        ]
        rows.append(keys_ref[:, lanes : lanes + HD].astype(F32))
        rows.append(values_ref[:, lanes : lanes + HD].astype(F32))
        message[target] = jnp.concatenate(rows, 0).astype(BF)
    own_gain[...] = jnp.broadcast_to(gain_ref[...].astype(F32).reshape(1, 512), (8, 512))
    for i in range(4):
        lane = lax.broadcasted_iota(jnp.int32, (1024, HD), 1)
        position = lax.broadcasted_iota(jnp.int32, (1024, HD), 0) + tp_of(i, x) * 1024
        hides[i] = jnp.where((lane == 0) & (position >= offset_ref[0]), LOWEST, 0.0).astype(BF)
    load_v.wait()
    for piece in range(4):
        rows = own_vals[piece * 256 : piece * 256 + 256, :].astype(F32)
        vals_t[place, :, piece * 256 : piece * 256 + 256] = rows.T.astype(BF)
    pl.semaphore_wait(barrier, len(peers))

    def exchange(j, _):
        target = (sp + j) % 16
        remote(message.at[target], received.at[sp], a2a_send.at[j], a2a_recv.at[j], (target, tp)).start()
        return 0

    lax.fori_loop(1, 16, exchange, 0)
    spread_k.send()
    spread_v.pair.start()
    received[sp] = message[sp]

    def arrived(j, _):
        block = received.at[(sp + 16 - j) % 16]
        remote(block, block, a2a_send.at[j], a2a_recv.at[j], (sp, tp)).wait()
        return 0

    lax.fori_loop(1, 16, arrived, 0)
    own_queries[...] = received[:, :32, :].reshape(4, 128, HD)
    queries[x, place] = own_queries[place]

    def ask(i, _):
        target = tp_of(i % 4, (x + i // 4) % 4)
        j = (target - tp + 16) % 16

        @pl.when(j > 0)
        def _():
            remote(own_queries.at[i % 4], queries.at[x, place], q_send.at[j], q_recv.at[j], (sp, target)).start()

        return 0

    lax.fori_loop(0, 16, ask, 0)
    spread_v.over.start()
    fresh = received[:, 32:, :].astype(F32).reshape(16, 2, 8, HD)
    new_keys[place] = fresh[:, 0].reshape(HD, HD).astype(BF)
    new_vals_t[place] = fresh[:, 1].reshape(HD, HD).T.astype(BF)

    def quad(i):
        peer = (place + i) % 4
        return (sp, tp_of(peer, x))

    def to_quad(i, kind, src, dst):
        index = 1 + kind * 6 + (i - 1) * 2
        return remote(src, dst, small_sem.at[index], small_sem.at[index + 1], quad(i))

    smalls = []
    for i in range(1, 4):
        peer = (place + i) % 4
        rows = pl.ds(pl.multiple_of(peer * 32, 32), 32)
        smalls.append(to_quad(i, 0, new_keys.at[place], new_keys.at[place]))
        smalls.append(to_quad(i, 1, new_vals_t.at[place], new_vals_t.at[place]))
        smalls.append(to_quad(i, 2, residual_ref.at[rows], residuals.at[place]))
        smalls.append(to_quad(i, 3, own_gain, gains.at[place]))
    for copy in smalls:
        copy.start()
    residuals[place] = residual_ref[pl.ds(pl.multiple_of(place * 32, 32), 32)]
    gains[place] = own_gain[...]
    spread_o.send()
    spread_k.near()
    spread_v.near()

    def attend(k, turn):
        asker = (x + 4 - k) % 4
        if turn == 0:

            @pl.when(k == 2)
            def _():
                spread_k.forward()

            for source in range(4):
                j = (tp - tp_of(source, asker) + 16) % 16

                @pl.when(j > 0)
                def _():
                    block = queries.at[asker, source]
                    remote(block, block, q_send.at[j], q_recv.at[j], (sp, tp)).wait_recv()

        q = queries[asker].reshape(512, HD)
        marked = jnp.concatenate([q, jnp.ones((512, HD), BF)], 1)
        if turn == 0:
            top = jnp.full((1, 512), LOWEST, F32)
            total = jnp.zeros((1, 512), F32)
            summed = jnp.zeros((HD, 512), F32)
        else:
            top = tops[k, 0:1, :]
            total = totals[k, 0:1, :]
            summed = sums[k]
        for chunk in range(4 + turn):
            if chunk < 4:
                held = (high + turn) % 2 * 2 + chunk // 2
                first = (chunk % 2) * 512
                block = jnp.concatenate(
                    [keys[held, first : first + 512, :], hides[held, first : first + 512, :]], 1
                )
                block_t = vals_t[held, :, first : first + 512]
            else:
                block = new_keys[...].reshape(512, HD)
                block_t = jnp.concatenate([new_vals_t[i] for i in range(4)], 1)
            scores = lax.dot_general(
                block, marked if chunk < 4 else q, (((1,), (1,)), ((), ())), preferred_element_type=F32
            )
            if chunk == 4:
                lane = lax.broadcasted_iota(jnp.int32, (128, 512), 1)
                token = ((lane // 256) * 4 + asker) * 256 + ((lane // 128) % 2) * 128
                token = token + place * 32 + ((lane // 32) % 4) * 8 + lane % 8
                ahead = lax.broadcasted_iota(jnp.int32, (128, 512), 0) - token
                scores = jnp.concatenate(
                    [
                        jnp.where(ahead <= -tp_of(i, x) * 128, scores[i * 128 : i * 128 + 128], LOWEST)
                        for i in range(4)
                    ],
                    0,
                )
            higher = jnp.maximum(top, jnp.max(scores, axis=0, keepdims=True))
            weights = jnp.exp2((scores - higher) * SCORE_SCALE)
            factor = jnp.exp2((top - higher) * SCORE_SCALE)
            total = total * factor + jnp.sum(weights, axis=0, keepdims=True)
            summed = summed * factor + jnp.dot(block_t, weights.astype(BF), preferred_element_type=F32)
            top = higher
        if turn == 0:
            tops[k] = jnp.broadcast_to(top, (8, 512))
            totals[k] = jnp.broadcast_to(total, (8, 512))
            sums[k] = summed
            return
        out_send[k] = summed.astype(BF)
        stat_send[k] = jnp.concatenate([jnp.broadcast_to(top, (4, 512)), jnp.broadcast_to(total, (4, 512))], 0)

        @pl.when(k > 0)
        def _():
            target = (sp, tp_of(place, asker))
            remote(out_send.at[k], out_recv.at[k], o_send.at[k], o_recv.at[k], target).start()
            remote(stat_send.at[k], stat_recv.at[k], st_send.at[k], st_recv.at[k], target).start()

    def attend_near(k, _):
        attend(k, 0)
        return 0

    def attend_far(k, _):
        attend((k + 1) % 4, 1)
        return 0

    lax.fori_loop(0, 4, attend_near, 0)
    spread_v.forward()
    spread_g.send()
    spread_k.finish()
    spread_v.finish()
    for copy in smalls:
        copy.wait()
    lax.fori_loop(0, 4, attend_far, 0)
    spread_o.forward()
    spread_u[0].send()

    def asked(j, _):
        remote(own_queries.at[0], queries.at[x, place], q_send.at[j], q_recv.at[j], (sp, tp)).wait_send()
        return 0

    lax.fori_loop(1, 16, asked, 0)

    def collect(k, _):
        remote(out_send.at[k], out_recv.at[k], o_send.at[k], o_recv.at[k], (sp, tp)).wait()
        remote(stat_send.at[k], stat_recv.at[k], st_send.at[k], st_recv.at[k], (sp, tp)).wait()
        return 0

    lax.fori_loop(1, 4, collect, 0)
    tops = [stat_send[0, 0:1, :]] + [stat_recv[k, 0:1, :] for k in range(1, 4)]
    highest = functools.reduce(jnp.maximum, tops)
    shares = [jnp.exp2((top - highest) * SCORE_SCALE) for top in tops]
    total = stat_send[0, 4:5, :] * shares[0]
    summed = out_send[0].astype(F32) * shares[0]
    for k in range(1, 4):
        total = total + stat_recv[k, 4:5, :] * shares[k]
        summed = summed + out_recv[k].astype(F32) * shares[k]
    mixed = (summed / total).T.reshape(16, 4, 8, HD)
    for h in range(4):
        own_attended[:, :, h * HD : (h + 1) * HD] = mixed[:, h].reshape(2, 64, HD).astype(BF)
    whole = GatherX(own_attended, attended, aa_send, aa_recv)
    spread_o.near()
    spread_o.finish()

    awaited = [0, 0]

    def project(target):
        if awaited[0] < 4:
            whole.have(target % 4)
            awaited[0] += 1
        rows = attended[target % 4, target // 4]
        return jnp.concatenate(
            [jnp.dot(rows, w_out[i], preferred_element_type=F32) for i in range(4)], 1
        )

    attn_out = scatter_z(
        project,
        sent_a,
        got_a,
        cross_a.at[0],
        cross_a.at[1],
        za_send,
        za_recv,
        cross_sem.at[pl.ds(0, 2)],
    )
    whole.sent()
    spread_g.forward()
    spread_u[0].forward()
    own_residual = jnp.concatenate([residuals[i] for i in range(4)], 1)
    stream[...] = (own_residual.astype(F32) + attn_out).astype(BF)
    wide = stream[...].astype(F32)
    own_squares[...] = jnp.broadcast_to(jnp.sum(wide * wide, axis=1, keepdims=True), (32, 128))
    tells = [
        remote(own_squares, squares.at[k], sq_send.at[k], sq_recv.at[k], (sp, tp_of(place, (x + k) % 4)))
        for k in range(1, 4)
    ]
    for copy in tells:
        copy.start()
    z = sp // 2

    def send_rest():
        spread_u[1].send()
        for copy in tells:
            copy.wait()
        mean = (own_squares[...] + squares[1] + squares[2] + squares[3]) / D
        own_scale[...] = jnp.concatenate([lax.rsqrt(mean + EPS)] * 4, 0).T[:8]
        scales[sp] = own_scale[...]

        def tell_scale(j, _):
            device = ((sp + j) % 16, tp)
            remote(own_scale, scales.at[sp], sc_send.at[j], sc_recv.at[j], device).start()
            return 0

        lax.fori_loop(1, 16, tell_scale, 0)
        spread_u[2].send()
        spread_d.send()

    def normalise(turn):
        gain = jnp.concatenate([gains[i, 0:1, :] for i in range(4)], 1)

        def one(i, _):
            source = (z + 7 + i // 2 + 4 * turn) % 8
            scale = jnp.broadcast_to(scales[source * 2 + i % 2, 0:1, :], (128, 128)).T[:32]
            scale = jnp.concatenate([scale] * 16, 1)
            normed[source, i % 2] = (streams[source, i % 2].astype(F32) * scale * gain).astype(BF)
            return 0

        lax.fori_loop(0, 8, one, 0)

    def start_gate():
        spread_u[1].forward()
        spread_g.near()
        spread_g.finish()

        def told_scale(j, _):
            block = scales.at[(sp + 16 - j) % 16]
            remote(own_scale, block, sc_send.at[j], sc_recv.at[j], (sp, tp)).wait()
            return 0

        lax.fori_loop(1, 16, told_scale, 0)
        normalise(0)
        open_gate(0)

    def start_up():
        pass_gate(0)
        spread_u[2].forward()
        for spread in spread_u:
            spread.near()
            spread.finish()
        open_up(0)

    def part(turn, column, up):
        rows = normed[(z + 7 + (x + column) % 4 + 4 * turn) % 8].reshape(64, 2048)
        weight = w_up if up else w_gate
        return jnp.dot(rows, weight[...].reshape(2048, 1024), preferred_element_type=F32)

    neighbours = ((sp, tp_of(place, (x + 1) % 4)), (sp, tp_of(place, (x + 3) % 4)))

    def hop(turn, which):
        index = turn * 6 + which
        return remote(
            x_sent.at[index], x_got.at[index], x_send.at[index], x_recv.at[index], neighbours[which // 3]
        )

    def post(turn, which, value):
        x_sent[turn * 6 + which] = value.astype(BF)
        hop(turn, which).start()

    def came(turn, which):
        hop(turn, which).wait_recv()
        return x_got[turn * 6 + which].astype(F32)

    def open_gate(turn):
        post(turn, 0, part(turn, 2, False))
        post(turn, 5, part(turn, 3, False))

    def open_up(turn):
        post(turn, 3, part(turn, 2, True))
        post(turn, 2, part(turn, 1, True))

    def pass_gate(turn):
        second = part(turn, 1, False)
        post(turn, 1, second + came(turn, 0))

    def pass_up(turn):
        second = part(turn, 3, True)
        post(turn, 4, second + came(turn, 3))

    def close_turn(turn):
        gate = part(turn, 0, False)
        up = part(turn, 0, True)
        gate = gate + came(turn, 5) + came(turn, 1)
        up = up + came(turn, 2) + came(turn, 4)
        own_hidden[turn] = (gate / (1.0 + jnp.exp(-gate)) * up).astype(BF)
        return GatherX(
            own_hidden.at[turn], hidden.at[turn], ah_send.at[pl.ds(4 * turn, 4)], ah_recv.at[pl.ds(4 * turn, 4)]
        )

    gather_z(
        stream,
        streams,
        zn_send,
        zn_recv,
        cross_sem.at[pl.ds(2, 2)],
        {0: send_rest, 1: lambda: None, 2: start_gate, 3: start_up},
    )
    normalise(1)
    open_gate(1)
    open_up(1)
    pass_up(0)
    pass_gate(1)
    first_half = close_turn(0)
    pass_up(1)
    second_half = close_turn(1)
    spread_d.forward()
    spread_d.near()
    spread_d.finish()
    for turn in range(2):
        for which in range(6):
            hop(turn, which).wait_send()

    def down(target):
        offset = (5, 4, 6, 3, 7, 2, 0, 1)[awaited[1]]
        awaited[1] += 1
        (first_half, second_half)[offset // 4].have(offset % 4)
        rows = hidden[offset // 4, offset % 4]
        return jnp.concatenate(
            [jnp.dot(rows, w_down[i], preferred_element_type=F32) for i in range(4)], 1
        )

    added = scatter_z(
        down, sent_d, got_d, cross_d.at[0], cross_d.at[1], zd_send, zd_recv, cross_sem.at[pl.ds(4, 2)]
    )
    first_half.sent()
    second_half.sent()
    result = (stream[...].astype(F32) + added).astype(BF)
    for i in range(4):
        own_out[i] = result[:, i * 512 : i * 512 + 512]
    mine = pl.ds(pl.multiple_of(place * 32, 32), 32)
    backs = [
        remote(own_out.at[(place + i) % 4], out_ref.at[mine], back_sem.at[2 * i], back_sem.at[2 * i + 1], quad(i))
        for i in range(1, 4)
    ]
    for copy in backs:
        copy.start()
    out_ref[mine] = own_out[place]
    for copy in backs:
        copy.wait()


def run_block(offset, queries, keys, values, residual, gain, cache_keys, cache_values, w_out, w_gate, w_up, w_down):
    hop = VM((2, 4, 2, 32, 2048), BF)
    vmem = pl.BlockSpec(memory_space=pltpu.VMEM)
    return pl.pallas_call(
        block_kernel,
        out_shape=jax.ShapeDtypeStruct((128, 512), BF),
        in_specs=[pl.BlockSpec(memory_space=pltpu.SMEM)] + [vmem] * 5 + [pl.BlockSpec(memory_space=pl.ANY)] * 6,
        out_specs=vmem,
        scratch_shapes=[
            VM((16, 48, HD), BF),
            VM((8, 512), F32),
            VM((4, 1024, HD), BF),
            VM((16, 48, HD), BF),
            VM((4, 1024, HD), BF),
            VM((1024, HD), BF),
            VM((4, HD, 1024), BF),
            VM((4, 128, HD), BF),
            VM((4, HD, 128), BF),
            VM((4, 128, HD), BF),
            VM((4, 4, 128, HD), BF),
            VM((4, 8, 512), F32),
            VM((4, 8, 512), F32),
            VM((4, HD, 512), F32),
            VM((4, HD, 512), BF),
            VM((4, HD, 512), BF),
            VM((4, 8, 512), F32),
            VM((4, 8, 512), F32),
            VM((2, 64, 512), BF),
            VM((4, 2, 64, 512), BF),
            VM((4, 512, 512), BF),
            VM((4, 512, 1024), BF),
            VM((4, 512, 1024), BF),
            VM((4, 1024, 512), BF),
            VM((4, 8, 512), F32),
            VM((4, 32, 512), BF),
            VM((32, 2048), BF),
            hop,
            hop,
            hop,
            hop,
            VM((2, 32, 2048), BF),
            VM((2, 32, 2048), BF),
            VM((32, 128), F32),
            VM((4, 32, 128), F32),
            VM((8, 128), F32),
            VM((16, 8, 128), F32),
            VM((8, 2, 32, 2048), BF),
            VM((8, 2, 32, 2048), BF),
            VM((12, 64, 1024), BF),
            VM((12, 64, 1024), BF),
            VM((2, 64, 1024), BF),
            VM((2, 4, 64, 1024), BF),
            VM((4, 32, 512), BF),
        ]
        + [DMA((16,))] * 2
        + [DMA((56,)), DMA((25,))]
        + [DMA((16,))] * 2
        + [DMA((4,))] * 6
        + [DMA((16,))] * 2
        + [DMA((4,))] * 2
        + [DMA((20,))] * 2
        + [DMA((12,))] * 2
        + [DMA((8,))] * 2
        + [DMA((16,))] * 2
        + [DMA((6,)), DMA((8,)), DMA((16,)), DMA((16,))],
        compiler_params=pltpu.CompilerParams(
            collective_id=0, has_side_effects=True, vmem_limit_bytes=VMEM_LIMIT
        ),
        name="block",
    )(offset, queries, keys, values, residual, gain, cache_keys, cache_values, w_out, w_gate, w_up, w_down)


def per_device(
    residual,
    queries,
    keys,
    values,
    cache_keys,
    cache_values,
    offset,
    w_out,
    norm_gain,
    w_gate,
    w_up,
    w_down,
):
    return run_block(
        offset,
        queries,
        keys,
        values,
        residual,
        norm_gain,
        cache_keys,
        cache_values,
        w_out,
        w_gate,
        w_up,
        w_down,
    )


def solution(mesh):
    in_specs = (
        P("sp", "tp"),
        P(("tp", "sp"), None),
        P(("tp", "sp"), None),
        P(("tp", "sp"), None),
        P("tp", None),
        P("tp", None),
        P(),
        P("sp", "tp"),
        P("tp"),
        P("tp", "sp"),
        P("tp", "sp"),
        P("sp", "tp"),
    )
    out_specs = P("sp", "tp")
    return jax.shard_map(
        per_device, mesh=mesh, in_specs=in_specs, out_specs=out_specs, check_vma=False
    )
```

```python
import functools

import jax
import jax.numpy as jnp
from jax import lax
from jax.experimental import pallas as pl
from jax.experimental.pallas import tpu as pltpu
from jax.sharding import PartitionSpec as P

D = 8192
H = 64
KV = 8
HD = 128
EPS = 1e-6
BF = jnp.bfloat16
F32 = jnp.float32
MESH = pl.DeviceIdType.MESH
VM = pltpu.VMEM
DMA = pltpu.SemaphoreType.DMA
SCORE_SCALE = 1.4426950408889634 / HD**0.5
LOWEST = -1e30
VMEM_LIMIT = 56 * 2**20


def remote(src, dst, send, recv, device):
    return pltpu.make_async_remote_copy(
        src_ref=src,
        dst_ref=dst,
        send_sem=send,
        recv_sem=recv,
        device_id=device,
        device_id_type=MESH,
    )


def tp_of(place, x):
    return ((place // 2) * 4 + x) * 2 + place % 2


class Spread:
    def __init__(self, source, buffer, sems, first, local=True, rows=None):
        sp, tp = lax.axis_index("sp"), lax.axis_index("tp")
        high, x, core = tp // 8, (tp // 2) % 4, tp % 2
        self.sibling = (sp, tp + 1 - 2 * core)
        opposite = (sp, (tp + 8) % 16)
        at = (lambda i: buffer.at[i]) if rows is None else (lambda i: buffer.at[i, rows])
        mine = at(high * 2 + core)
        self.local = pltpu.make_async_copy(source, mine, sems.at[first]) if local else None
        self.pair = remote(source, mine, sems.at[first + 1], sems.at[first + 2], self.sibling)
        self.over = remote(source, mine, sems.at[first + 3], sems.at[first + 4], opposite)
        across = at((1 - high) * 2 + core)
        self.passed = remote(across, across, sems.at[first + 5], sems.at[first + 6], self.sibling)

    def keep(self):
        self.local.start()

    def send(self):
        self.over.start()
        self.pair.start()

    def forward(self):
        self.over.wait_recv()
        self.passed.start()

    def near(self):
        if self.local is not None:
            self.local.wait()
        self.pair.wait_recv()

    def finish(self):
        self.pair.wait_send()
        self.over.wait_send()
        self.passed.wait()


class GatherX:
    def __init__(self, own, blocks, send_sem, recv_sem):
        sp, tp = lax.axis_index("sp"), lax.axis_index("tp")
        x, place = (tp // 2) % 4, (tp // 8) * 2 + tp % 2
        self.x = x
        self.blocks = blocks
        self.copies = {
            k: remote(own, blocks.at[x], send_sem.at[k], recv_sem.at[k], (sp, tp_of(place, (x + k) % 4)))
            for k in (1, 3, 2)
        }
        self.incoming = lambda k, block: remote(own, block, send_sem.at[k], recv_sem.at[k], (sp, tp))
        for copy in self.copies.values():
            copy.start()
        blocks[x] = own[...]

    def have(self, source):
        k = (self.x + 4 - source) % 4

        @pl.when(k > 0)
        def _():
            self.incoming(k, self.blocks.at[source]).wait_recv()

    def sent(self):
        for copy in self.copies.values():
            copy.wait_send()


def scatter_z(product, sent, got, cross_send, cross_recv, send_sem, recv_sem, cross_sem):
    sp, tp = lax.axis_index("sp"), lax.axis_index("tp")
    z, low = sp // 2, sp % 2
    neighbours = (((sp + 2) % 16, tp), ((sp + 14) % 16, tp))
    other = (sp + 1 - 2 * low, tp)

    def hop(way, step, r, h):
        return remote(
            sent.at[way, step, r, h],
            got.at[way, step, r, h],
            send_sem.at[way * 16 + step * 4 + r * 2 + h],
            recv_sem.at[way * 16 + step * 4 + r * 2 + h],
            neighbours[way],
        )

    def post(way, step, r, h, piece):
        sent[way, step, r, h] = piece.astype(BF)
        hop(way, step, r, h).start()

    def split(place):
        part = product(place)
        return jnp.where(low == 0, part[32:], part[:32]), jnp.where(low == 0, part[:32], part[32:])

    far = split((z + 4) % 8)
    for r in range(2):
        for way in range(2):
            post(way, 0, r, way, far[r][way * 16 : way * 16 + 16])
    for step in range(1, 4):
        parts = [split((z + 4 - step) % 8), split((z + 4 + step) % 8)]
        for r in range(2):
            for late in range(2):
                for way in range(2):
                    h = way if late else 1 - way
                    piece = parts[way][r][h * 16 : h * 16 + 16]
                    if step > 1 or late:
                        hop(way, step - 1, r, h).wait_recv()
                        piece = piece + got[way, step - 1, r, h].astype(F32)
                    post(way, step, r, h, piece)
    away, mine = split(z)

    def arrived(r):
        for late in range(2):
            for way in range(2):
                hop(way, 3, r, way if late else 1 - way).wait_recv()
        return got[0, 3, r].reshape(32, 2048).astype(F32) + got[1, 3, r].reshape(32, 2048).astype(F32)

    away = away + arrived(0)
    cross_send[...] = away.astype(BF)
    cross = remote(cross_send, cross_recv, cross_sem.at[0], cross_sem.at[1], other)
    cross.start()
    mine = mine + arrived(1)
    for way in range(2):
        for r in range(2):
            hop(way, 0, r, way).wait_send()
            for step in range(1, 4):
                for h in range(2):
                    hop(way, step, r, h).wait_send()
    cross.wait()
    return mine + cross_recv[...].astype(F32)


def gather_z(own, blocks, send_sem, recv_sem, cross_sem, beside):
    sp, tp = lax.axis_index("sp"), lax.axis_index("tp")
    z, low = sp // 2, sp % 2
    neighbours = (((sp + 2) % 16, tp), ((sp + 14) % 16, tp))
    other = (sp + 1 - 2 * low, tp)

    def hop(way, distance, place, r, h):
        block = blocks.at[place, low if r == 0 else 1 - low, pl.ds(h * 16, 16)]
        index = way * 20 + distance * 4 + r * 2 + h
        return remote(block, block, send_sem.at[index], recv_sem.at[index], neighbours[way])

    def cross(source, h):
        rows = pl.ds(h * 16, 16)
        return remote(
            own.at[rows], blocks.at[z, source, rows], cross_sem.at[2 * h], cross_sem.at[2 * h + 1], other
        )

    for h in range(2):
        cross(low, h).start()
    blocks[z, low] = own[...]
    for h in range(2):
        for way in range(2):
            hop(way, 1, z, 0, h).start()
    for h in range(2):
        cross(1 - low, h).wait_recv()
        for way in range(2):
            hop(way, 1, z, 1, h).start()
        if h == 0:
            beside[0]()
    for distance in range(1, 4):
        for r in range(2):
            for h in range(2):
                for way in range(2):
                    place = (z + (8 - distance if way == 0 else distance)) % 8
                    hop(way, distance, place, r, h).wait_recv()
                    if distance < 3 or r == way:
                        hop(way, distance + 1, place, r, h).start()
        beside[distance]()
    for way in range(2):
        for h in range(2):
            hop(way, 4, (z + 4) % 8, way, h).wait_recv()
    for h in range(2):
        cross(low, h).wait_send()
        for way in range(2):
            for distance in range(1, 4):
                for r in range(2):
                    hop(way, distance, z, r, h).wait_send()
            hop(way, 4, z, way, h).wait_send()


def block_kernel(
    offset_ref,
    queries_ref,
    keys_ref,
    values_ref,
    residual_ref,
    gain_ref,
    cache_k_ref,
    cache_v_ref,
    w_out_ref,
    w_gate_ref,
    w_up_ref,
    w_down_ref,
    out_ref,
    message,
    own_gain,
    hides,
    received,
    keys,
    own_vals,
    vals_t,
    new_keys,
    new_vals_t,
    own_queries,
    queries,
    tops,
    totals,
    sums,
    out_send,
    out_recv,
    stat_send,
    stat_recv,
    own_attended,
    attended,
    w_out,
    w_gate,
    w_up,
    w_down,
    gains,
    residuals,
    stream,
    sent_a,
    got_a,
    sent_d,
    got_d,
    cross_a,
    cross_d,
    own_squares,
    squares,
    own_scale,
    scales,
    streams,
    normed,
    x_sent,
    x_got,
    own_hidden,
    hidden,
    own_out,
    a2a_send,
    a2a_recv,
    spread_sem,
    small_sem,
    q_send,
    q_recv,
    o_send,
    o_recv,
    st_send,
    st_recv,
    aa_send,
    aa_recv,
    za_send,
    za_recv,
    sq_send,
    sq_recv,
    zn_send,
    zn_recv,
    x_send,
    x_recv,
    ah_send,
    ah_recv,
    zd_send,
    zd_recv,
    cross_sem,
    back_sem,
    sc_send,
    sc_recv,
):
    sp, tp = lax.axis_index("sp"), lax.axis_index("tp")
    high, x, core = tp // 8, (tp // 2) % 4, tp % 2
    place = high * 2 + core
    barrier = pltpu.get_barrier_semaphore()
    peers = [((sp + j) % 16, tp) for j in range(1, 16)] + [(sp, (tp + j) % 16) for j in range(1, 16)]
    for device in peers:
        pl.semaphore_signal(barrier, inc=1, device_id=device, device_id_type=MESH)
    columns = pl.ds(pl.multiple_of((sp // 2) * HD, HD), HD)
    spread_k = Spread(cache_k_ref.at[:, columns], keys, spread_sem, 0)
    spread_v = Spread(vals_t.at[place], vals_t, spread_sem, 7, local=False)
    spread_o = Spread(w_out_ref, w_out, spread_sem, 14)
    spread_g = Spread(w_gate_ref, w_gate, spread_sem, 21)
    spread_u = [
        Spread(w_up_ref.at[first : first + count], w_up, spread_sem, index, rows=pl.ds(first, count))
        for first, count, index in ((0, 256, 28), (256, 128, 35), (384, 128, 42))
    ]
    spread_d = Spread(w_down_ref, w_down, spread_sem, 49)
    load_v = pltpu.make_async_copy(cache_v_ref.at[:, columns], own_vals, small_sem.at[0])
    load_v.start()
    for spread in (spread_k, spread_o, spread_g, *spread_u, spread_d):
        spread.keep()
    for target in range(16):
        lanes = target // 2 * HD
        rows = [
            queries_ref[:, target * 512 + h * HD : target * 512 + h * HD + HD].astype(F32) for h in range(4)
        ]
        rows.append(keys_ref[:, lanes : lanes + HD].astype(F32))
        rows.append(values_ref[:, lanes : lanes + HD].astype(F32))
        message[target] = jnp.concatenate(rows, 0).astype(BF)
    own_gain[...] = jnp.broadcast_to(gain_ref[...].astype(F32).reshape(1, 512), (8, 512))
    for i in range(4):
        lane = lax.broadcasted_iota(jnp.int32, (1024, HD), 1)
        position = lax.broadcasted_iota(jnp.int32, (1024, HD), 0) + tp_of(i, x) * 1024
        hides[i] = jnp.where((lane == 0) & (position >= offset_ref[0]), LOWEST, 0.0).astype(BF)
    load_v.wait()
    for piece in range(4):
        rows = own_vals[piece * 256 : piece * 256 + 256, :].astype(F32)
        vals_t[place, :, piece * 256 : piece * 256 + 256] = rows.T.astype(BF)
    pl.semaphore_wait(barrier, len(peers))

    def exchange(j, _):
        target = (sp + j) % 16
        remote(message.at[target], received.at[sp], a2a_send.at[j], a2a_recv.at[j], (target, tp)).start()
        return 0

    lax.fori_loop(1, 16, exchange, 0)
    spread_k.send()
    spread_v.pair.start()
    received[sp] = message[sp]

    def arrived(j, _):
        block = received.at[(sp + 16 - j) % 16]
        remote(block, block, a2a_send.at[j], a2a_recv.at[j], (sp, tp)).wait()
        return 0

    lax.fori_loop(1, 16, arrived, 0)
    own_queries[...] = received[:, :32, :].reshape(4, 128, HD)
    queries[x, place] = own_queries[place]

    def ask(i, _):
        target = tp_of(i % 4, (x + i // 4) % 4)
        j = (target - tp + 16) % 16

        @pl.when(j > 0)
        def _():
            remote(own_queries.at[i % 4], queries.at[x, place], q_send.at[j], q_recv.at[j], (sp, target)).start()

        return 0

    lax.fori_loop(0, 16, ask, 0)
    spread_v.over.start()
    fresh = received[:, 32:, :].astype(F32).reshape(16, 2, 8, HD)
    new_keys[place] = fresh[:, 0].reshape(HD, HD).astype(BF)
    new_vals_t[place] = fresh[:, 1].reshape(HD, HD).T.astype(BF)

    def quad(i):
        peer = (place + i) % 4
        return (sp, tp_of(peer, x))

    def to_quad(i, kind, src, dst):
        index = 1 + kind * 6 + (i - 1) * 2
        return remote(src, dst, small_sem.at[index], small_sem.at[index + 1], quad(i))

    smalls = []
    for i in range(1, 4):
        peer = (place + i) % 4
        rows = pl.ds(pl.multiple_of(peer * 32, 32), 32)
        smalls.append(to_quad(i, 0, new_keys.at[place], new_keys.at[place]))
        smalls.append(to_quad(i, 1, new_vals_t.at[place], new_vals_t.at[place]))
        smalls.append(to_quad(i, 2, residual_ref.at[rows], residuals.at[place]))
        smalls.append(to_quad(i, 3, own_gain, gains.at[place]))
    for copy in smalls:
        copy.start()
    residuals[place] = residual_ref[pl.ds(pl.multiple_of(place * 32, 32), 32)]
    gains[place] = own_gain[...]
    spread_o.send()
    spread_k.near()
    spread_v.near()

    def attend(k, turn):
        asker = (x + 4 - k) % 4
        if turn == 0:

            @pl.when(k == 2)
            def _():
                spread_k.forward()

            for source in range(4):
                j = (tp - tp_of(source, asker) + 16) % 16

                @pl.when(j > 0)
                def _():
                    block = queries.at[asker, source]
                    remote(block, block, q_send.at[j], q_recv.at[j], (sp, tp)).wait_recv()

        q = queries[asker].reshape(512, HD)
        marked = jnp.concatenate([q, jnp.ones((512, HD), BF)], 1)
        if turn == 0:
            top = jnp.full((1, 512), LOWEST, F32)
            total = jnp.zeros((1, 512), F32)
            summed = jnp.zeros((HD, 512), F32)
        else:
            top = tops[k, 0:1, :]
            total = totals[k, 0:1, :]
            summed = sums[k]
        for chunk in range(4 + turn):
            if chunk < 4:
                held = (high + turn) % 2 * 2 + chunk // 2
                first = (chunk % 2) * 512
                block = jnp.concatenate(
                    [keys[held, first : first + 512, :], hides[held, first : first + 512, :]], 1
                )
                block_t = vals_t[held, :, first : first + 512]
            else:
                block = new_keys[...].reshape(512, HD)
                block_t = jnp.concatenate([new_vals_t[i] for i in range(4)], 1)
            scores = lax.dot_general(
                block, marked if chunk < 4 else q, (((1,), (1,)), ((), ())), preferred_element_type=F32
            )
            if chunk == 4:
                lane = lax.broadcasted_iota(jnp.int32, (128, 512), 1)
                token = ((lane // 256) * 4 + asker) * 256 + ((lane // 128) % 2) * 128
                token = token + place * 32 + ((lane // 32) % 4) * 8 + lane % 8
                ahead = lax.broadcasted_iota(jnp.int32, (128, 512), 0) - token
                scores = jnp.concatenate(
                    [
                        jnp.where(ahead <= -tp_of(i, x) * 128, scores[i * 128 : i * 128 + 128], LOWEST)
                        for i in range(4)
                    ],
                    0,
                )
            higher = jnp.maximum(top, jnp.max(scores, axis=0, keepdims=True))
            weights = jnp.exp2((scores - higher) * SCORE_SCALE)
            factor = jnp.exp2((top - higher) * SCORE_SCALE)
            total = total * factor + jnp.sum(weights, axis=0, keepdims=True)
            summed = summed * factor + jnp.dot(block_t, weights.astype(BF), preferred_element_type=F32)
            top = higher
        if turn == 0:
            tops[k] = jnp.broadcast_to(top, (8, 512))
            totals[k] = jnp.broadcast_to(total, (8, 512))
            sums[k] = summed
            return
        out_send[k] = summed.astype(BF)
        stat_send[k] = jnp.concatenate([jnp.broadcast_to(top, (4, 512)), jnp.broadcast_to(total, (4, 512))], 0)

        @pl.when(k > 0)
        def _():
            target = (sp, tp_of(place, asker))
            remote(out_send.at[k], out_recv.at[k], o_send.at[k], o_recv.at[k], target).start()
            remote(stat_send.at[k], stat_recv.at[k], st_send.at[k], st_recv.at[k], target).start()

    def attend_near(k, _):
        attend(k, 0)
        return 0

    def attend_far(k, _):
        attend((k + 1) % 4, 1)
        return 0

    lax.fori_loop(0, 4, attend_near, 0)
    spread_v.forward()
    spread_g.send()
    spread_k.finish()
    spread_v.finish()
    for copy in smalls:
        copy.wait()
    lax.fori_loop(0, 4, attend_far, 0)
    spread_u[0].send()

    def asked(j, _):
        remote(own_queries.at[0], queries.at[x, place], q_send.at[j], q_recv.at[j], (sp, tp)).wait_send()
        return 0

    lax.fori_loop(1, 16, asked, 0)

    def collect(k, _):
        remote(out_send.at[k], out_recv.at[k], o_send.at[k], o_recv.at[k], (sp, tp)).wait()
        remote(stat_send.at[k], stat_recv.at[k], st_send.at[k], st_recv.at[k], (sp, tp)).wait()
        return 0

    lax.fori_loop(1, 4, collect, 0)
    tops = [stat_send[0, 0:1, :]] + [stat_recv[k, 0:1, :] for k in range(1, 4)]
    highest = functools.reduce(jnp.maximum, tops)
    shares = [jnp.exp2((top - highest) * SCORE_SCALE) for top in tops]
    total = stat_send[0, 4:5, :] * shares[0]
    summed = out_send[0].astype(F32) * shares[0]
    for k in range(1, 4):
        total = total + stat_recv[k, 4:5, :] * shares[k]
        summed = summed + out_recv[k].astype(F32) * shares[k]
    mixed = (summed / total).T.reshape(16, 4, 8, HD)
    for h in range(4):
        own_attended[:, :, h * HD : (h + 1) * HD] = mixed[:, h].reshape(2, 64, HD).astype(BF)
    whole = GatherX(own_attended, attended, aa_send, aa_recv)
    spread_o.forward()
    spread_o.near()
    spread_o.finish()

    awaited = [0, 0]

    def project(target):
        if awaited[0] < 4:
            whole.have(target % 4)
            awaited[0] += 1
        rows = attended[target % 4, target // 4]
        return jnp.concatenate(
            [jnp.dot(rows, w_out[i], preferred_element_type=F32) for i in range(4)], 1
        )

    attn_out = scatter_z(
        project,
        sent_a,
        got_a,
        cross_a.at[0],
        cross_a.at[1],
        za_send,
        za_recv,
        cross_sem.at[pl.ds(0, 2)],
    )
    whole.sent()
    spread_g.forward()
    spread_u[0].forward()
    own_residual = jnp.concatenate([residuals[i] for i in range(4)], 1)
    stream[...] = (own_residual.astype(F32) + attn_out).astype(BF)
    wide = stream[...].astype(F32)
    own_squares[...] = jnp.broadcast_to(jnp.sum(wide * wide, axis=1, keepdims=True), (32, 128))
    tells = [
        remote(own_squares, squares.at[k], sq_send.at[k], sq_recv.at[k], (sp, tp_of(place, (x + k) % 4)))
        for k in range(1, 4)
    ]
    for copy in tells:
        copy.start()
    z = sp // 2

    def send_rest():
        spread_u[1].send()
        for copy in tells:
            copy.wait()
        mean = (own_squares[...] + squares[1] + squares[2] + squares[3]) / D
        own_scale[...] = jnp.concatenate([lax.rsqrt(mean + EPS)] * 4, 0).T[:8]
        scales[sp] = own_scale[...]

        def tell_scale(j, _):
            device = ((sp + j) % 16, tp)
            remote(own_scale, scales.at[sp], sc_send.at[j], sc_recv.at[j], device).start()
            return 0

        lax.fori_loop(1, 16, tell_scale, 0)
        spread_u[2].send()
        spread_d.send()

    def normalise(turn):
        gain = jnp.concatenate([gains[i, 0:1, :] for i in range(4)], 1)

        def one(i, _):
            source = (z + 7 + i // 2 + 4 * turn) % 8
            scale = jnp.broadcast_to(scales[source * 2 + i % 2, 0:1, :], (128, 128)).T[:32]
            scale = jnp.concatenate([scale] * 16, 1)
            normed[source, i % 2] = (streams[source, i % 2].astype(F32) * scale * gain).astype(BF)
            return 0

        lax.fori_loop(0, 8, one, 0)

    def start_gate():
        spread_u[1].forward()
        spread_g.near()
        spread_g.finish()

        def told_scale(j, _):
            block = scales.at[(sp + 16 - j) % 16]
            remote(own_scale, block, sc_send.at[j], sc_recv.at[j], (sp, tp)).wait()
            return 0

        lax.fori_loop(1, 16, told_scale, 0)
        normalise(0)
        open_gate(0)

    def start_up():
        pass_gate(0)
        spread_u[2].forward()
        for spread in spread_u:
            spread.near()
            spread.finish()
        open_up(0)

    def part(turn, column, up):
        rows = normed[(z + 7 + (x + column) % 4 + 4 * turn) % 8].reshape(64, 2048)
        weight = w_up if up else w_gate
        return jnp.dot(rows, weight[...].reshape(2048, 1024), preferred_element_type=F32)

    neighbours = ((sp, tp_of(place, (x + 1) % 4)), (sp, tp_of(place, (x + 3) % 4)))

    def hop(turn, which):
        index = turn * 6 + which
        return remote(
            x_sent.at[index], x_got.at[index], x_send.at[index], x_recv.at[index], neighbours[which // 3]
        )

    def post(turn, which, value):
        x_sent[turn * 6 + which] = value.astype(BF)
        hop(turn, which).start()

    def came(turn, which):
        hop(turn, which).wait_recv()
        return x_got[turn * 6 + which].astype(F32)

    def open_gate(turn):
        post(turn, 0, part(turn, 2, False))
        post(turn, 5, part(turn, 3, False))

    def open_up(turn):
        post(turn, 3, part(turn, 2, True))
        post(turn, 2, part(turn, 1, True))

    def pass_gate(turn):
        second = part(turn, 1, False)
        post(turn, 1, second + came(turn, 0))

    def pass_up(turn):
        second = part(turn, 3, True)
        post(turn, 4, second + came(turn, 3))

    def close_turn(turn):
        gate = part(turn, 0, False)
        up = part(turn, 0, True)
        gate = gate + came(turn, 5) + came(turn, 1)
        up = up + came(turn, 2) + came(turn, 4)
        own_hidden[turn] = (gate / (1.0 + jnp.exp(-gate)) * up).astype(BF)
        return GatherX(
            own_hidden.at[turn], hidden.at[turn], ah_send.at[pl.ds(4 * turn, 4)], ah_recv.at[pl.ds(4 * turn, 4)]
        )

    gather_z(
        stream,
        streams,
        zn_send,
        zn_recv,
        cross_sem.at[pl.ds(4, 4)],
        {0: send_rest, 1: lambda: None, 2: start_gate, 3: start_up},
    )
    normalise(1)
    open_gate(1)
    open_up(1)
    pass_up(0)
    pass_gate(1)
    first_half = close_turn(0)
    pass_up(1)
    second_half = close_turn(1)
    spread_d.forward()
    spread_d.near()
    spread_d.finish()
    for turn in range(2):
        for which in range(6):
            hop(turn, which).wait_send()

    def down(target):
        offset = (5, 4, 6, 3, 7, 2, 0, 1)[awaited[1]]
        awaited[1] += 1
        (first_half, second_half)[offset // 4].have(offset % 4)
        rows = hidden[offset // 4, offset % 4]
        return jnp.concatenate(
            [jnp.dot(rows, w_down[i], preferred_element_type=F32) for i in range(4)], 1
        )

    added = scatter_z(
        down, sent_d, got_d, cross_d.at[0], cross_d.at[1], zd_send, zd_recv, cross_sem.at[pl.ds(2, 2)]
    )
    first_half.sent()
    second_half.sent()
    result = (stream[...].astype(F32) + added).astype(BF)
    for i in range(4):
        own_out[i] = result[:, i * 512 : i * 512 + 512]
    mine = pl.ds(pl.multiple_of(place * 32, 32), 32)
    backs = [
        remote(own_out.at[(place + i) % 4], out_ref.at[mine], back_sem.at[2 * i], back_sem.at[2 * i + 1], quad(i))
        for i in range(1, 4)
    ]
    for copy in backs:
        copy.start()
    out_ref[mine] = own_out[place]
    for copy in backs:
        copy.wait()


def run_block(offset, queries, keys, values, residual, gain, cache_keys, cache_values, w_out, w_gate, w_up, w_down):
    hop = VM((2, 4, 2, 2, 16, 2048), BF)
    vmem = pl.BlockSpec(memory_space=pltpu.VMEM)
    return pl.pallas_call(
        block_kernel,
        out_shape=jax.ShapeDtypeStruct((128, 512), BF),
        in_specs=[pl.BlockSpec(memory_space=pltpu.SMEM)] + [vmem] * 5 + [pl.BlockSpec(memory_space=pl.ANY)] * 6,
        out_specs=vmem,
        scratch_shapes=[
            VM((16, 48, HD), BF),
            VM((8, 512), F32),
            VM((4, 1024, HD), BF),
            VM((16, 48, HD), BF),
            VM((4, 1024, HD), BF),
            VM((1024, HD), BF),
            VM((4, HD, 1024), BF),
            VM((4, 128, HD), BF),
            VM((4, HD, 128), BF),
            VM((4, 128, HD), BF),
            VM((4, 4, 128, HD), BF),
            VM((4, 8, 512), F32),
            VM((4, 8, 512), F32),
            VM((4, HD, 512), F32),
            VM((4, HD, 512), BF),
            VM((4, HD, 512), BF),
            VM((4, 8, 512), F32),
            VM((4, 8, 512), F32),
            VM((2, 64, 512), BF),
            VM((4, 2, 64, 512), BF),
            VM((4, 512, 512), BF),
            VM((4, 512, 1024), BF),
            VM((4, 512, 1024), BF),
            VM((4, 1024, 512), BF),
            VM((4, 8, 512), F32),
            VM((4, 32, 512), BF),
            VM((32, 2048), BF),
            hop,
            hop,
            hop,
            hop,
            VM((2, 32, 2048), BF),
            VM((2, 32, 2048), BF),
            VM((32, 128), F32),
            VM((4, 32, 128), F32),
            VM((8, 128), F32),
            VM((16, 8, 128), F32),
            VM((8, 2, 32, 2048), BF),
            VM((8, 2, 32, 2048), BF),
            VM((12, 64, 1024), BF),
            VM((12, 64, 1024), BF),
            VM((2, 64, 1024), BF),
            VM((2, 4, 64, 1024), BF),
            VM((4, 32, 512), BF),
        ]
        + [DMA((16,))] * 2
        + [DMA((56,)), DMA((25,))]
        + [DMA((16,))] * 2
        + [DMA((4,))] * 6
        + [DMA((32,))] * 2
        + [DMA((4,))] * 2
        + [DMA((40,))] * 2
        + [DMA((12,))] * 2
        + [DMA((8,))] * 2
        + [DMA((32,))] * 2
        + [DMA((8,)), DMA((8,)), DMA((16,)), DMA((16,))],
        compiler_params=pltpu.CompilerParams(
            collective_id=0, has_side_effects=True, vmem_limit_bytes=VMEM_LIMIT
        ),
        name="block",
    )(offset, queries, keys, values, residual, gain, cache_keys, cache_values, w_out, w_gate, w_up, w_down)


def per_device(
    residual,
    queries,
    keys,
    values,
    cache_keys,
    cache_values,
    offset,
    w_out,
    norm_gain,
    w_gate,
    w_up,
    w_down,
):
    return run_block(
        offset,
        queries,
        keys,
        values,
        residual,
        norm_gain,
        cache_keys,
        cache_values,
        w_out,
        w_gate,
        w_up,
        w_down,
    )


def solution(mesh):
    in_specs = (
        P("sp", "tp"),
        P(("tp", "sp"), None),
        P(("tp", "sp"), None),
        P(("tp", "sp"), None),
        P("tp", None),
        P("tp", None),
        P(),
        P("sp", "tp"),
        P("tp"),
        P("tp", "sp"),
        P("tp", "sp"),
        P("sp", "tp"),
    )
    out_specs = P("sp", "tp")
    return jax.shard_map(
        per_device, mesh=mesh, in_specs=in_specs, out_specs=out_specs, check_vma=False
    )
```

```python
import functools

import jax
import jax.numpy as jnp
from jax import lax
from jax.experimental import pallas as pl
from jax.experimental.pallas import tpu as pltpu
from jax.sharding import PartitionSpec as P

D = 8192
H = 64
KV = 8
HD = 128
EPS = 1e-6
BF = jnp.bfloat16
F32 = jnp.float32
MESH = pl.DeviceIdType.MESH
VM = pltpu.VMEM
DMA = pltpu.SemaphoreType.DMA
SCORE_SCALE = 1.4426950408889634 / HD**0.5
LOWEST = -1e30
VMEM_LIMIT = 56 * 2**20


def remote(src, dst, send, recv, device):
    return pltpu.make_async_remote_copy(
        src_ref=src,
        dst_ref=dst,
        send_sem=send,
        recv_sem=recv,
        device_id=device,
        device_id_type=MESH,
    )


def tp_of(place, x):
    return ((place // 2) * 4 + x) * 2 + place % 2


class Spread:
    def __init__(self, source, buffer, sems, first, local=True, rows=None):
        sp, tp = lax.axis_index("sp"), lax.axis_index("tp")
        high, x, core = tp // 8, (tp // 2) % 4, tp % 2
        self.sibling = (sp, tp + 1 - 2 * core)
        opposite = (sp, (tp + 8) % 16)
        at = (lambda i: buffer.at[i]) if rows is None else (lambda i: buffer.at[i, rows])
        mine = at(high * 2 + core)
        self.local = pltpu.make_async_copy(source, mine, sems.at[first]) if local else None
        self.pair = remote(source, mine, sems.at[first + 1], sems.at[first + 2], self.sibling)
        self.over = remote(source, mine, sems.at[first + 3], sems.at[first + 4], opposite)
        across = at((1 - high) * 2 + core)
        self.passed = remote(across, across, sems.at[first + 5], sems.at[first + 6], self.sibling)

    def keep(self):
        self.local.start()

    def send(self):
        self.over.start()
        self.pair.start()

    def forward(self):
        self.over.wait_recv()
        self.passed.start()

    def near(self):
        if self.local is not None:
            self.local.wait()
        self.pair.wait_recv()

    def finish(self):
        self.pair.wait_send()
        self.over.wait_send()
        self.passed.wait()


class GatherX:
    def __init__(self, own, blocks, send_sem, recv_sem):
        sp, tp = lax.axis_index("sp"), lax.axis_index("tp")
        x, place = (tp // 2) % 4, (tp // 8) * 2 + tp % 2
        self.x = x
        self.blocks = blocks
        self.copies = {
            k: remote(own, blocks.at[x], send_sem.at[k], recv_sem.at[k], (sp, tp_of(place, (x + k) % 4)))
            for k in (1, 3, 2)
        }
        self.incoming = lambda k, block: remote(own, block, send_sem.at[k], recv_sem.at[k], (sp, tp))
        for copy in self.copies.values():
            copy.start()
        blocks[x] = own[...]

    def have(self, source):
        k = (self.x + 4 - source) % 4

        @pl.when(k > 0)
        def _():
            self.incoming(k, self.blocks.at[source]).wait_recv()

    def sent(self):
        for copy in self.copies.values():
            copy.wait_send()


def scatter_z(product, sent, got, cross_send, cross_recv, send_sem, recv_sem, cross_sem):
    sp, tp = lax.axis_index("sp"), lax.axis_index("tp")
    z, low = sp // 2, sp % 2
    neighbours = (((sp + 2) % 16, tp), ((sp + 14) % 16, tp))
    other = (sp + 1 - 2 * low, tp)

    def hop(way, step, r, h):
        return remote(
            sent.at[way, step, r, h],
            got.at[way, step, r, h],
            send_sem.at[way * 16 + step * 4 + r * 2 + h],
            recv_sem.at[way * 16 + step * 4 + r * 2 + h],
            neighbours[way],
        )

    def post(way, step, r, h, piece):
        sent[way, step, r, h] = piece.astype(BF)
        hop(way, step, r, h).start()

    def split(place):
        part = product(place)
        return jnp.where(low == 0, part[32:], part[:32]), jnp.where(low == 0, part[:32], part[32:])

    far = split((z + 4) % 8)
    for r in range(2):
        for way in range(2):
            post(way, 0, r, way, far[r][way * 16 : way * 16 + 16])
    for step in range(1, 4):
        parts = [split((z + 4 - step) % 8), split((z + 4 + step) % 8)]
        for r in range(2):
            for late in range(2):
                for way in range(2):
                    h = way if late else 1 - way
                    piece = parts[way][r][h * 16 : h * 16 + 16]
                    if step > 1 or late:
                        hop(way, step - 1, r, h).wait_recv()
                        piece = piece + got[way, step - 1, r, h].astype(F32)
                    post(way, step, r, h, piece)
    away, mine = split(z)

    def arrived(r):
        for late in range(2):
            for way in range(2):
                hop(way, 3, r, way if late else 1 - way).wait_recv()
        return got[0, 3, r].reshape(32, 2048).astype(F32) + got[1, 3, r].reshape(32, 2048).astype(F32)

    away = away + arrived(0)
    cross_send[...] = away.astype(BF)
    cross = remote(cross_send, cross_recv, cross_sem.at[0], cross_sem.at[1], other)
    cross.start()
    mine = mine + arrived(1)
    for way in range(2):
        for r in range(2):
            hop(way, 0, r, way).wait_send()
            for step in range(1, 4):
                for h in range(2):
                    hop(way, step, r, h).wait_send()
    cross.wait()
    return mine + cross_recv[...].astype(F32)


def gather_z(own, blocks, send_sem, recv_sem, cross_sem, beside):
    sp, tp = lax.axis_index("sp"), lax.axis_index("tp")
    z, low = sp // 2, sp % 2
    neighbours = (((sp + 2) % 16, tp), ((sp + 14) % 16, tp))
    other = (sp + 1 - 2 * low, tp)

    def hop(way, distance, place, r, h):
        block = blocks.at[place, low if r == 0 else 1 - low, pl.ds(h * 16, 16)]
        index = way * 20 + distance * 4 + r * 2 + h
        return remote(block, block, send_sem.at[index], recv_sem.at[index], neighbours[way])

    def cross(source, h):
        rows = pl.ds(h * 16, 16)
        return remote(
            own.at[rows], blocks.at[z, source, rows], cross_sem.at[2 * h], cross_sem.at[2 * h + 1], other
        )

    for h in range(2):
        cross(low, h).start()
    blocks[z, low] = own[...]
    for h in range(2):
        for way in range(2):
            hop(way, 1, z, 0, h).start()
    for h in range(2):
        cross(1 - low, h).wait_recv()
        for way in range(2):
            hop(way, 1, z, 1, h).start()
        if h == 0:
            beside[0]()
    for distance in range(1, 4):
        for r in range(2):
            for h in range(2):
                for way in range(2):
                    place = (z + (8 - distance if way == 0 else distance)) % 8
                    hop(way, distance, place, r, h).wait_recv()
                    if distance < 3 or r == way:
                        hop(way, distance + 1, place, r, h).start()
        beside[distance]()
    for way in range(2):
        for h in range(2):
            hop(way, 4, (z + 4) % 8, way, h).wait_recv()
    for h in range(2):
        cross(low, h).wait_send()
        for way in range(2):
            for distance in range(1, 4):
                for r in range(2):
                    hop(way, distance, z, r, h).wait_send()
            hop(way, 4, z, way, h).wait_send()


def block_kernel(
    offset_ref,
    queries_ref,
    keys_ref,
    values_ref,
    residual_ref,
    gain_ref,
    cache_k_ref,
    cache_v_ref,
    w_out_ref,
    w_gate_ref,
    w_up_ref,
    w_down_ref,
    out_ref,
    message,
    own_gain,
    hides,
    received,
    keys,
    own_vals,
    vals_t,
    new_keys,
    new_vals_t,
    own_queries,
    queries,
    tops,
    totals,
    sums,
    out_send,
    out_recv,
    stat_send,
    stat_recv,
    own_attended,
    attended,
    w_out,
    w_gate,
    w_up,
    w_down,
    gains,
    residuals,
    stream,
    sent_a,
    got_a,
    sent_d,
    got_d,
    cross_a,
    cross_d,
    own_squares,
    squares,
    own_scale,
    scales,
    streams,
    normed,
    x_sent,
    x_got,
    own_hidden,
    hidden,
    own_out,
    a2a_send,
    a2a_recv,
    spread_sem,
    small_sem,
    q_send,
    q_recv,
    o_send,
    o_recv,
    st_send,
    st_recv,
    aa_send,
    aa_recv,
    za_send,
    za_recv,
    sq_send,
    sq_recv,
    zn_send,
    zn_recv,
    x_send,
    x_recv,
    ah_send,
    ah_recv,
    zd_send,
    zd_recv,
    cross_sem,
    back_sem,
    sc_send,
    sc_recv,
):
    sp, tp = lax.axis_index("sp"), lax.axis_index("tp")
    high, x, core = tp // 8, (tp // 2) % 4, tp % 2
    place = high * 2 + core
    barrier = pltpu.get_barrier_semaphore()
    peers = [((sp + j) % 16, tp) for j in range(1, 16)] + [(sp, (tp + j) % 16) for j in range(1, 16)]
    for device in peers:
        pl.semaphore_signal(barrier, inc=1, device_id=device, device_id_type=MESH)
    columns = pl.ds(pl.multiple_of((sp // 2) * HD, HD), HD)
    spread_k = Spread(cache_k_ref.at[:, columns], keys, spread_sem, 0)
    spread_v = Spread(vals_t.at[place], vals_t, spread_sem, 7, local=False)
    spread_o = Spread(w_out_ref, w_out, spread_sem, 14)
    spread_g = Spread(w_gate_ref, w_gate, spread_sem, 21)
    spread_u = [
        Spread(w_up_ref.at[first : first + count], w_up, spread_sem, index, rows=pl.ds(first, count))
        for first, count, index in ((0, 256, 28), (256, 128, 35), (384, 128, 42))
    ]
    spread_d = Spread(w_down_ref, w_down, spread_sem, 49)
    load_v = pltpu.make_async_copy(cache_v_ref.at[:, columns], own_vals, small_sem.at[0])
    load_v.start()
    for spread in (spread_k, spread_o, spread_g, *spread_u, spread_d):
        spread.keep()
    for target in range(16):
        lanes = target // 2 * HD
        rows = [
            queries_ref[:, target * 512 + h * HD : target * 512 + h * HD + HD].astype(F32) for h in range(4)
        ]
        rows.append(keys_ref[:, lanes : lanes + HD].astype(F32))
        rows.append(values_ref[:, lanes : lanes + HD].astype(F32))
        message[target] = jnp.concatenate(rows, 0).astype(BF)
    own_gain[...] = jnp.broadcast_to(gain_ref[...].astype(F32).reshape(1, 512), (8, 512))
    for i in range(4):
        lane = lax.broadcasted_iota(jnp.int32, (1024, HD), 1)
        position = lax.broadcasted_iota(jnp.int32, (1024, HD), 0) + tp_of(i, x) * 1024
        hides[i] = jnp.where((lane == 0) & (position >= offset_ref[0]), LOWEST, 0.0).astype(BF)
    load_v.wait()
    for piece in range(4):
        rows = own_vals[piece * 256 : piece * 256 + 256, :].astype(F32)
        vals_t[place, :, piece * 256 : piece * 256 + 256] = rows.T.astype(BF)
    pl.semaphore_wait(barrier, len(peers))

    def exchange(j, _):
        target = (sp + j) % 16
        remote(message.at[target], received.at[sp], a2a_send.at[j], a2a_recv.at[j], (target, tp)).start()
        return 0

    lax.fori_loop(1, 16, exchange, 0)
    spread_k.send()
    spread_v.pair.start()
    received[sp] = message[sp]

    def arrived(j, _):
        block = received.at[(sp + 16 - j) % 16]
        remote(block, block, a2a_send.at[j], a2a_recv.at[j], (sp, tp)).wait()
        return 0

    lax.fori_loop(1, 16, arrived, 0)
    own_queries[...] = received[:, :32, :].reshape(4, 128, HD)
    queries[x, place] = own_queries[place]

    def ask(i, _):
        target = tp_of(i % 4, (x + i // 4) % 4)
        j = (target - tp + 16) % 16

        @pl.when(j > 0)
        def _():
            remote(own_queries.at[i % 4], queries.at[x, place], q_send.at[j], q_recv.at[j], (sp, target)).start()

        return 0

    lax.fori_loop(0, 16, ask, 0)
    spread_v.over.start()
    fresh = received[:, 32:, :].astype(F32).reshape(16, 2, 8, HD)
    new_keys[place] = fresh[:, 0].reshape(HD, HD).astype(BF)
    new_vals_t[place] = fresh[:, 1].reshape(HD, HD).T.astype(BF)

    def quad(i):
        peer = (place + i) % 4
        return (sp, tp_of(peer, x))

    def to_quad(i, kind, src, dst):
        index = 1 + kind * 6 + (i - 1) * 2
        return remote(src, dst, small_sem.at[index], small_sem.at[index + 1], quad(i))

    smalls = []
    for i in range(1, 4):
        peer = (place + i) % 4
        rows = pl.ds(pl.multiple_of(peer * 32, 32), 32)
        smalls.append(to_quad(i, 0, new_keys.at[place], new_keys.at[place]))
        smalls.append(to_quad(i, 1, new_vals_t.at[place], new_vals_t.at[place]))
        smalls.append(to_quad(i, 2, residual_ref.at[rows], residuals.at[place]))
        smalls.append(to_quad(i, 3, own_gain, gains.at[place]))
    for copy in smalls:
        copy.start()
    residuals[place] = residual_ref[pl.ds(pl.multiple_of(place * 32, 32), 32)]
    gains[place] = own_gain[...]
    spread_o.send()
    spread_k.near()
    spread_v.near()

    def attend(k, turn):
        asker = (x + 4 - k) % 4
        if turn == 0:

            @pl.when(k == 2)
            def _():
                spread_k.forward()

            for source in range(4):
                j = (tp - tp_of(source, asker) + 16) % 16

                @pl.when(j > 0)
                def _():
                    block = queries.at[asker, source]
                    remote(block, block, q_send.at[j], q_recv.at[j], (sp, tp)).wait_recv()

        q = queries[asker].reshape(512, HD)
        marked = jnp.concatenate([q, jnp.ones((512, HD), BF)], 1)
        if turn == 0:
            top = jnp.full((1, 512), LOWEST, F32)
            total = jnp.zeros((1, 512), F32)
            summed = jnp.zeros((HD, 512), F32)
        else:
            top = tops[k, 0:1, :]
            total = totals[k, 0:1, :]
            summed = sums[k]
        for chunk in range(4 + turn):
            if chunk < 4:
                held = (high + turn) % 2 * 2 + chunk // 2
                first = (chunk % 2) * 512
                block = jnp.concatenate(
                    [keys[held, first : first + 512, :], hides[held, first : first + 512, :]], 1
                )
                block_t = vals_t[held, :, first : first + 512]
            else:
                block = new_keys[...].reshape(512, HD)
                block_t = jnp.concatenate([new_vals_t[i] for i in range(4)], 1)
            scores = lax.dot_general(
                block, marked if chunk < 4 else q, (((1,), (1,)), ((), ())), preferred_element_type=F32
            )
            if chunk == 4:
                lane = lax.broadcasted_iota(jnp.int32, (128, 512), 1)
                token = ((lane // 256) * 4 + asker) * 256 + ((lane // 128) % 2) * 128
                token = token + place * 32 + ((lane // 32) % 4) * 8 + lane % 8
                ahead = lax.broadcasted_iota(jnp.int32, (128, 512), 0) - token
                scores = jnp.concatenate(
                    [
                        jnp.where(ahead <= -tp_of(i, x) * 128, scores[i * 128 : i * 128 + 128], LOWEST)
                        for i in range(4)
                    ],
                    0,
                )
            higher = jnp.maximum(top, jnp.max(scores, axis=0, keepdims=True))
            weights = jnp.exp2((scores - higher) * SCORE_SCALE)
            factor = jnp.exp2((top - higher) * SCORE_SCALE)
            total = total * factor + jnp.sum(weights, axis=0, keepdims=True)
            summed = summed * factor + jnp.dot(block_t, weights.astype(BF), preferred_element_type=F32)
            top = higher
        if turn == 0:
            tops[k] = jnp.broadcast_to(top, (8, 512))
            totals[k] = jnp.broadcast_to(total, (8, 512))
            sums[k] = summed
            return
        out_send[k] = summed.astype(BF)
        stat_send[k] = jnp.concatenate([jnp.broadcast_to(top, (4, 512)), jnp.broadcast_to(total, (4, 512))], 0)

        @pl.when(k > 0)
        def _():
            target = (sp, tp_of(place, asker))
            remote(out_send.at[k], out_recv.at[k], o_send.at[k], o_recv.at[k], target).start()
            remote(stat_send.at[k], stat_recv.at[k], st_send.at[k], st_recv.at[k], target).start()

    def attend_near(k, _):
        attend(k, 0)
        return 0

    def attend_far(k, _):
        attend((k + 1) % 4, 1)
        return 0

    lax.fori_loop(0, 4, attend_near, 0)
    spread_v.forward()
    spread_g.send()
    spread_k.finish()
    spread_v.finish()
    for copy in smalls:
        copy.wait()
    lax.fori_loop(0, 4, attend_far, 0)
    spread_u[0].send()

    def asked(j, _):
        remote(own_queries.at[0], queries.at[x, place], q_send.at[j], q_recv.at[j], (sp, tp)).wait_send()
        return 0

    lax.fori_loop(1, 16, asked, 0)

    def collect(k, _):
        remote(out_send.at[k], out_recv.at[k], o_send.at[k], o_recv.at[k], (sp, tp)).wait()
        remote(stat_send.at[k], stat_recv.at[k], st_send.at[k], st_recv.at[k], (sp, tp)).wait()
        return 0

    lax.fori_loop(1, 4, collect, 0)
    tops = [stat_send[0, 0:1, :]] + [stat_recv[k, 0:1, :] for k in range(1, 4)]
    highest = functools.reduce(jnp.maximum, tops)
    shares = [jnp.exp2((top - highest) * SCORE_SCALE) for top in tops]
    total = stat_send[0, 4:5, :] * shares[0]
    summed = out_send[0].astype(F32) * shares[0]
    for k in range(1, 4):
        total = total + stat_recv[k, 4:5, :] * shares[k]
        summed = summed + out_recv[k].astype(F32) * shares[k]
    mixed = (summed / total).T.reshape(16, 4, 8, HD)
    for h in range(4):
        own_attended[:, :, h * HD : (h + 1) * HD] = mixed[:, h].reshape(2, 64, HD).astype(BF)
    whole = GatherX(own_attended, attended, aa_send, aa_recv)
    spread_o.forward()
    spread_o.near()
    spread_o.finish()

    awaited = [0, 0]

    def project(target):
        if awaited[0] < 4:
            whole.have(target % 4)
            awaited[0] += 1
        rows = attended[target % 4, target // 4]
        return jnp.concatenate(
            [jnp.dot(rows, w_out[i], preferred_element_type=F32) for i in range(4)], 1
        )

    attn_out = scatter_z(
        project,
        sent_a,
        got_a,
        cross_a.at[0],
        cross_a.at[1],
        za_send,
        za_recv,
        cross_sem.at[pl.ds(0, 2)],
    )
    whole.sent()
    spread_g.forward()
    spread_u[0].forward()
    own_residual = jnp.concatenate([residuals[i] for i in range(4)], 1)
    stream[...] = (own_residual.astype(F32) + attn_out).astype(BF)
    wide = stream[...].astype(F32)
    own_squares[...] = jnp.broadcast_to(jnp.sum(wide * wide, axis=1, keepdims=True), (32, 128))
    tells = [
        remote(own_squares, squares.at[k], sq_send.at[k], sq_recv.at[k], (sp, tp_of(place, (x + k) % 4)))
        for k in range(1, 4)
    ]
    for copy in tells:
        copy.start()
    z = sp // 2

    def send_rest():
        spread_u[1].send()
        for copy in tells:
            copy.wait()
        mean = (own_squares[...] + squares[1] + squares[2] + squares[3]) / D
        own_scale[...] = jnp.concatenate([lax.rsqrt(mean + EPS)] * 4, 0).T[:8]
        scales[sp] = own_scale[...]

        def tell_scale(j, _):
            device = ((sp + j) % 16, tp)
            remote(own_scale, scales.at[sp], sc_send.at[j], sc_recv.at[j], device).start()
            return 0

        lax.fori_loop(1, 16, tell_scale, 0)
        spread_u[2].send()
        spread_d.send()

    def normalise(turn, members):
        gain = jnp.concatenate([gains[i, 0:1, :] for i in range(4)], 1)

        for member in members:
            source = (z + 7 + member + 4 * turn) % 8
            for b in range(2):
                scale = jnp.broadcast_to(scales[source * 2 + b, 0:1, :], (128, 128)).T[:32]
                scale = jnp.concatenate([scale] * 16, 1)
                normed[source, b] = (streams[source, b].astype(F32) * scale * gain).astype(BF)

    def start_gate():
        spread_u[1].forward()
        spread_g.near()
        spread_g.finish()

        def told_scale(j, _):
            block = scales.at[(sp + 16 - j) % 16]
            remote(own_scale, block, sc_send.at[j], sc_recv.at[j], (sp, tp)).wait()
            return 0

        lax.fori_loop(1, 16, told_scale, 0)
        normalise(0, (0, 1, 2, 3))
        open_gate(0)

    def start_up():
        pass_gate(0)
        spread_u[2].forward()
        for spread in spread_u:
            spread.near()
            spread.finish()
        open_up(0)
        normalise(1, (3, 0, 2))

    def part(turn, column, up):
        rows = normed[(z + 7 + (x + column) % 4 + 4 * turn) % 8].reshape(64, 2048)
        weight = w_up if up else w_gate
        return jnp.dot(rows, weight[...].reshape(2048, 1024), preferred_element_type=F32)

    neighbours = ((sp, tp_of(place, (x + 1) % 4)), (sp, tp_of(place, (x + 3) % 4)))

    def hop(turn, which):
        index = turn * 6 + which
        return remote(
            x_sent.at[index], x_got.at[index], x_send.at[index], x_recv.at[index], neighbours[which // 3]
        )

    def post(turn, which, value):
        x_sent[turn * 6 + which] = value.astype(BF)
        hop(turn, which).start()

    def came(turn, which):
        hop(turn, which).wait_recv()
        return x_got[turn * 6 + which].astype(F32)

    def open_gate(turn):
        post(turn, 0, part(turn, 2, False))
        post(turn, 5, part(turn, 3, False))

    def open_up(turn):
        post(turn, 3, part(turn, 2, True))
        post(turn, 2, part(turn, 1, True))

    def pass_gate(turn):
        second = part(turn, 1, False)
        post(turn, 1, second + came(turn, 0))

    def pass_up(turn):
        second = part(turn, 3, True)
        post(turn, 4, second + came(turn, 3))

    def close_turn(turn):
        gate = part(turn, 0, False)
        up = part(turn, 0, True)
        gate = gate + came(turn, 5) + came(turn, 1)
        up = up + came(turn, 2) + came(turn, 4)
        own_hidden[turn] = (gate / (1.0 + jnp.exp(-gate)) * up).astype(BF)
        return GatherX(
            own_hidden.at[turn], hidden.at[turn], ah_send.at[pl.ds(4 * turn, 4)], ah_recv.at[pl.ds(4 * turn, 4)]
        )

    gather_z(
        stream,
        streams,
        zn_send,
        zn_recv,
        cross_sem.at[pl.ds(4, 4)],
        {0: send_rest, 1: lambda: None, 2: start_gate, 3: start_up},
    )
    normalise(1, (1,))
    open_gate(1)
    open_up(1)
    pass_up(0)
    pass_gate(1)
    pass_up(1)
    first_half = close_turn(0)
    second_half = close_turn(1)
    spread_d.forward()
    spread_d.near()
    spread_d.finish()
    for turn in range(2):
        for which in range(6):
            hop(turn, which).wait_send()

    def down(target):
        offset = (5, 4, 6, 3, 7, 2, 0, 1)[awaited[1]]
        awaited[1] += 1
        (first_half, second_half)[offset // 4].have(offset % 4)
        rows = hidden[offset // 4, offset % 4]
        return jnp.concatenate(
            [jnp.dot(rows, w_down[i], preferred_element_type=F32) for i in range(4)], 1
        )

    added = scatter_z(
        down, sent_d, got_d, cross_d.at[0], cross_d.at[1], zd_send, zd_recv, cross_sem.at[pl.ds(2, 2)]
    )
    first_half.sent()
    second_half.sent()
    result = (stream[...].astype(F32) + added).astype(BF)
    for i in range(4):
        own_out[i] = result[:, i * 512 : i * 512 + 512]
    mine = pl.ds(pl.multiple_of(place * 32, 32), 32)
    backs = [
        remote(own_out.at[(place + i) % 4], out_ref.at[mine], back_sem.at[2 * i], back_sem.at[2 * i + 1], quad(i))
        for i in range(1, 4)
    ]
    for copy in backs:
        copy.start()
    out_ref[mine] = own_out[place]
    for copy in backs:
        copy.wait()


def run_block(offset, queries, keys, values, residual, gain, cache_keys, cache_values, w_out, w_gate, w_up, w_down):
    hop = VM((2, 4, 2, 2, 16, 2048), BF)
    vmem = pl.BlockSpec(memory_space=pltpu.VMEM)
    return pl.pallas_call(
        block_kernel,
        out_shape=jax.ShapeDtypeStruct((128, 512), BF),
        in_specs=[pl.BlockSpec(memory_space=pltpu.SMEM)] + [vmem] * 5 + [pl.BlockSpec(memory_space=pl.ANY)] * 6,
        out_specs=vmem,
        scratch_shapes=[
            VM((16, 48, HD), BF),
            VM((8, 512), F32),
            VM((4, 1024, HD), BF),
            VM((16, 48, HD), BF),
            VM((4, 1024, HD), BF),
            VM((1024, HD), BF),
            VM((4, HD, 1024), BF),
            VM((4, 128, HD), BF),
            VM((4, HD, 128), BF),
            VM((4, 128, HD), BF),
            VM((4, 4, 128, HD), BF),
            VM((4, 8, 512), F32),
            VM((4, 8, 512), F32),
            VM((4, HD, 512), F32),
            VM((4, HD, 512), BF),
            VM((4, HD, 512), BF),
            VM((4, 8, 512), F32),
            VM((4, 8, 512), F32),
            VM((2, 64, 512), BF),
            VM((4, 2, 64, 512), BF),
            VM((4, 512, 512), BF),
            VM((4, 512, 1024), BF),
            VM((4, 512, 1024), BF),
            VM((4, 1024, 512), BF),
            VM((4, 8, 512), F32),
            VM((4, 32, 512), BF),
            VM((32, 2048), BF),
            hop,
            hop,
            hop,
            hop,
            VM((2, 32, 2048), BF),
            VM((2, 32, 2048), BF),
            VM((32, 128), F32),
            VM((4, 32, 128), F32),
            VM((8, 128), F32),
            VM((16, 8, 128), F32),
            VM((8, 2, 32, 2048), BF),
            VM((8, 2, 32, 2048), BF),
            VM((12, 64, 1024), BF),
            VM((12, 64, 1024), BF),
            VM((2, 64, 1024), BF),
            VM((2, 4, 64, 1024), BF),
            VM((4, 32, 512), BF),
        ]
        + [DMA((16,))] * 2
        + [DMA((56,)), DMA((25,))]
        + [DMA((16,))] * 2
        + [DMA((4,))] * 6
        + [DMA((32,))] * 2
        + [DMA((4,))] * 2
        + [DMA((40,))] * 2
        + [DMA((12,))] * 2
        + [DMA((8,))] * 2
        + [DMA((32,))] * 2
        + [DMA((8,)), DMA((8,)), DMA((16,)), DMA((16,))],
        compiler_params=pltpu.CompilerParams(
            collective_id=0, has_side_effects=True, vmem_limit_bytes=VMEM_LIMIT
        ),
        name="block",
    )(offset, queries, keys, values, residual, gain, cache_keys, cache_values, w_out, w_gate, w_up, w_down)


def per_device(
    residual,
    queries,
    keys,
    values,
    cache_keys,
    cache_values,
    offset,
    w_out,
    norm_gain,
    w_gate,
    w_up,
    w_down,
):
    return run_block(
        offset,
        queries,
        keys,
        values,
        residual,
        norm_gain,
        cache_keys,
        cache_values,
        w_out,
        w_gate,
        w_up,
        w_down,
    )


def solution(mesh):
    in_specs = (
        P("sp", "tp"),
        P(("tp", "sp"), None),
        P(("tp", "sp"), None),
        P(("tp", "sp"), None),
        P("tp", None),
        P("tp", None),
        P(),
        P("sp", "tp"),
        P("tp"),
        P("tp", "sp"),
        P("tp", "sp"),
        P("sp", "tp"),
    )
    out_specs = P("sp", "tp")
    return jax.shard_map(
        per_device, mesh=mesh, in_specs=in_specs, out_specs=out_specs, check_vma=False
    )
```

```python
import functools

import jax
import jax.numpy as jnp
from jax import lax
from jax.experimental import pallas as pl
from jax.experimental.pallas import tpu as pltpu
from jax.sharding import PartitionSpec as P

D = 8192
H = 64
KV = 8
HD = 128
EPS = 1e-6
BF = jnp.bfloat16
F32 = jnp.float32
MESH = pl.DeviceIdType.MESH
VM = pltpu.VMEM
DMA = pltpu.SemaphoreType.DMA
SCORE_SCALE = 1.4426950408889634 / HD**0.5
LOWEST = -1e30
VMEM_LIMIT = 56 * 2**20


def remote(src, dst, send, recv, device):
    return pltpu.make_async_remote_copy(
        src_ref=src,
        dst_ref=dst,
        send_sem=send,
        recv_sem=recv,
        device_id=device,
        device_id_type=MESH,
    )


def tp_of(place, x):
    return ((place // 2) * 4 + x) * 2 + place % 2


class Spread:
    def __init__(self, source, buffer, sems, first, local=True, rows=None):
        sp, tp = lax.axis_index("sp"), lax.axis_index("tp")
        high, x, core = tp // 8, (tp // 2) % 4, tp % 2
        self.sibling = (sp, tp + 1 - 2 * core)
        opposite = (sp, (tp + 8) % 16)
        at = (lambda i: buffer.at[i]) if rows is None else (lambda i: buffer.at[i, rows])
        mine = at(high * 2 + core)
        self.local = pltpu.make_async_copy(source, mine, sems.at[first]) if local else None
        self.pair = remote(source, mine, sems.at[first + 1], sems.at[first + 2], self.sibling)
        self.over = remote(source, mine, sems.at[first + 3], sems.at[first + 4], opposite)
        across = at((1 - high) * 2 + core)
        self.passed = remote(across, across, sems.at[first + 5], sems.at[first + 6], self.sibling)

    def keep(self):
        self.local.start()

    def send(self):
        self.over.start()
        self.pair.start()

    def forward(self):
        self.over.wait_recv()
        self.passed.start()

    def near(self):
        if self.local is not None:
            self.local.wait()
        self.pair.wait_recv()

    def finish(self):
        self.pair.wait_send()
        self.over.wait_send()
        self.passed.wait()


class GatherX:
    def __init__(self, own, blocks, send_sem, recv_sem):
        sp, tp = lax.axis_index("sp"), lax.axis_index("tp")
        x, place = (tp // 2) % 4, (tp // 8) * 2 + tp % 2
        self.x = x
        self.blocks = blocks
        self.copies = {
            k: remote(own, blocks.at[x], send_sem.at[k], recv_sem.at[k], (sp, tp_of(place, (x + k) % 4)))
            for k in (1, 3, 2)
        }
        self.incoming = lambda k, block: remote(own, block, send_sem.at[k], recv_sem.at[k], (sp, tp))
        for copy in self.copies.values():
            copy.start()
        blocks[x] = own[...]

    def have(self, source):
        k = (self.x + 4 - source) % 4

        @pl.when(k > 0)
        def _():
            self.incoming(k, self.blocks.at[source]).wait_recv()

    def sent(self):
        for copy in self.copies.values():
            copy.wait_send()


def scatter_z(product, sent, got, cross_send, cross_recv, send_sem, recv_sem, cross_sem):
    sp, tp = lax.axis_index("sp"), lax.axis_index("tp")
    z, low = sp // 2, sp % 2
    neighbours = (((sp + 2) % 16, tp), ((sp + 14) % 16, tp))
    other = (sp + 1 - 2 * low, tp)

    def hop(way, step, r, h):
        return remote(
            sent.at[way, step, r, h],
            got.at[way, step, r, h],
            send_sem.at[way * 16 + step * 4 + r * 2 + h],
            recv_sem.at[way * 16 + step * 4 + r * 2 + h],
            neighbours[way],
        )

    def post(way, step, r, h, piece):
        sent[way, step, r, h] = piece.astype(BF)
        hop(way, step, r, h).start()

    def split(place):
        part = product(place)
        return jnp.where(low == 0, part[32:], part[:32]), jnp.where(low == 0, part[:32], part[32:])

    far = split((z + 4) % 8)
    for r in range(2):
        for way in range(2):
            post(way, 0, r, way, far[r][way * 16 : way * 16 + 16])
    for step in range(1, 4):
        parts = [split((z + 4 - step) % 8), split((z + 4 + step) % 8)]
        for r in range(2):
            for late in range(2):
                for way in range(2):
                    h = way if late else 1 - way
                    piece = parts[way][r][h * 16 : h * 16 + 16]
                    if step > 1 or late:
                        hop(way, step - 1, r, h).wait_recv()
                        piece = piece + got[way, step - 1, r, h].astype(F32)
                    post(way, step, r, h, piece)
    away, mine = split(z)

    def arrived(r):
        for late in range(2):
            for way in range(2):
                hop(way, 3, r, way if late else 1 - way).wait_recv()
        return got[0, 3, r].reshape(32, 2048).astype(F32) + got[1, 3, r].reshape(32, 2048).astype(F32)

    away = away + arrived(0)
    cross_send[...] = away.astype(BF)
    cross = remote(cross_send, cross_recv, cross_sem.at[0], cross_sem.at[1], other)
    cross.start()
    mine = mine + arrived(1)
    for way in range(2):
        for r in range(2):
            hop(way, 0, r, way).wait_send()
            for step in range(1, 4):
                for h in range(2):
                    hop(way, step, r, h).wait_send()
    cross.wait()
    return mine + cross_recv[...].astype(F32)


def gather_z(own, blocks, send_sem, recv_sem, cross_sem, beside):
    sp, tp = lax.axis_index("sp"), lax.axis_index("tp")
    z, low = sp // 2, sp % 2
    neighbours = (((sp + 2) % 16, tp), ((sp + 14) % 16, tp))
    other = (sp + 1 - 2 * low, tp)

    def hop(way, distance, place, r, h):
        block = blocks.at[place, low if r == 0 else 1 - low, pl.ds(h * 16, 16)]
        index = way * 20 + distance * 4 + r * 2 + h
        return remote(block, block, send_sem.at[index], recv_sem.at[index], neighbours[way])

    def cross(source, h):
        rows = pl.ds(h * 16, 16)
        return remote(
            own.at[rows], blocks.at[z, source, rows], cross_sem.at[2 * h], cross_sem.at[2 * h + 1], other
        )

    for h in range(2):
        cross(low, h).start()
    blocks[z, low] = own[...]
    for h in range(2):
        for way in range(2):
            hop(way, 1, z, 0, h).start()
    for h in range(2):
        cross(1 - low, h).wait_recv()
        for way in range(2):
            hop(way, 1, z, 1, h).start()
        if h == 0:
            beside[0]()
    for distance in range(1, 4):
        for r in range(2):
            for h in range(2):
                for way in range(2):
                    place = (z + (8 - distance if way == 0 else distance)) % 8
                    hop(way, distance, place, r, h).wait_recv()
                    if distance < 3 or r == way:
                        hop(way, distance + 1, place, r, h).start()
        beside[distance]()
    for way in range(2):
        for h in range(2):
            hop(way, 4, (z + 4) % 8, way, h).wait_recv()
    for h in range(2):
        cross(low, h).wait_send()
        for way in range(2):
            for distance in range(1, 4):
                for r in range(2):
                    hop(way, distance, z, r, h).wait_send()
            hop(way, 4, z, way, h).wait_send()


def block_kernel(
    offset_ref,
    queries_ref,
    keys_ref,
    values_ref,
    residual_ref,
    gain_ref,
    cache_k_ref,
    cache_v_ref,
    w_out_ref,
    w_gate_ref,
    w_up_ref,
    w_down_ref,
    out_ref,
    message,
    own_gain,
    hides,
    received,
    keys,
    own_vals,
    vals_t,
    new_keys,
    new_vals_t,
    own_queries,
    queries,
    tops,
    totals,
    sums,
    out_send,
    out_recv,
    stat_send,
    stat_recv,
    own_attended,
    attended,
    w_out,
    w_gate,
    w_up,
    w_down,
    gains,
    residuals,
    stream,
    sent_a,
    got_a,
    sent_d,
    got_d,
    cross_a,
    cross_d,
    own_squares,
    squares,
    own_scale,
    scales,
    streams,
    normed,
    x_sent,
    x_got,
    own_hidden,
    hidden,
    own_out,
    a2a_send,
    a2a_recv,
    spread_sem,
    small_sem,
    q_send,
    q_recv,
    o_send,
    o_recv,
    st_send,
    st_recv,
    aa_send,
    aa_recv,
    za_send,
    za_recv,
    sq_send,
    sq_recv,
    zn_send,
    zn_recv,
    x_send,
    x_recv,
    ah_send,
    ah_recv,
    zd_send,
    zd_recv,
    cross_sem,
    back_sem,
    sc_send,
    sc_recv,
):
    sp, tp = lax.axis_index("sp"), lax.axis_index("tp")
    high, x, core = tp // 8, (tp // 2) % 4, tp % 2
    place = high * 2 + core
    barrier = pltpu.get_barrier_semaphore()
    peers = [((sp + j) % 16, tp) for j in range(1, 16)] + [(sp, (tp + j) % 16) for j in range(1, 16)]
    for device in peers:
        pl.semaphore_signal(barrier, inc=1, device_id=device, device_id_type=MESH)
    columns = pl.ds(pl.multiple_of((sp // 2) * HD, HD), HD)
    spread_k = Spread(cache_k_ref.at[:, columns], keys, spread_sem, 0)
    spread_v = Spread(vals_t.at[place], vals_t, spread_sem, 7, local=False)
    spread_o = Spread(w_out_ref, w_out, spread_sem, 14)
    spread_g = Spread(w_gate_ref, w_gate, spread_sem, 21)
    spread_u = [
        Spread(w_up_ref.at[first : first + count], w_up, spread_sem, index, rows=pl.ds(first, count))
        for first, count, index in ((0, 256, 28), (256, 128, 35), (384, 128, 42))
    ]
    spread_d = Spread(w_down_ref, w_down, spread_sem, 49)
    load_v = pltpu.make_async_copy(cache_v_ref.at[:, columns], own_vals, small_sem.at[0])
    load_v.start()
    for spread in (spread_k, spread_o, spread_g, *spread_u, spread_d):
        spread.keep()
    for target in range(16):
        lanes = target // 2 * HD
        rows = [
            queries_ref[:, target * 512 + h * HD : target * 512 + h * HD + HD].astype(F32) for h in range(4)
        ]
        rows.append(keys_ref[:, lanes : lanes + HD].astype(F32))
        rows.append(values_ref[:, lanes : lanes + HD].astype(F32))
        message[target] = jnp.concatenate(rows, 0).astype(BF)
    own_gain[...] = jnp.broadcast_to(gain_ref[...].astype(F32).reshape(1, 512), (8, 512))
    for i in range(4):
        lane = lax.broadcasted_iota(jnp.int32, (1024, HD), 1)
        position = lax.broadcasted_iota(jnp.int32, (1024, HD), 0) + tp_of(i, x) * 1024
        hides[i] = jnp.where((lane == 0) & (position >= offset_ref[0]), LOWEST, 0.0).astype(BF)
    load_v.wait()
    for piece in range(4):
        rows = own_vals[piece * 256 : piece * 256 + 256, :].astype(F32)
        vals_t[place, :, piece * 256 : piece * 256 + 256] = rows.T.astype(BF)
    pl.semaphore_wait(barrier, len(peers))

    def exchange(j, _):
        target = (sp + j) % 16
        remote(message.at[target], received.at[sp], a2a_send.at[j], a2a_recv.at[j], (target, tp)).start()
        return 0

    lax.fori_loop(1, 16, exchange, 0)
    spread_k.send()
    spread_v.pair.start()
    received[sp] = message[sp]

    def arrived(j, _):
        block = received.at[(sp + 16 - j) % 16]
        remote(block, block, a2a_send.at[j], a2a_recv.at[j], (sp, tp)).wait()
        return 0

    lax.fori_loop(1, 16, arrived, 0)
    own_queries[...] = received[:, :32, :].reshape(4, 128, HD)
    queries[x, place] = own_queries[place]

    def ask(i, _):
        target = tp_of(i % 4, (x + i // 4) % 4)
        j = (target - tp + 16) % 16

        @pl.when(j > 0)
        def _():
            remote(own_queries.at[i % 4], queries.at[x, place], q_send.at[j], q_recv.at[j], (sp, target)).start()

        return 0

    lax.fori_loop(0, 16, ask, 0)
    spread_v.over.start()
    fresh = received[:, 32:, :].astype(F32).reshape(16, 2, 8, HD)
    new_keys[place] = fresh[:, 0].reshape(HD, HD).astype(BF)
    new_vals_t[place] = fresh[:, 1].reshape(HD, HD).T.astype(BF)

    def quad(i):
        peer = (place + i) % 4
        return (sp, tp_of(peer, x))

    def to_quad(i, kind, src, dst):
        index = 1 + kind * 6 + (i - 1) * 2
        return remote(src, dst, small_sem.at[index], small_sem.at[index + 1], quad(i))

    smalls = []
    for i in range(1, 4):
        peer = (place + i) % 4
        rows = pl.ds(pl.multiple_of(peer * 32, 32), 32)
        smalls.append(to_quad(i, 0, new_keys.at[place], new_keys.at[place]))
        smalls.append(to_quad(i, 1, new_vals_t.at[place], new_vals_t.at[place]))
        smalls.append(to_quad(i, 2, residual_ref.at[rows], residuals.at[place]))
        smalls.append(to_quad(i, 3, own_gain, gains.at[place]))
    for copy in smalls:
        copy.start()
    residuals[place] = residual_ref[pl.ds(pl.multiple_of(place * 32, 32), 32)]
    gains[place] = own_gain[...]
    spread_o.send()
    spread_k.near()
    spread_v.near()

    def attend(k, turn):
        asker = (x + 4 - k) % 4
        if turn == 0:

            @pl.when(k == 2)
            def _():
                spread_k.forward()

            for source in range(4):
                j = (tp - tp_of(source, asker) + 16) % 16

                @pl.when(j > 0)
                def _():
                    block = queries.at[asker, source]
                    remote(block, block, q_send.at[j], q_recv.at[j], (sp, tp)).wait_recv()

        q = queries[asker].reshape(512, HD)
        marked = jnp.concatenate([q, jnp.ones((512, HD), BF)], 1)
        if turn == 0:
            top = jnp.full((1, 512), LOWEST, F32)
            total = jnp.zeros((1, 512), F32)
            summed = jnp.zeros((HD, 512), F32)
        else:
            top = tops[k, 0:1, :]
            total = totals[k, 0:1, :]
            summed = sums[k]
        for chunk in range(4 + turn):
            if chunk < 4:
                held = (high + turn) % 2 * 2 + chunk // 2
                first = (chunk % 2) * 512
                block = jnp.concatenate(
                    [keys[held, first : first + 512, :], hides[held, first : first + 512, :]], 1
                )
                block_t = vals_t[held, :, first : first + 512]
            else:
                block = new_keys[...].reshape(512, HD)
                block_t = jnp.concatenate([new_vals_t[i] for i in range(4)], 1)
            scores = lax.dot_general(
                block, marked if chunk < 4 else q, (((1,), (1,)), ((), ())), preferred_element_type=F32
            )
            if chunk == 4:
                lane = lax.broadcasted_iota(jnp.int32, (128, 512), 1)
                token = ((lane // 256) * 4 + asker) * 256 + ((lane // 128) % 2) * 128
                token = token + place * 32 + ((lane // 32) % 4) * 8 + lane % 8
                ahead = lax.broadcasted_iota(jnp.int32, (128, 512), 0) - token
                scores = jnp.concatenate(
                    [
                        jnp.where(ahead <= -tp_of(i, x) * 128, scores[i * 128 : i * 128 + 128], LOWEST)
                        for i in range(4)
                    ],
                    0,
                )
            higher = jnp.maximum(top, jnp.max(scores, axis=0, keepdims=True))
            weights = jnp.exp2((scores - higher) * SCORE_SCALE)
            factor = jnp.exp2((top - higher) * SCORE_SCALE)
            total = total * factor + jnp.sum(weights, axis=0, keepdims=True)
            summed = summed * factor + jnp.dot(block_t, weights.astype(BF), preferred_element_type=F32)
            top = higher
        if turn == 0:
            tops[k] = jnp.broadcast_to(top, (8, 512))
            totals[k] = jnp.broadcast_to(total, (8, 512))
            sums[k] = summed
            return
        out_send[k] = summed.astype(BF)
        stat_send[k] = jnp.concatenate([jnp.broadcast_to(top, (4, 512)), jnp.broadcast_to(total, (4, 512))], 0)

        @pl.when(k > 0)
        def _():
            target = (sp, tp_of(place, asker))
            remote(out_send.at[k], out_recv.at[k], o_send.at[k], o_recv.at[k], target).start()
            remote(stat_send.at[k], stat_recv.at[k], st_send.at[k], st_recv.at[k], target).start()

    def attend_near(k, _):
        attend(k, 0)
        return 0

    def attend_far(k, _):
        attend((k + 1) % 4, 1)
        return 0

    lax.fori_loop(0, 4, attend_near, 0)
    spread_v.forward()
    spread_g.send()
    spread_k.finish()
    spread_v.finish()
    for copy in smalls:
        copy.wait()
    lax.fori_loop(0, 4, attend_far, 0)
    spread_u[0].send()

    def asked(j, _):
        remote(own_queries.at[0], queries.at[x, place], q_send.at[j], q_recv.at[j], (sp, tp)).wait_send()
        return 0

    lax.fori_loop(1, 16, asked, 0)

    def collect(k, _):
        remote(out_send.at[k], out_recv.at[k], o_send.at[k], o_recv.at[k], (sp, tp)).wait()
        remote(stat_send.at[k], stat_recv.at[k], st_send.at[k], st_recv.at[k], (sp, tp)).wait()
        return 0

    lax.fori_loop(1, 4, collect, 0)
    tops = [stat_send[0, 0:1, :]] + [stat_recv[k, 0:1, :] for k in range(1, 4)]
    highest = functools.reduce(jnp.maximum, tops)
    shares = [jnp.exp2((top - highest) * SCORE_SCALE) for top in tops]
    total = stat_send[0, 4:5, :] * shares[0]
    summed = out_send[0].astype(F32) * shares[0]
    for k in range(1, 4):
        total = total + stat_recv[k, 4:5, :] * shares[k]
        summed = summed + out_recv[k].astype(F32) * shares[k]
    mixed = (summed / total).T.reshape(16, 4, 8, HD)
    for h in range(4):
        own_attended[:, :, h * HD : (h + 1) * HD] = mixed[:, h].reshape(2, 64, HD).astype(BF)
    whole = GatherX(own_attended, attended, aa_send, aa_recv)
    spread_o.forward()
    spread_o.near()
    spread_o.finish()

    awaited = [0, 0]

    def project(target):
        if awaited[0] < 4:
            whole.have(target % 4)
            awaited[0] += 1
        rows = attended[target % 4, target // 4]
        return jnp.concatenate(
            [jnp.dot(rows, w_out[i], preferred_element_type=F32) for i in range(4)], 1
        )

    attn_out = scatter_z(
        project,
        sent_a,
        got_a,
        cross_a.at[0],
        cross_a.at[1],
        za_send,
        za_recv,
        cross_sem.at[pl.ds(0, 2)],
    )
    whole.sent()
    spread_g.forward()
    spread_u[0].forward()
    own_residual = jnp.concatenate([residuals[i] for i in range(4)], 1)
    stream[...] = (own_residual.astype(F32) + attn_out).astype(BF)
    wide = stream[...].astype(F32)
    own_squares[...] = jnp.broadcast_to(jnp.sum(wide * wide, axis=1, keepdims=True), (32, 128))
    tells = [
        remote(own_squares, squares.at[k], sq_send.at[k], sq_recv.at[k], (sp, tp_of(place, (x + k) % 4)))
        for k in range(1, 4)
    ]
    for copy in tells:
        copy.start()
    z = sp // 2

    def send_rest():
        spread_u[1].send()
        for copy in tells:
            copy.wait()
        mean = (own_squares[...] + squares[1] + squares[2] + squares[3]) / D
        own_scale[...] = jnp.concatenate([lax.rsqrt(mean + EPS)] * 4, 0).T[:8]
        scales[sp] = own_scale[...]

        def tell_scale(j, _):
            device = ((sp + j) % 16, tp)
            remote(own_scale, scales.at[sp], sc_send.at[j], sc_recv.at[j], device).start()
            return 0

        lax.fori_loop(1, 16, tell_scale, 0)
        spread_u[2].send()
        spread_d.send()

    def normalise(turn, members):
        gain = jnp.concatenate([gains[i, 0:1, :] for i in range(4)], 1)

        for member in members:
            source = (z + 7 + member + 4 * turn) % 8
            for b in range(2):
                scale = jnp.broadcast_to(scales[source * 2 + b, 0:1, :], (128, 128)).T[:32]
                scale = jnp.concatenate([scale] * 16, 1)
                normed[source, b] = (streams[source, b].astype(F32) * scale * gain).astype(BF)

    def have_scales():
        spread_u[1].forward()
        spread_g.near()
        spread_g.finish()

        def told_scale(j, _):
            block = scales.at[(sp + 16 - j) % 16]
            remote(own_scale, block, sc_send.at[j], sc_recv.at[j], (sp, tp)).wait()
            return 0

        lax.fori_loop(1, 16, told_scale, 0)
        normalise(0, (1, 0, 2))

    def start_gate():
        normalise(0, (3,))
        open_gate(0)

    def start_up():
        pass_gate(0)
        spread_u[2].forward()
        for spread in spread_u:
            spread.near()
            spread.finish()
        open_up(0)
        normalise(1, (3, 0, 2))

    def part(turn, column, up):
        rows = normed[(z + 7 + (x + column) % 4 + 4 * turn) % 8].reshape(64, 2048)
        weight = w_up if up else w_gate
        return jnp.dot(rows, weight[...].reshape(2048, 1024), preferred_element_type=F32)

    neighbours = ((sp, tp_of(place, (x + 1) % 4)), (sp, tp_of(place, (x + 3) % 4)))

    def hop(turn, which):
        index = turn * 6 + which
        return remote(
            x_sent.at[index], x_got.at[index], x_send.at[index], x_recv.at[index], neighbours[which // 3]
        )

    def post(turn, which, value):
        x_sent[turn * 6 + which] = value.astype(BF)
        hop(turn, which).start()

    def came(turn, which):
        hop(turn, which).wait_recv()
        return x_got[turn * 6 + which].astype(F32)

    def open_gate(turn):
        post(turn, 0, part(turn, 2, False))
        post(turn, 5, part(turn, 3, False))

    def open_up(turn):
        post(turn, 3, part(turn, 2, True))
        post(turn, 2, part(turn, 1, True))

    def pass_gate(turn):
        second = part(turn, 1, False)
        post(turn, 1, second + came(turn, 0))

    def pass_up(turn):
        second = part(turn, 3, True)
        post(turn, 4, second + came(turn, 3))

    def close_turn(turn):
        gate = part(turn, 0, False)
        up = part(turn, 0, True)
        gate = gate + came(turn, 5) + came(turn, 1)
        up = up + came(turn, 2) + came(turn, 4)
        own_hidden[turn] = (gate / (1.0 + jnp.exp(-gate)) * up).astype(BF)
        return GatherX(
            own_hidden.at[turn], hidden.at[turn], ah_send.at[pl.ds(4 * turn, 4)], ah_recv.at[pl.ds(4 * turn, 4)]
        )

    gather_z(
        stream,
        streams,
        zn_send,
        zn_recv,
        cross_sem.at[pl.ds(4, 4)],
        {0: send_rest, 1: have_scales, 2: start_gate, 3: start_up},
    )
    normalise(1, (1,))
    open_gate(1)
    open_up(1)
    pass_up(0)
    pass_gate(1)
    pass_up(1)
    first_half = close_turn(0)
    second_half = close_turn(1)
    spread_d.forward()
    spread_d.near()
    spread_d.finish()
    for turn in range(2):
        for which in range(6):
            hop(turn, which).wait_send()

    def down(target):
        offset = (5, 4, 6, 3, 7, 2, 0, 1)[awaited[1]]
        awaited[1] += 1
        (first_half, second_half)[offset // 4].have(offset % 4)
        rows = hidden[offset // 4, offset % 4]
        return jnp.concatenate(
            [jnp.dot(rows, w_down[i], preferred_element_type=F32) for i in range(4)], 1
        )

    added = scatter_z(
        down, sent_d, got_d, cross_d.at[0], cross_d.at[1], zd_send, zd_recv, cross_sem.at[pl.ds(2, 2)]
    )
    first_half.sent()
    second_half.sent()
    result = (stream[...].astype(F32) + added).astype(BF)
    for i in range(4):
        own_out[i] = result[:, i * 512 : i * 512 + 512]
    mine = pl.ds(pl.multiple_of(place * 32, 32), 32)
    backs = [
        remote(own_out.at[(place + i) % 4], out_ref.at[mine], back_sem.at[2 * i], back_sem.at[2 * i + 1], quad(i))
        for i in range(1, 4)
    ]
    for copy in backs:
        copy.start()
    out_ref[mine] = own_out[place]
    for copy in backs:
        copy.wait()


def run_block(offset, queries, keys, values, residual, gain, cache_keys, cache_values, w_out, w_gate, w_up, w_down):
    hop = VM((2, 4, 2, 2, 16, 2048), BF)
    vmem = pl.BlockSpec(memory_space=pltpu.VMEM)
    return pl.pallas_call(
        block_kernel,
        out_shape=jax.ShapeDtypeStruct((128, 512), BF),
        in_specs=[pl.BlockSpec(memory_space=pltpu.SMEM)] + [vmem] * 5 + [pl.BlockSpec(memory_space=pl.ANY)] * 6,
        out_specs=vmem,
        scratch_shapes=[
            VM((16, 48, HD), BF),
            VM((8, 512), F32),
            VM((4, 1024, HD), BF),
            VM((16, 48, HD), BF),
            VM((4, 1024, HD), BF),
            VM((1024, HD), BF),
            VM((4, HD, 1024), BF),
            VM((4, 128, HD), BF),
            VM((4, HD, 128), BF),
            VM((4, 128, HD), BF),
            VM((4, 4, 128, HD), BF),
            VM((4, 8, 512), F32),
            VM((4, 8, 512), F32),
            VM((4, HD, 512), F32),
            VM((4, HD, 512), BF),
            VM((4, HD, 512), BF),
            VM((4, 8, 512), F32),
            VM((4, 8, 512), F32),
            VM((2, 64, 512), BF),
            VM((4, 2, 64, 512), BF),
            VM((4, 512, 512), BF),
            VM((4, 512, 1024), BF),
            VM((4, 512, 1024), BF),
            VM((4, 1024, 512), BF),
            VM((4, 8, 512), F32),
            VM((4, 32, 512), BF),
            VM((32, 2048), BF),
            hop,
            hop,
            hop,
            hop,
            VM((2, 32, 2048), BF),
            VM((2, 32, 2048), BF),
            VM((32, 128), F32),
            VM((4, 32, 128), F32),
            VM((8, 128), F32),
            VM((16, 8, 128), F32),
            VM((8, 2, 32, 2048), BF),
            VM((8, 2, 32, 2048), BF),
            VM((12, 64, 1024), BF),
            VM((12, 64, 1024), BF),
            VM((2, 64, 1024), BF),
            VM((2, 4, 64, 1024), BF),
            VM((4, 32, 512), BF),
        ]
        + [DMA((16,))] * 2
        + [DMA((56,)), DMA((25,))]
        + [DMA((16,))] * 2
        + [DMA((4,))] * 6
        + [DMA((32,))] * 2
        + [DMA((4,))] * 2
        + [DMA((40,))] * 2
        + [DMA((12,))] * 2
        + [DMA((8,))] * 2
        + [DMA((32,))] * 2
        + [DMA((8,)), DMA((8,)), DMA((16,)), DMA((16,))],
        compiler_params=pltpu.CompilerParams(
            collective_id=0, has_side_effects=True, vmem_limit_bytes=VMEM_LIMIT
        ),
        name="block",
    )(offset, queries, keys, values, residual, gain, cache_keys, cache_values, w_out, w_gate, w_up, w_down)


def per_device(
    residual,
    queries,
    keys,
    values,
    cache_keys,
    cache_values,
    offset,
    w_out,
    norm_gain,
    w_gate,
    w_up,
    w_down,
):
    return run_block(
        offset,
        queries,
        keys,
        values,
        residual,
        norm_gain,
        cache_keys,
        cache_values,
        w_out,
        w_gate,
        w_up,
        w_down,
    )


def solution(mesh):
    in_specs = (
        P("sp", "tp"),
        P(("tp", "sp"), None),
        P(("tp", "sp"), None),
        P(("tp", "sp"), None),
        P("tp", None),
        P("tp", None),
        P(),
        P("sp", "tp"),
        P("tp"),
        P("tp", "sp"),
        P("tp", "sp"),
        P("sp", "tp"),
    )
    out_specs = P("sp", "tp")
    return jax.shard_map(
        per_device, mesh=mesh, in_specs=in_specs, out_specs=out_specs, check_vma=False
    )
```
